32 devices in a mesh: group: 2 (over x), expert: 8 (over z, y), tensor: 2 (over core).
Axes of the slice: x: 2, y: 2, z: 4, core: 2. Of those that a mesh axis runs over, the one named last changes fastest.
Arguments:
- tokens: bfloat16 [2048, 2048], P(('group', 'expert'), 'tensor'), parts along dimension 0, may hold values from -6 to 6
- expert_ids: int32 [2048, 4], P(('group', 'expert')), parts along dimension 0, may hold values from 0 to 7, as said below
- router_weights: float32 [2048, 4], P(('group', 'expert')), parts along dimension 0, may hold values from 0.02 to 0.5
- gate_weight: bfloat16 [8, 2048, 768], P('expert', None, 'tensor'), may hold values from -0.125 to 0.125
- up_weight: bfloat16 [8, 2048, 768], P('expert', None, 'tensor'), may hold values from -0.125 to 0.125
- down_weight: bfloat16 [8, 768, 2048], P('expert', 'tensor'), may hold values from -0.21875 to 0.21875
- grad_out: bfloat16 [2048, 2048], P(('group', 'expert'), 'tensor'), parts along dimension 0, may hold values from -1.5 to 1.5
Outputs:
- layer_out: bfloat16 [2048, 2048], P(('group', 'expert'), 'tensor'), parts along dimension 0
- input_grad: bfloat16 [2048, 2048], P(('group', 'expert'), 'tensor'), parts along dimension 0
- weight_grad: float32 [2048, 4], P(('group', 'expert')), parts along dimension 0
- gate_grad: bfloat16 [16, 2048, 768], P(('group', 'expert'), None, 'tensor'), parts along dimension 0
- up_grad: bfloat16 [16, 2048, 768], P(('group', 'expert'), None, 'tensor'), parts along dimension 0
- down_grad: bfloat16 [16, 768, 2048], P(('group', 'expert'), 'tensor'), parts along dimension 0
The draws below stay inside these ranges and needn't reach their ends.
There are 2 independent parts, one for each index of `group`. The reference program is written for one: setup_inputs(seed, part) draws one part's arguments, and reference() takes and returns one part's arrays. A program takes and returns all parts, laid end to end along the dimension named above; an argument that names none is the same for every part. Nothing has to cross between parts.
Inputs may be any that keep to these rules, and one draw needn't show every extreme that they name: `expert_ids`: each token names 4 different experts. Among the 128 tokens held by one device along `expert` no expert is named by more than 96 of them, and one expert, the same on every index, is named by exactly 96 of them on each.
All inputs are finite; a program needn't handle non-finite values.
Results may differ from the reference program's by a relative error of at most 0.0073.
Values may be sent and summed in bfloat16 or wider, within the bound.
No kernel may reach another device: no remote copies, remote signals or barrier semaphores. Data moves between devices by JAX's collectives and lax.ppermute only.
A program may use at most 128 MiB of HBM per device.

```python
import math
import jax
import jax.numpy as jnp
from jax import lax

D = 2048
H = 768
TOPK = 4
TOK_DEV = 128
EXPERTS = 8
CAP = 96
TOKENS = 1024
N_EXPERT = 8
N_TENSOR = 2


def block_ids(block_key, hottest):
    assignments = TOK_DEV * TOPK
    others = EXPERTS - 1
    remaining = assignments - CAP
    base_count = remaining // others
    extra_count = remaining - base_count * others
    subkeys = jax.random.split(block_key, 5)
    other_ids = (hottest + 1 + jax.random.permutation(subkeys[0], others).astype(jnp.int32)) % EXPERTS
    counts = base_count + (jnp.arange(others) < extra_count).astype(jnp.int32)
    pair_count = others // 2
    for round_key in (subkeys[1], subkeys[2]):
        shuffled = jax.random.permutation(round_key, others)
        donors = shuffled[:pair_count]
        takers = shuffled[pair_count:2 * pair_count]
        allowed = jnp.minimum(counts[donors], CAP - counts[takers])
        shifted = jax.random.randint(jax.random.fold_in(round_key, 5), (pair_count,), 0, allowed + 1)
        counts = counts.at[donors].add(-shifted).at[takers].add(shifted)
    run_sizes = jnp.concatenate([jnp.full((1,), CAP, jnp.int32), counts.astype(jnp.int32)])
    run_order = jnp.concatenate([jnp.reshape(hottest, (1,)), other_ids]).astype(jnp.int32)
    run_ends = jnp.cumsum(run_sizes)
    position = jnp.sum((jnp.arange(assignments)[:, None] >= run_ends[None, :]).astype(jnp.int32), axis=1)
    labels = run_order[position]
    table_ids = labels.reshape(TOPK, TOK_DEV).T
    table_ids = table_ids[jax.random.permutation(subkeys[3], TOK_DEV)]
    shuffles = jax.vmap(lambda row_key: jax.random.permutation(row_key, TOPK))(jax.random.split(subkeys[4], TOK_DEV))
    return jnp.take_along_axis(table_ids, shuffles, axis=1).astype(jnp.int32)


def draw_expert_ids(key, part):
    key = jax.random.fold_in(key, 11)
    hottest = jax.random.randint(jax.random.fold_in(key, 1), (), 0, EXPERTS).astype(jnp.int32)
    block_keys = jax.random.split(jax.random.fold_in(key, 2), TOKENS // TOK_DEV)
    blocks = jax.vmap(lambda block_key: block_ids(block_key, hottest))(block_keys)
    return blocks.reshape(TOKENS, TOPK).astype(jnp.int32)


def steps_of(key, extent, shards, low, high):
    def one(axis_at, parts):
        steps = jax.random.uniform(jax.random.fold_in(jax.random.fold_in(key, 6), axis_at), (parts,), jnp.float32, low / len(shards), high / len(shards))
        return jnp.repeat(jnp.exp(steps), extent[axis_at] // parts).reshape((-1,) + (1,) * (len(extent) - axis_at - 1))

    factor_of = one(*shards[0])
    for cut in shards[1:]:
        factor_of = factor_of * one(*cut)
    return factor_of


def bell_draw(key, extent, width, reach, shards=(), kind=jnp.bfloat16):
    values = jax.random.normal(key, extent, jnp.float32) * width
    if len(shards) > 0:
        values = steps_of(key, extent, shards, -0.22, 0.18) * values
    return jnp.clip(values, min=-reach, max=reach).astype(kind)


def setup_inputs(seed: int = 0, part: int = 0) -> dict:
    keys = jax.random.split(jax.random.key(seed), 8)
    part_splits = jax.random.split(jax.random.fold_in(keys[7], part), 8)
    tokens = bell_draw(part_splits[0], (TOKENS, D), 1.0, 6.0, ((0, 8), (1, 2)))
    expert_ids = draw_expert_ids(jax.random.fold_in(jax.random.fold_in(keys[7], part), 71), part)
    router_weights = jnp.clip(jnp.exp(math.log(0.5) - 3.218876 * jax.random.uniform(part_splits[2], (TOKENS, TOPK), jnp.float32) ** steps_of(part_splits[2], (TOKENS, TOPK), ((0, 8),), -0.2, 0.2)), 0.02, 0.5)
    gate_weight = bell_draw(keys[3], (EXPERTS, D, H), D ** -0.5, 0.125, ((0, 8), (2, 2)))
    up_weight = bell_draw(keys[4], (EXPERTS, D, H), D ** -0.5, 0.125, ((0, 8), (2, 2)))
    down_weight = bell_draw(keys[5], (EXPERTS, H, D), H ** -0.5, 0.21875, ((0, 8), (1, 2)))
    grad_out = bell_draw(part_splits[6], (TOKENS, D), 0.25, 1.5, ((0, 8), (1, 2)))
    return dict(tokens=tokens, expert_ids=expert_ids, router_weights=router_weights, gate_weight=gate_weight, up_weight=up_weight, down_weight=down_weight, grad_out=grad_out)


def expert_pass(expert_rows, expert_grads, gate_matrix, up_matrix, down_matrix):
    contract_last = (((1,), (1,)), ((), ()))
    contract_rows = (((0,), (0,)), ((), ()))
    block_width = H // N_TENSOR
    gate_values = jnp.dot(expert_rows, gate_matrix, preferred_element_type=jnp.float32)
    upward = jnp.dot(expert_rows, up_matrix, preferred_element_type=jnp.float32)
    hidden = (jax.nn.silu(gate_values) * upward).astype(jnp.bfloat16)
    out_total = jnp.zeros((expert_rows.shape[0], D), jnp.float32)
    for block in range(N_TENSOR):
        lower = block * block_width
        upper = lower + block_width
        term = jnp.dot(hidden[:, lower:upper], down_matrix[lower:upper], preferred_element_type=jnp.float32)
        out_total = out_total + term.astype(jnp.bfloat16).astype(jnp.float32)
    expert_out = out_total.astype(jnp.bfloat16)
    grad_hidden = lax.dot_general(expert_grads, down_matrix, contract_last, preferred_element_type=jnp.float32)
    sigmoid_gate = jax.nn.sigmoid(gate_values)
    grad_gate = (grad_hidden * upward * sigmoid_gate * (1.0 + gate_values * (1.0 - sigmoid_gate))).astype(jnp.bfloat16)
    grad_up = (grad_hidden * gate_values * sigmoid_gate).astype(jnp.bfloat16)
    in_total = jnp.zeros((expert_rows.shape[0], D), jnp.float32)
    for block in range(N_TENSOR):
        lower = block * block_width
        upper = lower + block_width
        term = lax.dot_general(grad_gate[:, lower:upper], gate_matrix[:, lower:upper], contract_last,
                               preferred_element_type=jnp.float32)
        term = term + lax.dot_general(grad_up[:, lower:upper], up_matrix[:, lower:upper], contract_last,
                                      preferred_element_type=jnp.float32)
        in_total = in_total + term.astype(jnp.bfloat16).astype(jnp.float32)
    down_part = lax.dot_general(hidden, expert_grads, contract_rows, preferred_element_type=jnp.float32)
    gate_part = lax.dot_general(expert_rows, grad_gate, contract_rows, preferred_element_type=jnp.float32)
    up_part = lax.dot_general(expert_rows, grad_up, contract_rows, preferred_element_type=jnp.float32)
    return (expert_out, in_total.astype(jnp.bfloat16), gate_part.astype(jnp.bfloat16),
            up_part.astype(jnp.bfloat16), down_part.astype(jnp.bfloat16))


def reference(tokens, expert_ids, router_weights, gate_weight, up_weight, down_weight, grad_out):
    assignments = TOKENS * TOPK
    largest = N_EXPERT * CAP
    flat_ids = expert_ids.reshape(-1).astype(jnp.int32)
    sorted_order = jnp.argsort(flat_ids, stable=True).astype(jnp.int32)
    onehot = (flat_ids[:, None] == jnp.arange(EXPERTS, dtype=jnp.int32)[None, :]).astype(jnp.int32)
    counts = jnp.sum(onehot, axis=0).astype(jnp.int32)
    run_starts = (jnp.cumsum(counts) - counts).astype(jnp.int32)
    padded = jnp.concatenate([sorted_order, jnp.zeros((largest,), jnp.int32)])
    scaled = (router_weights[:, :, None] * grad_out.astype(jnp.float32)[:, None, :]).astype(jnp.bfloat16)
    scaled = scaled.reshape(assignments, D)

    def one_expert(expert_index):
        chosen = lax.dynamic_slice_in_dim(padded, run_starts[expert_index], largest).astype(jnp.int32)
        is_valid = jnp.arange(largest, dtype=jnp.int32) < counts[expert_index]
        expert_rows = jnp.where(is_valid[:, None], tokens[chosen // TOPK], jnp.zeros((), tokens.dtype))
        expert_grads = jnp.where(is_valid[:, None], scaled[chosen], jnp.zeros((), scaled.dtype))
        results = expert_pass(expert_rows, expert_grads, gate_weight[expert_index],
                              up_weight[expert_index], down_weight[expert_index])
        targets = jnp.where(is_valid, chosen, assignments).astype(jnp.int32)
        return results + (targets,)

    expert_outs, expert_input_grads, gate_grad, up_grad, down_grad, targets = lax.map(
        one_expert, jnp.arange(EXPERTS, dtype=jnp.int32))
    flat_targets = targets.reshape(-1)
    outputs = jnp.zeros((assignments + 1, D), expert_outs.dtype).at[flat_targets].set(expert_outs.reshape(-1, D))
    outputs = outputs[:assignments].reshape(TOKENS, TOPK, D)
    row_grads = jnp.zeros((assignments + 1, D), expert_input_grads.dtype).at[flat_targets].set(
        expert_input_grads.reshape(-1, D))
    row_grads = row_grads[:assignments].reshape(TOKENS, TOPK, D)
    layer_out = jnp.sum(router_weights[:, :, None] * outputs.astype(jnp.float32), axis=1).astype(jnp.bfloat16)
    weight_grad = jnp.sum(grad_out.astype(jnp.float32)[:, None, :] * outputs.astype(jnp.float32), axis=2)
    input_grad = jnp.sum(row_grads.astype(jnp.float32), axis=1).astype(jnp.bfloat16)
    return (layer_out, input_grad, weight_grad, gate_grad, up_grad, down_grad)
```

```python
import jax
import jax.numpy as jnp
from jax import lax
from jax.sharding import PartitionSpec as P

BF = jnp.bfloat16
F32 = jnp.float32


def dot(a, b, contract):
    return lax.dot_general(a, b, (contract, ((), ())), preferred_element_type=F32)


def split_three(values):
    high = lax.reduce_precision(values, 8, 7)
    rest = values - high
    middle = lax.reduce_precision(rest, 8, 7)
    low = rest - middle
    return [part.astype(BF) for part in (high, middle, low)]


def per_device(tokens, expert_ids, router_weights, gate_weight, up_weight, down_weight, grad_out):
    token_count, half_width = tokens.shape
    top_count = expert_ids.shape[1]
    experts = lax.axis_size("expert")
    capacity = min(token_count, 3 * token_count * top_count // (2 * experts))
    lines = experts // 2
    mine = lax.axis_index("expert")
    core = lax.axis_index("tensor")
    peer = mine + 1 - 2 * (mine % 2)

    def over_pair(x):
        return lax.ppermute(x, "expert", [(i, i + 1 - 2 * (i % 2)) for i in range(experts)])

    def over_line(x, k):
        return lax.ppermute(
            x, "expert",
            [(i, ((i // 2 + k) % lines) * 2 + i % 2) for i in range(experts)],
        )

    def over_core(x):
        return lax.ppermute(x, "tensor", [(0, 1), (1, 0)])

    chosen = expert_ids[:, :, None] == jnp.arange(experts, dtype=jnp.int32)[None, None, :]
    table = jnp.sum(jnp.where(chosen, router_weights[:, :, None], 0.0), axis=1).T
    part_rows = experts * token_count // half_width
    parts = jnp.concatenate([p.reshape(part_rows, half_width) for p in split_three(table)])
    extra = -(-3 * part_rows // 16) * 16
    parts = jnp.pad(parts, ((0, extra - 3 * part_rows), (0, 0)))
    first = jnp.concatenate([tokens, parts])

    line_blocks = [first] + [over_line(first, k) for k in range(1, lines)]
    line_grads = [grad_out] + [over_line(grad_out, k) for k in range(1, lines)]

    dense_w, placings, sent_w = [], [], []
    for k in range(lines):
        rows = line_blocks[k][token_count:token_count + 3 * part_rows].astype(F32)
        rows = jnp.sum(rows.reshape(3, part_rows, half_width), axis=0)
        held = rows.reshape(experts, token_count)
        dense_w.append(lax.dynamic_index_in_dim(held, mine, 0, False))
        theirs = lax.dynamic_index_in_dim(held, peer, 0, False)
        named = theirs > 0.0
        rank = jnp.cumsum(named.astype(jnp.int32)) - 1
        picked = (jnp.arange(capacity, dtype=jnp.int32)[:, None] == rank[None, :]) & named[None, :]
        placings.append(picked)
        sent_w.append(jnp.sum(jnp.where(picked, theirs[None, :], 0.0), axis=1))
    pair_w = over_pair(jnp.stack(sent_w))
    places = [p.astype(BF) for p in placings]

    def packed(k, x):
        return dot(places[k], x, ((1,), (0,))).astype(BF)

    pair_blocks = [over_pair(packed(k, line_blocks[k][:token_count])) for k in range(lines)]
    pair_grads = [over_pair(packed(k, line_grads[k])) for k in range(lines)]

    def whole(dense, compact):
        held = jnp.concatenate([d[:token_count] for d in dense] + compact)
        other = over_core(held)
        lower = jnp.where(core == 0, held, other)
        upper = jnp.where(core == 0, other, held)
        return jnp.concatenate([lower, upper], axis=1)

    weights = jnp.concatenate(dense_w + [pair_w.reshape(-1)])[:, None]
    gate_local = gate_weight[0]
    up_local = up_weight[0]
    down_local = down_weight[0]
    rows = whole(line_blocks, pair_blocks)
    gate = dot(rows, gate_local, ((1,), (0,)))
    upward = dot(rows, up_local, ((1,), (0,)))
    sig = jax.nn.sigmoid(gate)
    hidden = gate * sig * upward
    scaled_hidden = (weights * hidden).astype(BF)

    def summed_over_cores(make):
        sent = over_core(make(1 - core).astype(BF))
        return make(core) + sent.astype(F32)

    def half_of(x, which, axis):
        return lax.dynamic_slice_in_dim(x, which * half_width, half_width, axis)

    dense_rows = lines * token_count

    def go_home(both):
        back = over_pair(both[dense_rows:].astype(BF))
        total = None
        for k in range(lines):
            block = both[k * token_count:(k + 1) * token_count]
            block = block + dot(places[k], back[k * capacity:(k + 1) * capacity], ((0,), (0,)))
            if k:
                block = over_line(block.astype(BF), lines - k).astype(F32)
            total = block if total is None else total + block
        return total.astype(BF)

    layer_out = go_home(summed_over_cores(
        lambda c: dot(scaled_hidden, half_of(down_local, c, 1), ((1,), (0,)))))

    grads = whole(line_grads, pair_grads)
    grad_plain = dot(grads, down_local, ((1,), (1,)))
    row_value = jnp.sum(hidden * grad_plain, axis=1)
    grad_hidden = weights * grad_plain
    grad_gate = (grad_hidden * upward * sig * (1.0 + gate * (1.0 - sig))).astype(BF)
    grad_up = (grad_hidden * gate * sig).astype(BF)
    input_grad = go_home(summed_over_cores(
        lambda c: dot(grad_gate, half_of(gate_local, c, 0), ((1,), (1,)))
        + dot(grad_up, half_of(up_local, c, 0), ((1,), (1,)))))

    down_grad = dot(scaled_hidden, grads, ((0,), (0,))).astype(BF)
    gate_grad = dot(rows, grad_gate, ((0,), (0,))).astype(BF)
    up_grad = dot(rows, grad_up, ((0,), (0,))).astype(BF)

    row_value = row_value + over_core(row_value)
    back_value = over_pair(row_value[dense_rows:])
    by_line = []
    for k in range(lines):
        own = row_value[k * token_count:(k + 1) * token_count]
        value = back_value[k * capacity:(k + 1) * capacity]
        value = jnp.sum(jnp.where(placings[k], value[:, None], 0.0), axis=0)
        both = jnp.stack([own, value])
        by_line.append(over_line(both, lines - k) if k else both)
    held = jnp.stack(by_line)
    ids_line = expert_ids // 2
    place = (ids_line - mine // 2) % lines
    is_peer = (expert_ids % 2) != (mine % 2)
    slot = place * 2 + is_peer.astype(jnp.int32)
    flat = held.reshape(experts, token_count)
    match = slot[:, :, None] == jnp.arange(experts, dtype=jnp.int32)[None, None, :]
    weight_grad = jnp.sum(jnp.where(match, flat.T[:, None, :], 0.0), axis=2)
    return (layer_out, input_grad, weight_grad, gate_grad[None], up_grad[None], down_grad[None])


def solution(mesh):
    in_specs = (
        P(("group", "expert"), "tensor"),
        P(("group", "expert"), None),
        P(("group", "expert"), None),
        P("expert", None, "tensor"),
        P("expert", None, "tensor"),
        P("expert", "tensor", None),
        P(("group", "expert"), "tensor"),
    )
    out_specs = (
        P(("group", "expert"), "tensor"),
        P(("group", "expert"), "tensor"),
        P(("group", "expert"), None),
        P(("group", "expert"), None, "tensor"),
        P(("group", "expert"), None, "tensor"),
        P(("group", "expert"), "tensor", None),
    )
    return jax.shard_map(
        per_device, mesh=mesh, in_specs=in_specs, out_specs=out_specs, check_vma=False
    )
```

```python
import functools

import jax
import jax.numpy as jnp
import numpy as np
from jax import lax
from jax.experimental import pallas as pl
from jax.experimental.pallas import tpu as pltpu
from jax.sharding import PartitionSpec as P

BF = jnp.bfloat16
F32 = jnp.float32
I32 = jnp.int32
TAIL = 16


def dot(a, b, contract):
    return lax.dot_general(a, b, (contract, ((), ())), preferred_element_type=F32)


def split_three(values):
    high = lax.reduce_precision(values, 8, 7)
    rest = values - high
    middle = lax.reduce_precision(rest, 8, 7)
    low = rest - middle
    return [part.astype(BF) for part in (high, middle, low)]


def slot_source(lines, z, slot):
    if z < lines // 2:
        above = lines - 1 - z
        return ("down", slot) if slot <= above else ("up", slot - above)
    return ("up", slot) if slot <= z else ("down", slot - z)


def slot_place(lines, z, slot):
    if slot == 0:
        return 0
    direction, distance = slot_source(lines, z, slot)
    return distance if direction == "up" else lines - distance


def vmem_params(limit=48 * 1024 * 1024):
    return pltpu.CompilerParams(vmem_limit_bytes=limit)


SMEM_SPEC = pl.BlockSpec(memory_space=pltpu.SMEM)
VMEM_SPEC = pl.BlockSpec(memory_space=pltpu.VMEM)
ANY_SPEC = pl.BlockSpec(memory_space=pl.ANY)


def token_slot_kernel(count, part_rows, capacity, padded, info, *refs):
    blocks = refs[:count]
    dense, compact, place, table, parts = refs[count:]
    tokens = dense.shape[0] - TAIL
    width = dense.shape[1]
    per_row = width // tokens
    for i, block in enumerate(blocks):
        @pl.when(info[0] == i)
        def _():
            dense[:tokens, :] = block[:tokens, :]
            table[...] = block[tokens:, :].astype(F32)

    def parts_of(expert):
        row, lane = expert // per_row, pl.multiple_of((expert % per_row) * tokens, tokens)
        parts[...] = jnp.zeros_like(parts)
        for p in range(3):
            found = lax.broadcasted_iota(I32, (table.shape[0], tokens), 0) == p * part_rows + row
            parts[p:p + 1, :] = jnp.sum(
                jnp.where(found, table[:, pl.ds(lane, tokens)], 0.0), axis=0, keepdims=True)
        return parts[...]

    dense[tokens:, :] = jnp.zeros((TAIL, width), BF)
    dense[tokens:, :tokens] = parts_of(info[1]).astype(BF)
    theirs = parts_of(info[2])
    named = jnp.sum(theirs, axis=0, keepdims=True) > 0.0
    row_at = lax.broadcasted_iota(I32, (tokens, tokens), 0)
    column_at = lax.broadcasted_iota(I32, (tokens, tokens), 1)
    until = (row_at <= column_at).astype(F32).astype(BF)
    ones = jnp.broadcast_to(named.astype(F32), (TAIL, tokens)).astype(BF)
    rank = jnp.dot(ones, until, preferred_element_type=F32)[:1, :].astype(I32) - 1
    picked = ((row_at == rank) & named & (row_at < capacity)).astype(F32).astype(BF)
    place[...] = picked[:padded, :]
    compact[:padded, :] = jnp.dot(
        picked[:padded, :], dense[:tokens, :], preferred_element_type=F32).astype(BF)
    compact[padded:, :] = jnp.zeros((TAIL, width), BF)
    compact[padded:, :tokens] = dot(theirs.astype(BF), picked, ((1,), (1,))).astype(BF)


def grad_slot_kernel(count, info, *refs):
    blocks = refs[:count]
    place, dense, compact = refs[count:]
    for i, block in enumerate(blocks):
        @pl.when(info[0] == i)
        def _():
            dense[...] = block[...]
    compact[...] = jnp.dot(place[...], dense[...], preferred_element_type=F32).astype(BF)


def gather_rows(lines, tokens, padded, width, info, mine, other, rows, sems):
    core = info[lines]
    copies = []
    for half, blocks in enumerate((mine, other)):
        which = core if half == 0 else 1 - core
        lane = pl.multiple_of(which * width, width)
        for j in range(lines):
            at = info[j]
            dense, compact = blocks[j], blocks[lines + j]
            copies.append(pltpu.make_async_copy(
                dense.at[pl.ds(0, tokens), :],
                rows.at[pl.ds(pl.multiple_of(at * tokens, tokens), tokens), pl.ds(lane, width)],
                sems.at[len(copies)]))
            copies.append(pltpu.make_async_copy(
                compact.at[pl.ds(0, padded), :],
                rows.at[pl.ds(pl.multiple_of(lines * tokens + at * padded, 16), padded),
                        pl.ds(lane, width)],
                sems.at[len(copies)]))
    for copy in copies:
        copy.start()
    return copies


def gather_tokens_kernel(lines, tokens, padded, width, info, *refs):
    mine, other = refs[:2 * lines], refs[2 * lines:4 * lines]
    tails = refs[4 * lines:6 * lines]
    places = refs[6 * lines:7 * lines]
    rows, weights, ring, sems = refs[7 * lines:]
    copies = gather_rows(lines, tokens, padded, width, info, mine, other, rows, sems)
    eye = (lax.broadcasted_iota(I32, (tokens, tokens), 0)
           == lax.broadcasted_iota(I32, (tokens, tokens), 1))
    for j in range(lines):
        at = info[j]
        for i, (first, size) in enumerate(((0, tokens), (lines * tokens, padded))):
            row = jnp.sum(tails[i * lines + j][...].astype(F32), axis=0, keepdims=True)
            column = jnp.sum(jnp.where(eye, row, 0.0), axis=1, keepdims=True)
            weights[pl.ds(pl.multiple_of(first + at * size, 16), size), :] = column[:size]
        ring[at] = places[j][...]
    for copy in copies:
        copy.wait()


def gather_grads_kernel(lines, tokens, padded, width, info, *refs):
    mine, other = refs[:2 * lines], refs[2 * lines:4 * lines]
    rows, sems = refs[4 * lines:]
    for copy in gather_rows(lines, tokens, padded, width, info, mine, other, rows, sems):
        copy.wait()


def per_device(tokens, expert_ids, router_weights, gate_weight, up_weight, down_weight, grad_out):
    token_count, half_width = tokens.shape
    top_count = expert_ids.shape[1]
    experts = lax.axis_size("expert")
    capacity = min(token_count, 3 * token_count * top_count // (2 * experts))
    padded = -(-capacity // 16) * 16
    lines = experts // 2
    mine = lax.axis_index("expert")
    core = lax.axis_index("tensor")
    at_line = mine // 2
    peer = mine + 1 - 2 * (mine % 2)

    def over_pair(x):
        return lax.ppermute(x, "expert", [(i, i + 1 - 2 * (i % 2)) for i in range(experts)])

    def over_line(x, k):
        return lax.ppermute(
            x, "expert",
            [(i, ((i // 2 + k) % lines) * 2 + i % 2) for i in range(experts)],
        )

    def hop(x, k, step):
        low, high = (k - 1, lines - 1) if step > 0 else (1, lines - k + 1)
        return lax.ppermute(
            x, "expert",
            [(2 * z + y, 2 * (z + step) + y) for z in range(low, high) for y in range(2)],
        )

    def over_core(x):
        return lax.ppermute(x, "tensor", [(0, 1), (1, 0)])

    chosen = expert_ids[:, :, None] == jnp.arange(experts, dtype=I32)[None, None, :]
    table = jnp.sum(jnp.where(chosen, router_weights[:, :, None], 0.0), axis=1).T
    part_rows = experts * token_count // half_width
    parts = jnp.concatenate([p.reshape(part_rows, half_width) for p in split_three(table)])
    tail = -(-3 * part_rows // TAIL) * TAIL
    parts = jnp.pad(parts, ((0, tail - 3 * part_rows), (0, 0)))
    first = jnp.concatenate([tokens, parts])

    def along_line(start):
        up, down = {0: start}, {0: start}
        for k in range(1, lines):
            up[k] = hop(up[k - 1], k, 1)
            down[k] = hop(down[k - 1], k, -1)
        return up, down

    up, down = along_line(first)
    held_back, _, _ = lax.optimization_barrier((grad_out, up[min(2, lines - 1)], down[min(2, lines - 1)]))
    grad_up_line, grad_down_line = along_line(held_back)

    def candidates(slot, ups, downs):
        if slot == 0:
            return [ups[0]], jnp.zeros((), I32)
        sources = [slot_source(lines, z, slot) for z in range(lines)]
        names = sorted(set(sources))
        which = jnp.asarray(np.array([names.index(s) for s in sources], np.int32))[at_line]
        return [(ups if d == "up" else downs)[n] for d, n in names], which

    dense_blocks, compact_blocks, places = [], [], []
    for slot in range(lines):
        blocks, which = candidates(slot, up, down)
        info = jnp.stack([which, mine, peer]).astype(I32)
        dense, compact, place = pl.pallas_call(
            functools.partial(token_slot_kernel, len(blocks), part_rows, capacity, padded),
            out_shape=(
                jax.ShapeDtypeStruct((token_count + TAIL, half_width), BF),
                jax.ShapeDtypeStruct((padded + TAIL, half_width), BF),
                jax.ShapeDtypeStruct((padded, token_count), BF),
            ),
            in_specs=[SMEM_SPEC] + [VMEM_SPEC] * len(blocks),
            out_specs=(VMEM_SPEC,) * 3,
            scratch_shapes=[pltpu.VMEM((tail, half_width), F32), pltpu.VMEM((TAIL, token_count), F32)],
            compiler_params=vmem_params(),
            cost_estimate=pl.CostEstimate(flops=10**8, bytes_accessed=10**6, transcendentals=0),
        )(info, *blocks)
        dense_blocks.append(dense)
        compact_blocks.append(over_pair(compact))
        places.append(place)

    grad_dense, grad_compact = [], []
    for slot in range(lines):
        blocks, which = candidates(slot, grad_up_line, grad_down_line)
        if slot == 0:
            blocks = [grad_out]
        dense, compact = pl.pallas_call(
            functools.partial(grad_slot_kernel, len(blocks)),
            out_shape=(
                jax.ShapeDtypeStruct((token_count, half_width), BF),
                jax.ShapeDtypeStruct((padded, half_width), BF),
            ),
            in_specs=[SMEM_SPEC] + [VMEM_SPEC] * (len(blocks) + 1),
            out_specs=(VMEM_SPEC,) * 2,
            compiler_params=vmem_params(),
            cost_estimate=pl.CostEstimate(flops=10**8, bytes_accessed=10**6, transcendentals=0),
        )(which[None], *blocks, places[slot])
        grad_dense.append(dense)
        grad_compact.append(over_pair(compact))

    place_of = np.array([[slot_place(lines, z, s) for s in range(lines)] for z in range(lines)], np.int32)
    order = jnp.concatenate([jnp.asarray(place_of)[at_line], core[None].astype(I32)])
    dense_rows = lines * token_count
    row_count = lines * (token_count + padded)
    rows_shape = jax.ShapeDtypeStruct((row_count, 2 * half_width), BF)
    sem_shape = pltpu.SemaphoreType.DMA((4 * lines,))

    blocks = dense_blocks + compact_blocks
    other = [over_core(b) for b in blocks]
    tails = ([b[token_count:, :token_count] for b in dense_blocks]
             + [b[padded:, :token_count] for b in compact_blocks])
    rows, weights, ring = pl.pallas_call(
        functools.partial(gather_tokens_kernel, lines, token_count, padded, half_width),
        out_shape=(
            rows_shape,
            jax.ShapeDtypeStruct((row_count, 1), F32),
            jax.ShapeDtypeStruct((lines, padded, token_count), BF),
        ),
        in_specs=[SMEM_SPEC] + [ANY_SPEC] * (4 * lines) + [VMEM_SPEC] * (3 * lines),
        out_specs=(VMEM_SPEC,) * 3,
        scratch_shapes=[sem_shape],
        compiler_params=vmem_params(),
        cost_estimate=pl.CostEstimate(flops=10**6, bytes_accessed=8 * 10**6, transcendentals=0),
    )(order, *blocks, *other, *tails, *places)

    gate_local = gate_weight[0]
    up_local = up_weight[0]
    down_local = down_weight[0]
    gate = dot(rows, gate_local, ((1,), (0,)))
    upward = dot(rows, up_local, ((1,), (0,)))
    sig = jax.nn.sigmoid(gate)
    hidden = gate * sig * upward
    scaled_hidden = (weights * hidden).astype(BF)

    def summed_over_cores(make):
        sent = over_core(make(1 - core).astype(BF))
        return make(core) + sent.astype(F32)

    def half_of(x, which, axis):
        return lax.dynamic_slice_in_dim(x, which * half_width, half_width, axis)

    def go_home(both):
        total = None
        for k in list(range(1, lines)) + [0]:
            at = dense_rows + k * padded
            back = over_pair(both[at:at + padded].astype(BF))
            block = both[k * token_count:(k + 1) * token_count]
            block = block + dot(ring[k], back, ((0,), (0,)))
            if k:
                block = over_line(block.astype(BF), lines - k).astype(F32)
            total = block if total is None else total + block
        return total.astype(BF)

    layer_out = go_home(summed_over_cores(
        lambda c: dot(scaled_hidden, half_of(down_local, c, 1), ((1,), (0,)))))

    blocks = grad_dense + grad_compact
    other = [over_core(b) for b in blocks]
    grads = pl.pallas_call(
        functools.partial(gather_grads_kernel, lines, token_count, padded, half_width),
        out_shape=rows_shape,
        in_specs=[SMEM_SPEC] + [ANY_SPEC] * (4 * lines),
        out_specs=VMEM_SPEC,
        scratch_shapes=[sem_shape],
        compiler_params=vmem_params(),
        cost_estimate=pl.CostEstimate(flops=10**6, bytes_accessed=8 * 10**6, transcendentals=0),
    )(order, *blocks, *other)

    grad_plain = dot(grads, down_local, ((1,), (1,)))
    row_value = jnp.sum(hidden * grad_plain, axis=1)
    grad_hidden = weights * grad_plain
    grad_gate = (grad_hidden * upward * sig * (1.0 + gate * (1.0 - sig))).astype(BF)
    grad_up = (grad_hidden * gate * sig).astype(BF)
    input_grad = go_home(summed_over_cores(
        lambda c: dot(grad_gate, half_of(gate_local, c, 0), ((1,), (1,)))
        + dot(grad_up, half_of(up_local, c, 0), ((1,), (1,)))))

    down_grad = dot(scaled_hidden, grads, ((0,), (0,))).astype(BF)
    gate_grad = dot(rows, grad_gate, ((0,), (0,))).astype(BF)
    up_grad = dot(rows, grad_up, ((0,), (0,))).astype(BF)

    row_value = row_value + over_core(row_value)
    back_value = over_pair(row_value[dense_rows:])
    by_line = []
    for k in range(lines):
        own = row_value[k * token_count:(k + 1) * token_count]
        value = back_value[k * padded:(k + 1) * padded]
        value = jnp.sum(ring[k].astype(F32) * value[:, None], axis=0)
        both = jnp.stack([own, value])
        by_line.append(over_line(both, lines - k) if k else both)
    held = jnp.stack(by_line)
    ids_line = expert_ids // 2
    place = (ids_line - mine // 2) % lines
    is_peer = (expert_ids % 2) != (mine % 2)
    slot = place * 2 + is_peer.astype(jnp.int32)
    flat = held.reshape(experts, token_count)
    match = slot[:, :, None] == jnp.arange(experts, dtype=jnp.int32)[None, None, :]
    weight_grad = jnp.sum(jnp.where(match, flat.T[:, None, :], 0.0), axis=2)
    return (layer_out, input_grad, weight_grad, gate_grad[None], up_grad[None], down_grad[None])


def solution(mesh):
    in_specs = (
        P(("group", "expert"), "tensor"),
        P(("group", "expert"), None),
        P(("group", "expert"), None),
        P("expert", None, "tensor"),
        P("expert", None, "tensor"),
        P("expert", "tensor", None),
        P(("group", "expert"), "tensor"),
    )
    out_specs = (
        P(("group", "expert"), "tensor"),
        P(("group", "expert"), "tensor"),
        P(("group", "expert"), None),
        P(("group", "expert"), None, "tensor"),
        P(("group", "expert"), None, "tensor"),
        P(("group", "expert"), "tensor", None),
    )
    return jax.shard_map(
        per_device, mesh=mesh, in_specs=in_specs, out_specs=out_specs, check_vma=False
    )
```

```python
import functools

import jax
import jax.numpy as jnp
import numpy as np
from jax import lax
from jax.experimental import pallas as pl
from jax.experimental.pallas import tpu as pltpu
from jax.sharding import PartitionSpec as P

BF = jnp.bfloat16
F32 = jnp.float32
I32 = jnp.int32
TAIL = 16


def dot(a, b, contract):
    return lax.dot_general(a, b, (contract, ((), ())), preferred_element_type=F32)


def split_three(values):
    high = lax.reduce_precision(values, 8, 7)
    rest = values - high
    middle = lax.reduce_precision(rest, 8, 7)
    low = rest - middle
    return [part.astype(BF) for part in (high, middle, low)]


def slot_source(lines, z, slot):
    if z < lines // 2:
        above = lines - 1 - z
        return ("down", slot) if slot <= above else ("up", slot - above)
    return ("up", slot) if slot <= z else ("down", slot - z)


def slot_place(lines, z, slot):
    if slot == 0:
        return 0
    direction, distance = slot_source(lines, z, slot)
    return distance if direction == "up" else lines - distance


def vmem_params(*shapes):
    total = sum(int(np.prod(x.shape)) * x.dtype.itemsize for x in shapes)
    return pltpu.CompilerParams(vmem_limit_bytes=int(total * 1.3) + 3 * 1024 * 1024)


def shape_of(shape, dtype=BF):
    return jax.ShapeDtypeStruct(shape, dtype)


def local_call(kernel, outs, args, scratch=(), in_specs=None, flops=10**8):
    moved = sum(int(np.prod(x.shape)) * x.dtype.itemsize for x in tuple(args) + tuple(outs))
    return pl.pallas_call(
        kernel,
        out_shape=tuple(outs),
        in_specs=in_specs or [SMEM_SPEC] + [VMEM_SPEC] * (len(args) - 1),
        out_specs=(VMEM_SPEC,) * len(outs),
        scratch_shapes=list(scratch),
        compiler_params=vmem_params(*args, *outs),
        cost_estimate=pl.CostEstimate(flops=flops, bytes_accessed=moved, transcendentals=0),
    )(*args)


SMEM_SPEC = pl.BlockSpec(memory_space=pltpu.SMEM)
VMEM_SPEC = pl.BlockSpec(memory_space=pltpu.VMEM)


def token_slot_kernel(count, which_at, tokens, part_rows, capacity, padded, info, *refs):
    blocks = refs[:count]
    compact, place, own_parts, table, parts = refs[count:]
    width = compact.shape[1]
    per_row = width // tokens
    for i, block in enumerate(blocks):
        @pl.when(info[which_at] == i)
        def _():
            table[...] = block[tokens:, :].astype(F32)

    def parts_of(expert):
        row, lane = expert // per_row, pl.multiple_of((expert % per_row) * tokens, tokens)
        parts[...] = jnp.zeros_like(parts)
        for p in range(3):
            found = lax.broadcasted_iota(I32, (table.shape[0], tokens), 0) == p * part_rows + row
            parts[p:p + 1, :] = jnp.sum(
                jnp.where(found, table[:, pl.ds(lane, tokens)], 0.0), axis=0, keepdims=True)
        return parts[...]

    own_parts[...] = parts_of(info[0]).astype(BF)
    theirs = parts_of(info[1])
    named = jnp.sum(theirs, axis=0, keepdims=True) > 0.0
    row_at = lax.broadcasted_iota(I32, (tokens, tokens), 0)
    column_at = lax.broadcasted_iota(I32, (tokens, tokens), 1)
    until = (row_at <= column_at).astype(F32).astype(BF)
    ones = jnp.broadcast_to(named.astype(F32), (TAIL, tokens)).astype(BF)
    rank = jnp.dot(ones, until, preferred_element_type=F32)[:1, :].astype(I32) - 1
    picked = ((row_at == rank) & named & (row_at < capacity)).astype(F32).astype(BF)
    place[...] = picked[:padded, :]
    for i, block in enumerate(blocks):
        @pl.when(info[which_at] == i)
        def _():
            compact[:padded, :] = jnp.dot(
                place[...], block[:tokens, :], preferred_element_type=F32).astype(BF)
    compact[padded:, :] = jnp.zeros((TAIL, width), BF)
    compact[padded:, :tokens] = dot(theirs.astype(BF), picked, ((1,), (1,))).astype(BF)


def grad_slot_kernel(count, which_at, info, *refs):
    blocks = refs[:count]
    place, compact = refs[count:]
    for i, block in enumerate(blocks):
        @pl.when(info[which_at] == i)
        def _():
            compact[...] = jnp.dot(
                place[...], block[...], preferred_element_type=F32).astype(BF)


def line_kernel(counts, which_at, place_at, tokens, info, *refs):
    whole = refs[-1]
    at = 0
    for slot, count in enumerate(counts):
        first = pl.multiple_of(info[place_at + slot] * tokens, tokens)
        for i in range(count):
            block = refs[at + i]

            @pl.when(info[which_at + slot] == i)
            def _():
                whole[pl.ds(first, tokens), :] = block[:tokens, :]
        at += count


def rows_copies(lines, tokens, padded, width, place_at, info, dense, compact, rows, sems):
    core = info[2]
    copies = []
    for half in range(2):
        lane = pl.multiple_of((core if half == 0 else 1 - core) * width, width)
        copies.append(pltpu.make_async_copy(
            dense[half], rows.at[pl.ds(0, lines * tokens), pl.ds(lane, width)],
            sems.at[len(copies)]))
        for j in range(lines):
            first = pl.multiple_of(lines * tokens + info[place_at + j] * padded, 16)
            copies.append(pltpu.make_async_copy(
                compact[half][j].at[pl.ds(0, padded), :],
                rows.at[pl.ds(first, padded), pl.ds(lane, width)],
                sems.at[len(copies)]))
    for copy in copies:
        copy.start()
    return copies


def token_rows_kernel(lines, tokens, padded, width, place_at, info, *refs):
    n = lines
    dense = refs[:2]
    compact = (refs[2:2 + n], refs[2 + n:2 + 2 * n])
    own_parts = refs[2 + 2 * n:2 + 3 * n]
    places = refs[2 + 3 * n:2 + 4 * n]
    rows, weights, ring, sems = refs[2 + 4 * n:]
    copies = rows_copies(n, tokens, padded, width, place_at, info, dense, compact, rows, sems)
    eye = (lax.broadcasted_iota(I32, (tokens, tokens), 0)
           == lax.broadcasted_iota(I32, (tokens, tokens), 1))
    for j in range(n):
        at = info[place_at + j]
        for first, size, tail in (
            (0, tokens, own_parts[j][...]),
            (n * tokens, padded, compact[0][j][padded:, :tokens]),
        ):
            row = jnp.sum(tail.astype(F32), axis=0, keepdims=True)
            column = jnp.sum(jnp.where(eye, row, 0.0), axis=1, keepdims=True)
            weights[pl.ds(pl.multiple_of(first + at * size, 16), size), :] = column[:size]
        ring[at] = places[j][...]
    for copy in copies:
        copy.wait()


def grad_rows_kernel(lines, tokens, padded, width, place_at, info, *refs):
    n = lines
    dense = refs[:2]
    compact = (refs[2:2 + n], refs[2 + n:2 + 2 * n])
    rows, sems = refs[2 + 2 * n:]
    for copy in rows_copies(n, tokens, padded, width, place_at, info, dense, compact, rows, sems):
        copy.wait()


def pack_kernel(lines, tokens, padded, info, both, tails, *messages):
    for k in range(lines):
        at = lines * tokens + k * padded
        messages[k][:padded, :] = both[at:at + padded, :].astype(BF)
        messages[k][padded:, :] = jnp.zeros((TAIL, both.shape[1]), BF)
        messages[k][padded:, :tokens] = tails[k].astype(BF)


def home_kernel(k, tokens, padded, info, both, back, ring, tails, message):
    place = ring[k]
    block = both[k * tokens:(k + 1) * tokens, :] + dot(place, back[:padded, :], ((0,), (0,)))
    message[:tokens, :] = block.astype(BF)
    message[tokens:, :] = jnp.zeros((TAIL, both.shape[1]), BF)
    theirs = dot(back[padded:, :padded], place, ((1,), (0,)))
    message[tokens:, :tokens] = jnp.concatenate(
        [tails[k][:8], theirs[:8]], axis=0).astype(BF)


def per_device(tokens, expert_ids, router_weights, gate_weight, up_weight, down_weight, grad_out):
    token_count, half_width = tokens.shape
    top_count = expert_ids.shape[1]
    experts = lax.axis_size("expert")
    capacity = min(token_count, 3 * token_count * top_count // (2 * experts))
    padded = -(-capacity // 16) * 16
    lines = experts // 2
    mine = lax.axis_index("expert")
    core = lax.axis_index("tensor")
    at_line = mine // 2
    peer = mine + 1 - 2 * (mine % 2)

    def over_pair(x):
        return lax.ppermute(x, "expert", [(i, i + 1 - 2 * (i % 2)) for i in range(experts)])

    def over_line(x, k):
        return lax.ppermute(
            x, "expert",
            [(i, ((i // 2 + k) % lines) * 2 + i % 2) for i in range(experts)],
        )

    def hop(x, k, step):
        low, high = (k - 1, lines - 1) if step > 0 else (1, lines - k + 1)
        return lax.ppermute(
            x, "expert",
            [(2 * z + y, 2 * (z + step) + y) for z in range(low, high) for y in range(2)],
        )

    def over_core(x):
        return lax.ppermute(x, "tensor", [(0, 1), (1, 0)])

    chosen = expert_ids[:, :, None] == jnp.arange(experts, dtype=I32)[None, None, :]
    table = jnp.sum(jnp.where(chosen, router_weights[:, :, None], 0.0), axis=1).T
    part_rows = experts * token_count // half_width
    parts = jnp.concatenate([p.reshape(part_rows, half_width) for p in split_three(table)])
    tail = -(-3 * part_rows // TAIL) * TAIL
    parts = jnp.pad(parts, ((0, tail - 3 * part_rows), (0, 0)))
    first = jnp.concatenate([tokens, parts])

    def along_line(start):
        up, down = {0: start}, {0: start}
        for k in range(1, lines):
            up[k] = hop(up[k - 1], k, 1)
            down[k] = hop(down[k - 1], k, -1)
        return up, down

    up, down = along_line(first)

    def sources_of(slot):
        if slot == 0:
            return [(None, 0)], np.zeros(lines, np.int32)
        sources = [slot_source(lines, z, slot) for z in range(lines)]
        names = sorted(set(sources))
        return names, np.array([names.index(n) for n in sources], np.int32)

    names_of = [sources_of(slot)[0] for slot in range(lines)]
    which_of = np.stack([sources_of(slot)[1] for slot in range(lines)], 1)
    place_of = np.array([[slot_place(lines, z, n) for n in range(lines)] for z in range(lines)], np.int32)
    known = jnp.asarray(np.concatenate([which_of, place_of], 1))[at_line]
    info = jnp.concatenate([jnp.stack([mine, peer, core]).astype(I32), known])
    which_at, place_at = 3, 3 + lines

    def candidates(slot, ups, downs):
        return [(downs if d == "down" else ups)[n] for d, n in names_of[slot]]

    counts = [len(n) for n in names_of]
    compact_shape = shape_of((padded + TAIL, half_width))
    packed, compact_blocks, places, own_parts = [], [], [], []
    for slot in range(lines):
        blocks = candidates(slot, up, down)
        compact, place, parts = local_call(
            functools.partial(token_slot_kernel, len(blocks), which_at + slot, token_count,
                              part_rows, capacity, padded),
            (compact_shape, shape_of((padded, token_count)), shape_of((TAIL, token_count))),
            (info, *blocks),
            (pltpu.VMEM((tail, half_width), F32), pltpu.VMEM((TAIL, token_count), F32)),
        )
        packed.append(compact)
        compact_blocks.append(over_pair(compact))
        places.append(place)
        own_parts.append(parts)

    def lined(ups, downs):
        blocks = [x for slot in range(lines) for x in candidates(slot, ups, downs)]
        (whole,) = local_call(
            functools.partial(line_kernel, counts, which_at, place_at, token_count),
            (shape_of((lines * token_count, half_width)),), (info, *blocks), flops=10**6)
        return whole

    dense_rows = lines * token_count
    row_count = lines * (token_count + padded)
    rows_shape = shape_of((row_count, 2 * half_width))
    sems = (pltpu.SemaphoreType.DMA((2 * (lines + 1),)),)
    sizes = (lines, token_count, padded, half_width, place_at)

    dense_own = lined(up, down)
    rows, weights, ring = local_call(
        functools.partial(token_rows_kernel, *sizes),
        (rows_shape, shape_of((row_count, 1), F32), shape_of((lines, padded, token_count))),
        (info, dense_own, over_core(dense_own), *compact_blocks,
         *[over_core(x) for x in compact_blocks], *own_parts, *places),
        sems, flops=10**6)

    held_grad, _ = lax.optimization_barrier((grad_out, packed[min(2, lines - 1)]))
    grad_ups, grad_downs = along_line(held_grad)
    grad_compact = []
    for slot in range(lines):
        blocks = candidates(slot, grad_ups, grad_downs)
        (compact,) = local_call(
            functools.partial(grad_slot_kernel, len(blocks), which_at + slot),
            (shape_of((padded, half_width)),), (info, *blocks, places[slot]))
        grad_compact.append(over_pair(compact))

    gate_local = gate_weight[0]
    up_local = up_weight[0]
    down_local = down_weight[0]
    gate = dot(rows, gate_local, ((1,), (0,)))
    upward = dot(rows, up_local, ((1,), (0,)))
    sig = jax.nn.sigmoid(gate)
    hidden = gate * sig * upward
    scaled_hidden = (weights * hidden).astype(BF)

    def summed_over_cores(make):
        sent = over_core(make(1 - core).astype(BF))
        return make(core) + sent.astype(F32)

    def half_of(x, which, axis):
        return lax.dynamic_slice_in_dim(x, which * half_width, half_width, axis)

    message_shape = shape_of((token_count + TAIL, half_width))

    def crossed(both, compact_tails):
        messages = local_call(
            functools.partial(pack_kernel, lines, token_count, padded),
            (compact_shape,) * lines, (info, both, compact_tails), flops=10**6)
        return [over_pair(m) for m in messages]

    def to_home(both, backs, dense_tails):
        return [
            local_call(
                functools.partial(home_kernel, k, token_count, padded),
                (message_shape,), (info, both, backs[k], ring, dense_tails))[0]
            for k in range(lines)
        ]

    def go_home(blocks):
        return [blocks[0]] + [over_line(blocks[k], lines - k) for k in range(1, lines)]

    def summed(blocks):
        total = blocks[0][:token_count].astype(F32)
        for block in blocks[1:]:
            total = total + block[:token_count].astype(F32)
        return total.astype(BF)

    no_tails = jnp.zeros((lines, TAIL, token_count), F32)
    out_both = summed_over_cores(
        lambda c: dot(scaled_hidden, half_of(down_local, c, 1), ((1,), (0,))))
    out_backs = crossed(out_both, no_tails)
    out_blocks = to_home(out_both, out_backs, no_tails)
    layer_out = summed(go_home(out_blocks))

    grad_own = lined(grad_ups, grad_downs)
    grad_own, _ = lax.optimization_barrier((grad_own, out_both))
    (grads,) = local_call(
        functools.partial(grad_rows_kernel, *sizes), (rows_shape,),
        (info, grad_own, over_core(grad_own), *grad_compact, *[over_core(x) for x in grad_compact]),
        sems, flops=10**6)
    grad_plain = dot(grads, down_local, ((1,), (1,)))
    row_value = jnp.sum(hidden * grad_plain, axis=1)
    grad_hidden = weights * grad_plain
    grad_gate = (grad_hidden * upward * sig * (1.0 + gate * (1.0 - sig))).astype(BF)
    grad_up = (grad_hidden * gate * sig).astype(BF)
    in_both = summed_over_cores(
        lambda c: dot(grad_gate, half_of(gate_local, c, 0), ((1,), (1,)))
        + dot(grad_up, half_of(up_local, c, 0), ((1,), (1,))))
    in_both, _ = lax.optimization_barrier((in_both, out_blocks))

    def tails_of(values):
        values = jnp.pad(values, ((0, 0), (0, token_count - values.shape[1])))
        parts = jnp.stack([p.astype(F32) for p in split_three(values)], axis=1)
        return jnp.pad(parts, ((0, 0), (0, TAIL - 3), (0, 0)))

    dense_tails = tails_of(row_value[:dense_rows].reshape(lines, token_count))
    compact_tails = tails_of(row_value[dense_rows:].reshape(lines, padded))
    in_backs = crossed(in_both, compact_tails)
    in_blocks = to_home(in_both, in_backs, dense_tails)
    came_home = go_home(in_blocks)
    input_grad = summed(came_home)

    down_grad = dot(scaled_hidden, grads, ((0,), (0,))).astype(BF)
    gate_grad = dot(rows, grad_gate, ((0,), (0,))).astype(BF)
    up_grad = dot(rows, grad_up, ((0,), (0,))).astype(BF)

    held = []
    for block in came_home:
        rows_back = block[token_count:, :token_count].astype(F32)
        held.append(jnp.stack([jnp.sum(rows_back[:8], axis=0), jnp.sum(rows_back[8:], axis=0)]))
    flat = jnp.stack(held).reshape(experts, token_count)
    place = (expert_ids // 2 - at_line) % lines
    slot = place * 2 + ((expert_ids % 2) != (mine % 2)).astype(I32)
    match = slot[:, :, None] == jnp.arange(experts, dtype=I32)[None, None, :]
    half_value = jnp.sum(jnp.where(match, flat.T[:, None, :], 0.0), axis=2)
    weight_grad = half_value + over_core(half_value)
    return (layer_out, input_grad, weight_grad, gate_grad[None], up_grad[None], down_grad[None])


def solution(mesh):
    in_specs = (
        P(("group", "expert"), "tensor"),
        P(("group", "expert"), None),
        P(("group", "expert"), None),
        P("expert", None, "tensor"),
        P("expert", None, "tensor"),
        P("expert", "tensor", None),
        P(("group", "expert"), "tensor"),
    )
    out_specs = (
        P(("group", "expert"), "tensor"),
        P(("group", "expert"), "tensor"),
        P(("group", "expert"), None),
        P(("group", "expert"), None, "tensor"),
        P(("group", "expert"), None, "tensor"),
        P(("group", "expert"), "tensor", None),
    )
    return jax.shard_map(
        per_device, mesh=mesh, in_specs=in_specs, out_specs=out_specs, check_vma=False
    )
```

```python
import functools

import jax
import jax.numpy as jnp
import numpy as np
from jax import lax
from jax.experimental import pallas as pl
from jax.experimental.pallas import tpu as pltpu
from jax.sharding import PartitionSpec as P

BF = jnp.bfloat16
F32 = jnp.float32
I32 = jnp.int32
TAIL = 16


def dot(a, b, contract):
    return lax.dot_general(a, b, (contract, ((), ())), preferred_element_type=F32)


def split_three(values):
    high = lax.reduce_precision(values, 8, 7)
    rest = values - high
    middle = lax.reduce_precision(rest, 8, 7)
    low = rest - middle
    return [part.astype(BF) for part in (high, middle, low)]


def slot_source(lines, z, slot):
    if z < lines // 2:
        above = lines - 1 - z
        return ("down", slot) if slot <= above else ("up", slot - above)
    return ("up", slot) if slot <= z else ("down", slot - z)


def slot_place(lines, z, slot):
    if slot == 0:
        return 0
    direction, distance = slot_source(lines, z, slot)
    return distance if direction == "up" else lines - distance


def vmem_params(*shapes):
    total = sum(int(np.prod(x.shape)) * x.dtype.itemsize for x in shapes)
    return pltpu.CompilerParams(vmem_limit_bytes=int(total * 1.3) + 3 * 1024 * 1024)


def shape_of(shape, dtype=BF):
    return jax.ShapeDtypeStruct(shape, dtype)


def local_call(kernel, outs, args, scratch=(), in_specs=None, flops=10**8):
    moved = sum(int(np.prod(x.shape)) * x.dtype.itemsize for x in tuple(args) + tuple(outs))
    return pl.pallas_call(
        kernel,
        out_shape=tuple(outs),
        in_specs=in_specs or [SMEM_SPEC] + [VMEM_SPEC] * (len(args) - 1),
        out_specs=(VMEM_SPEC,) * len(outs),
        scratch_shapes=list(scratch),
        compiler_params=vmem_params(*args, *outs),
        cost_estimate=pl.CostEstimate(flops=flops, bytes_accessed=moved, transcendentals=0),
    )(*args)


SMEM_SPEC = pl.BlockSpec(memory_space=pltpu.SMEM)
VMEM_SPEC = pl.BlockSpec(memory_space=pltpu.VMEM)


def token_slot_kernel(count, which_at, tokens, part_rows, capacity, padded, info, *refs):
    blocks = refs[:count]
    compact, place, own_parts, table, parts = refs[count:]
    width = compact.shape[1]
    per_row = width // tokens
    for i, block in enumerate(blocks):
        @pl.when(info[which_at] == i)
        def _():
            table[...] = block[tokens:, :].astype(F32)

    def parts_of(expert):
        row, lane = expert // per_row, pl.multiple_of((expert % per_row) * tokens, tokens)
        parts[...] = jnp.zeros_like(parts)
        for p in range(3):
            found = lax.broadcasted_iota(I32, (table.shape[0], tokens), 0) == p * part_rows + row
            parts[p:p + 1, :] = jnp.sum(
                jnp.where(found, table[:, pl.ds(lane, tokens)], 0.0), axis=0, keepdims=True)
        return parts[...]

    own_parts[...] = parts_of(info[0]).astype(BF)
    theirs = parts_of(info[1])
    named = jnp.sum(theirs, axis=0, keepdims=True) > 0.0
    row_at = lax.broadcasted_iota(I32, (tokens, tokens), 0)
    column_at = lax.broadcasted_iota(I32, (tokens, tokens), 1)
    until = (row_at <= column_at).astype(F32).astype(BF)
    ones = jnp.broadcast_to(named.astype(F32), (TAIL, tokens)).astype(BF)
    rank = jnp.dot(ones, until, preferred_element_type=F32)[:1, :].astype(I32) - 1
    picked = ((row_at == rank) & named & (row_at < capacity)).astype(F32).astype(BF)
    place[...] = picked[:padded, :]
    for i, block in enumerate(blocks):
        @pl.when(info[which_at] == i)
        def _():
            compact[:padded, :] = jnp.dot(
                place[...], block[:tokens, :], preferred_element_type=F32).astype(BF)
    compact[padded:, :] = jnp.zeros((TAIL, width), BF)
    compact[padded:, :tokens] = dot(theirs.astype(BF), picked, ((1,), (1,))).astype(BF)


def grad_slot_kernel(count, which_at, info, *refs):
    blocks = refs[:count]
    place, compact = refs[count:]
    for i, block in enumerate(blocks):
        @pl.when(info[which_at] == i)
        def _():
            compact[...] = jnp.dot(
                place[...], block[...], preferred_element_type=F32).astype(BF)


def line_kernel(counts, which_at, place_at, tokens, info, *refs):
    whole = refs[-1]
    at = 0
    for slot, count in enumerate(counts):
        first = pl.multiple_of(info[place_at + slot] * tokens, tokens)
        for i in range(count):
            block = refs[at + i]

            @pl.when(info[which_at + slot] == i)
            def _():
                whole[pl.ds(first, tokens), :] = block[:tokens, :]
        at += count


def rows_copies(lines, tokens, padded, width, place_at, info, dense, compact, rows, sems):
    core = info[2]
    copies = []
    for half in range(2):
        lane = pl.multiple_of((core if half == 0 else 1 - core) * width, width)
        copies.append(pltpu.make_async_copy(
            dense[half], rows.at[pl.ds(0, lines * tokens), pl.ds(lane, width)],
            sems.at[len(copies)]))
        for j in range(lines):
            first = pl.multiple_of(lines * tokens + info[place_at + j] * padded, 16)
            copies.append(pltpu.make_async_copy(
                compact[half][j].at[pl.ds(0, padded), :],
                rows.at[pl.ds(first, padded), pl.ds(lane, width)],
                sems.at[len(copies)]))
    for copy in copies:
        copy.start()
    return copies


def token_rows_kernel(lines, tokens, padded, width, place_at, info, *refs):
    n = lines
    dense = refs[:2]
    compact = (refs[2:2 + n], refs[2 + n:2 + 2 * n])
    own_parts = refs[2 + 2 * n:2 + 3 * n]
    places = refs[2 + 3 * n:2 + 4 * n]
    rows, weights, ring, sems = refs[2 + 4 * n:]
    copies = rows_copies(n, tokens, padded, width, place_at, info, dense, compact, rows, sems)
    eye = (lax.broadcasted_iota(I32, (tokens, tokens), 0)
           == lax.broadcasted_iota(I32, (tokens, tokens), 1))
    for j in range(n):
        at = info[place_at + j]
        for first, size, tail in (
            (0, tokens, own_parts[j][...]),
            (n * tokens, padded, compact[0][j][padded:, :tokens]),
        ):
            row = jnp.sum(tail.astype(F32), axis=0, keepdims=True)
            column = jnp.sum(jnp.where(eye, row, 0.0), axis=1, keepdims=True)
            weights[pl.ds(pl.multiple_of(first + at * size, 16), size), :] = column[:size]
        ring[at] = places[j][...]
    for copy in copies:
        copy.wait()


def grad_rows_kernel(lines, tokens, padded, width, place_at, info, *refs):
    n = lines
    dense = refs[:2]
    compact = (refs[2:2 + n], refs[2 + n:2 + 2 * n])
    rows, sems = refs[2 + 2 * n:]
    for copy in rows_copies(n, tokens, padded, width, place_at, info, dense, compact, rows, sems):
        copy.wait()


def pack_kernel(lines, tokens, padded, tailed, info, both, *refs):
    tails, messages = (refs[0], refs[1:]) if tailed else (None, refs)
    for k in range(lines):
        at = lines * tokens + k * padded
        messages[k][:padded, :] = both[at:at + padded, :].astype(BF)
        if tails is not None:
            messages[k][padded:, :] = jnp.zeros((TAIL, both.shape[1]), BF)
            messages[k][padded:, :tokens] = tails[k].astype(BF)


def home_kernel(k, tokens, padded, tailed, info, both, back, ring, *refs):
    message = refs[-1]
    place = ring[k]
    block = both[k * tokens:(k + 1) * tokens, :] + dot(place, back[:padded, :], ((0,), (0,)))
    message[:tokens, :] = block.astype(BF)
    if not tailed:
        return
    tails = refs[0]
    message[tokens:, :] = jnp.zeros((TAIL, both.shape[1]), BF)
    theirs = dot(back[padded:, :padded], place, ((1,), (0,)))
    message[tokens:, :tokens] = jnp.concatenate(
        [tails[k][:8], theirs[:8]], axis=0).astype(BF)


def per_device(tokens, expert_ids, router_weights, gate_weight, up_weight, down_weight, grad_out):
    token_count, half_width = tokens.shape
    top_count = expert_ids.shape[1]
    experts = lax.axis_size("expert")
    capacity = min(token_count, 3 * token_count * top_count // (2 * experts))
    padded = -(-capacity // 16) * 16
    lines = experts // 2
    mine = lax.axis_index("expert")
    core = lax.axis_index("tensor")
    at_line = mine // 2
    peer = mine + 1 - 2 * (mine % 2)

    def over_pair(x):
        return lax.ppermute(x, "expert", [(i, i + 1 - 2 * (i % 2)) for i in range(experts)])

    def over_line(x, k):
        return lax.ppermute(
            x, "expert",
            [(i, ((i // 2 + k) % lines) * 2 + i % 2) for i in range(experts)],
        )

    def hop(x, k, step):
        low, high = (k - 1, lines - 1) if step > 0 else (1, lines - k + 1)
        return lax.ppermute(
            x, "expert",
            [(2 * z + y, 2 * (z + step) + y) for z in range(low, high) for y in range(2)],
        )

    def over_core(x):
        return lax.ppermute(x, "tensor", [(0, 1), (1, 0)])

    chosen = expert_ids[:, :, None] == jnp.arange(experts, dtype=I32)[None, None, :]
    table = jnp.sum(jnp.where(chosen, router_weights[:, :, None], 0.0), axis=1).T
    part_rows = experts * token_count // half_width
    parts = jnp.concatenate([p.reshape(part_rows, half_width) for p in split_three(table)])
    tail = -(-3 * part_rows // TAIL) * TAIL
    parts = jnp.pad(parts, ((0, tail - 3 * part_rows), (0, 0)))
    first = jnp.concatenate([tokens, parts])

    def sources_of(slot):
        if slot == 0:
            return [(None, 0)], np.zeros(lines, np.int32)
        sources = [slot_source(lines, z, slot) for z in range(lines)]
        names = sorted(set(sources))
        return names, np.array([names.index(n) for n in sources], np.int32)

    names_of = [sources_of(slot)[0] for slot in range(lines)]
    which_of = np.stack([sources_of(slot)[1] for slot in range(lines)], 1)
    place_of = np.array([[slot_place(lines, z, n) for n in range(lines)] for z in range(lines)], np.int32)
    known = jnp.asarray(np.concatenate([which_of, place_of], 1))[at_line]
    info = jnp.concatenate([jnp.stack([mine, peer, core]).astype(I32), known])
    which_at, place_at = 3, 3 + lines
    counts = [len(n) for n in names_of]
    dense_rows = lines * token_count
    row_count = lines * (token_count + padded)
    rows_shape = shape_of((row_count, 2 * half_width))
    sems = (pltpu.SemaphoreType.DMA((2 * (lines + 1),)),)
    sizes = (lines, token_count, padded, half_width, place_at)
    gate_local = gate_weight[0]
    up_local = up_weight[0]
    down_local = down_weight[0]

    def candidates(slot, ups, downs):
        return [(downs if d == "down" else ups)[n] for d, n in names_of[slot]]

    def token_slot(slot, ups, downs):
        blocks = candidates(slot, ups, downs)
        return local_call(
            functools.partial(token_slot_kernel, len(blocks), which_at + slot, token_count,
                              part_rows, capacity, padded),
            (shape_of((padded + TAIL, half_width)), shape_of((padded, token_count)),
             shape_of((TAIL, token_count))),
            (info, *blocks),
            (pltpu.VMEM((tail, half_width), F32), pltpu.VMEM((TAIL, token_count), F32)),
        )

    def grad_slot(slot, ups, downs, place):
        blocks = candidates(slot, ups, downs)
        return local_call(
            functools.partial(grad_slot_kernel, len(blocks), which_at + slot),
            (shape_of((padded, half_width)),), (info, *blocks, place))[0]

    def lined(ups, downs):
        blocks = [x for slot in range(lines) for x in candidates(slot, ups, downs)]
        return local_call(
            functools.partial(line_kernel, counts, which_at, place_at, token_count),
            (shape_of((lines * token_count, half_width)),), (info, *blocks), flops=10**6)[0]

    def summed_over_cores(make):
        sent = over_core(make(1 - core).astype(BF))
        return make(core) + sent.astype(F32)

    def half_of(x, which, axis):
        return lax.dynamic_slice_in_dim(x, which * half_width, half_width, axis)

    def packed_rows(both, *tails):
        extra = TAIL if tails else 0
        return list(local_call(
            functools.partial(pack_kernel, lines, token_count, padded, bool(tails)),
            (shape_of((padded + extra, half_width)),) * lines, (info, both, *tails), flops=10**6))

    def to_home(k, both, back, ring, *tails):
        extra = TAIL if tails else 0
        return local_call(
            functools.partial(home_kernel, k, token_count, padded, bool(tails)),
            (shape_of((token_count + extra, half_width)),), (info, both, back, ring, *tails))[0]

    def summed(blocks):
        total = blocks[0][:token_count].astype(F32)
        for block in blocks[1:]:
            total = total + block[:token_count].astype(F32)
        return total.astype(BF)

    def tails_of(values):
        values = jnp.pad(values, ((0, 0), (0, token_count - values.shape[1])))
        parts = jnp.stack([p.astype(F32) for p in split_three(values)], axis=1)
        return jnp.pad(parts, ((0, 0), (0, TAIL - 3), (0, 0)))

    settle = lax.optimization_barrier

    up, down = {0: first}, {0: first}
    grad_ups, grad_downs = {0: grad_out}, {0: grad_out}
    compact, compact_other, places, own_parts = {}, {}, {}, {}

    def token_pair(slot):
        block, places[slot], own_parts[slot] = token_slot(slot, up, down)
        compact[slot] = over_pair(block)

    for k in range(1, lines):
        up[k], down[k] = hop(up[k - 1], k, 1), hop(down[k - 1], k, -1)
        token_pair(k - 1)
        if k > 1:
            compact_other[k - 2] = over_core(compact[k - 2])
        up, down, grad_ups, grad_downs, compact, compact_other, places, own_parts = settle(
            (up, down, grad_ups, grad_downs, compact, compact_other, places, own_parts))

    def grad_hop(k):
        grad_ups[k], grad_downs[k] = hop(grad_ups[k - 1], k, 1), hop(grad_downs[k - 1], k, -1)

    grad_hop(1)
    token_pair(lines - 1)
    if lines > 1:
        compact_other[lines - 2] = over_core(compact[lines - 2])
    dense_own = lined(up, down)
    dense_other = over_core(dense_own)
    grad_ups, grad_downs, compact, compact_other, places, own_parts, dense_own, dense_other = settle(
        (grad_ups, grad_downs, compact, compact_other, places, own_parts, dense_own, dense_other))

    grad_compact, grad_other = {}, {}

    def grad_pair(slot):
        grad_compact[slot] = over_pair(grad_slot(slot, grad_ups, grad_downs, places[slot]))

    grad_hop(2)
    grad_pair(0)
    compact_other[lines - 1] = over_core(compact[lines - 1])
    order = range(lines)
    rows, weights, ring = local_call(
        functools.partial(token_rows_kernel, *sizes),
        (rows_shape, shape_of((row_count, 1), F32), shape_of((lines, padded, token_count))),
        (info, dense_own, dense_other, *[compact[j] for j in order],
         *[compact_other[j] for j in order], *[own_parts[j] for j in order],
         *[places[j] for j in order]),
        sems, flops=10**6)
    gate = dot(rows, gate_local, ((1,), (0,)))
    upward = dot(rows, up_local, ((1,), (0,)))
    hidden = gate * jax.nn.sigmoid(gate) * upward
    scaled_hidden = (weights * hidden).astype(BF)
    out_both = summed_over_cores(
        lambda c: dot(scaled_hidden, half_of(down_local, c, 1), ((1,), (0,))))
    saved = (rows, weights, ring, gate, upward, scaled_hidden)
    grad_ups, grad_downs, grad_compact, places, saved, out_both = settle(
        (grad_ups, grad_downs, grad_compact, places, saved, out_both))

    sent_order = sorted(range(1, lines), key=lambda k: -min(k, lines - k)) + [0]
    out_packed = packed_rows(out_both)
    out_back = {}
    for k in range(3, lines):
        grad_hop(k)
        grad_pair(k - 2)
        grad_other[k - 3] = over_core(grad_compact[k - 3])
        if k == 3:
            out_back[sent_order[0]] = over_pair(out_packed[sent_order[0]])
        grad_ups, grad_downs, grad_compact, grad_other, places, saved, out_both, out_packed, out_back = settle(
            (grad_ups, grad_downs, grad_compact, grad_other, places, saved, out_both, out_packed, out_back))

    rows, weights, ring, gate, upward, scaled_hidden = saved
    grad_pair(lines - 2)
    grad_pair(lines - 1)
    grad_own = lined(grad_ups, grad_downs)
    grad_line_other = over_core(grad_own)
    out_home = {}

    def out_send(k):
        block = to_home(k, out_both, out_back[k], ring)
        out_home[k] = over_line(block, lines - k) if k else block

    out_send(sent_order[0])
    grad_other[lines - 3] = over_core(grad_compact[lines - 3])
    (grad_compact, grad_other, grad_own, grad_line_other, saved, out_both, out_packed, out_home) = settle(
        (grad_compact, grad_other, grad_own, grad_line_other, saved, out_both, out_packed, out_home))

    rows, weights, ring, gate, upward, scaled_hidden = saved
    for k in sent_order[1:]:
        out_back[k] = over_pair(out_packed[k])
        out_send(k)
    for j in (lines - 2, lines - 1):
        grad_other[j] = over_core(grad_compact[j])
    (grads,) = local_call(
        functools.partial(grad_rows_kernel, *sizes), (rows_shape,),
        (info, grad_own, grad_line_other, *[grad_compact[j] for j in order],
         *[grad_other[j] for j in order]),
        sems, flops=10**6)
    sig = jax.nn.sigmoid(gate)
    grad_plain = dot(grads, down_local, ((1,), (1,)))
    row_value = jnp.sum(gate * sig * upward * grad_plain, axis=1)
    grad_hidden = weights * grad_plain
    grad_gate = (grad_hidden * upward * sig * (1.0 + gate * (1.0 - sig))).astype(BF)
    grad_up = (grad_hidden * gate * sig).astype(BF)
    in_both = summed_over_cores(
        lambda c: dot(grad_gate, half_of(gate_local, c, 0), ((1,), (1,)))
        + dot(grad_up, half_of(up_local, c, 0), ((1,), (1,))))
    dense_tails = tails_of(row_value[:dense_rows].reshape(lines, token_count))
    compact_tails = tails_of(row_value[dense_rows:].reshape(lines, padded))
    in_packed = packed_rows(in_both, compact_tails)
    in_packed, in_both, dense_tails, ring, out_home, rows, scaled_hidden, grad_gate, grad_up, grads = settle(
        (in_packed, in_both, dense_tails, ring, out_home, rows, scaled_hidden, grad_gate, grad_up, grads))

    layer_out = summed([out_home[k] for k in range(lines)])
    came_home = {}
    for k in sent_order:
        block = to_home(k, in_both, over_pair(in_packed[k]), ring, dense_tails)
        came_home[k] = over_line(block, lines - k) if k else block
    input_grad = summed([came_home[k] for k in range(lines)])

    down_grad = dot(scaled_hidden, grads, ((0,), (0,))).astype(BF)
    gate_grad = dot(rows, grad_gate, ((0,), (0,))).astype(BF)
    up_grad = dot(rows, grad_up, ((0,), (0,))).astype(BF)

    held = []
    for k in range(lines):
        rows_back = came_home[k][token_count:, :token_count].astype(F32)
        held.append(jnp.stack([jnp.sum(rows_back[:8], axis=0), jnp.sum(rows_back[8:], axis=0)]))
    flat = jnp.stack(held).reshape(experts, token_count)
    place = (expert_ids // 2 - at_line) % lines
    slot = place * 2 + ((expert_ids % 2) != (mine % 2)).astype(I32)
    match = slot[:, :, None] == jnp.arange(experts, dtype=I32)[None, None, :]
    half_value = jnp.sum(jnp.where(match, flat.T[:, None, :], 0.0), axis=2)
    weight_grad = half_value + over_core(half_value)
    return (layer_out, input_grad, weight_grad, gate_grad[None], up_grad[None], down_grad[None])


def solution(mesh):
    in_specs = (
        P(("group", "expert"), "tensor"),
        P(("group", "expert"), None),
        P(("group", "expert"), None),
        P("expert", None, "tensor"),
        P("expert", None, "tensor"),
        P("expert", "tensor", None),
        P(("group", "expert"), "tensor"),
    )
    out_specs = (
        P(("group", "expert"), "tensor"),
        P(("group", "expert"), "tensor"),
        P(("group", "expert"), None),
        P(("group", "expert"), None, "tensor"),
        P(("group", "expert"), None, "tensor"),
        P(("group", "expert"), "tensor", None),
    )
    return jax.shard_map(
        per_device, mesh=mesh, in_specs=in_specs, out_specs=out_specs, check_vma=False
    )
```

```python
import functools

import jax
import jax.numpy as jnp
import numpy as np
from jax import lax
from jax.experimental import pallas as pl
from jax.experimental.pallas import tpu as pltpu
from jax.sharding import PartitionSpec as P

BF = jnp.bfloat16
F32 = jnp.float32
I32 = jnp.int32
TAIL = 16
ROWS = ((1,), (0,))
LAST = ((1,), (1,))
FIRST = ((0,), (0,))

SMEM_SPEC = pl.BlockSpec(memory_space=pltpu.SMEM)
VMEM_SPEC = pl.BlockSpec(memory_space=pltpu.VMEM)


def dot(a, b, contract):
    return lax.dot_general(a, b, (contract, ((), ())), preferred_element_type=F32)


def split_three(values):
    high = lax.reduce_precision(values, 8, 7)
    rest = values - high
    middle = lax.reduce_precision(rest, 8, 7)
    low = rest - middle
    return [part.astype(BF) for part in (high, middle, low)]


def shape_of(shape, dtype=BF):
    return jax.ShapeDtypeStruct(shape, dtype)


def local_call(kernel, outs, args, scratch=()):
    total = sum(int(np.prod(x.shape)) * x.dtype.itemsize for x in tuple(args) + tuple(outs))
    return pl.pallas_call(
        kernel,
        out_shape=tuple(outs),
        in_specs=[SMEM_SPEC] + [VMEM_SPEC] * (len(args) - 1),
        out_specs=(VMEM_SPEC,) * len(outs),
        scratch_shapes=list(scratch),
        compiler_params=pltpu.CompilerParams(vmem_limit_bytes=int(total * 1.25) + 4 * 1024 * 1024),
        cost_estimate=pl.CostEstimate(flops=1000, bytes_accessed=1000, transcendentals=0),
    )(*args)


def row_chunks(count):
    pieces = -(-count // 256)
    if count % (16 * pieces):
        pieces = 1
    return pieces, count // pieces


def token_pack_kernel(tokens, part_rows, capacity, padded, info, block, compact, place, own_parts, table, parts):
    width = compact.shape[1]
    per_row = width // tokens
    table[...] = block[tokens:, :].astype(F32)

    def parts_of(expert):
        row, lane = expert // per_row, pl.multiple_of((expert % per_row) * tokens, tokens)
        parts[...] = jnp.zeros_like(parts)
        for p in range(3):
            found = lax.broadcasted_iota(I32, (table.shape[0], tokens), 0) == p * part_rows + row
            parts[p:p + 1, :] = jnp.sum(
                jnp.where(found, table[:, pl.ds(lane, tokens)], 0.0), axis=0, keepdims=True)
        return parts[...]

    own_parts[...] = parts_of(info[0]).astype(BF)
    theirs = parts_of(info[1])
    named = jnp.sum(theirs, axis=0, keepdims=True) > 0.0
    row_at = lax.broadcasted_iota(I32, (tokens, tokens), 0)
    column_at = lax.broadcasted_iota(I32, (tokens, tokens), 1)
    until = (row_at <= column_at).astype(F32).astype(BF)
    ones = jnp.broadcast_to(named.astype(F32), (TAIL, tokens)).astype(BF)
    rank = jnp.dot(ones, until, preferred_element_type=F32)[:1, :].astype(I32) - 1
    picked = ((row_at == rank) & named & (row_at < capacity)).astype(F32).astype(BF)
    place[...] = picked[:padded, :]
    compact[:padded, :] = dot(picked[:padded, :], block[:tokens, :], ROWS).astype(BF)
    compact[padded:, :] = jnp.zeros((TAIL, width), BF)
    compact[padded:, :tokens] = dot(theirs.astype(BF), picked, LAST).astype(BF)


def grad_pack_kernel(info, block, place, compact):
    compact[...] = dot(place[...], block[...], ROWS).astype(BF)


def lay_out(lines, tokens, padded, blocks, compact, rows):
    for k in range(lines):
        rows[k * tokens:(k + 1) * tokens, :] = blocks[k][:tokens, :]
        at = lines * tokens + k * padded
        rows[at:at + padded, :] = compact[k][:padded, :]


def token_rows_kernel(lines, tokens, padded, info, *refs):
    n = lines
    blocks, compact, own_parts = refs[:n], refs[n:2 * n], refs[2 * n:3 * n]
    rows, weights = refs[3 * n:]
    lay_out(n, tokens, padded, blocks, compact, rows)
    eye = (lax.broadcasted_iota(I32, (tokens, tokens), 0)
           == lax.broadcasted_iota(I32, (tokens, tokens), 1))
    for k in range(n):
        for first, size, tail in (
            (k * tokens, tokens, own_parts[k][...]),
            (n * tokens + k * padded, padded, compact[k][padded:, :tokens]),
        ):
            row = jnp.sum(tail.astype(F32), axis=0, keepdims=True)
            column = jnp.sum(jnp.where(eye, row, 0.0), axis=1, keepdims=True)
            weights[first:first + size, :] = column[:size]


def grad_rows_kernel(lines, tokens, padded, info, *refs):
    lay_out(lines, tokens, padded, refs[:lines], refs[lines:2 * lines], refs[2 * lines])


def halves(info, width):
    core = info[2]
    return pl.ds(pl.multiple_of(core * width, width), width), pl.ds(pl.multiple_of((1 - core) * width, width), width)


def forward_kernel(pieces, chunk, info, own, other, weights, gate_w, up_w, down_w, gate, upward, scaled, sent):
    mine, theirs = halves(info, own.shape[1])

    @pl.loop(0, pieces)
    def _(i):
        at = pl.ds(pl.multiple_of(i * chunk, 16), chunk)
        a, b = own[at, :], other[at, :]
        g = dot(a, gate_w[mine, :], ROWS) + dot(b, gate_w[theirs, :], ROWS)
        u = dot(a, up_w[mine, :], ROWS) + dot(b, up_w[theirs, :], ROWS)
        gate[at, :] = g
        upward[at, :] = u
        h = (weights[at, :] * (g * jax.nn.sigmoid(g) * u)).astype(BF)
        scaled[at, :] = h
        sent[at, :] = dot(h, down_w[:, theirs], ROWS).astype(BF)


def backward_kernel(pieces, chunk, lines, tokens, padded, info, own, other, weights, gate, upward, gate_w, up_w,
                    down_w, grad_gate, grad_up, sent, dense_tails, compact_tails, values):
    mine, theirs = halves(info, own.shape[1])

    @pl.loop(0, pieces)
    def _(i):
        at = pl.ds(pl.multiple_of(i * chunk, 16), chunk)
        plain = dot(own[at, :], down_w[:, mine], LAST) + dot(other[at, :], down_w[:, theirs], LAST)
        g, u = gate[at, :], upward[at, :]
        sig = jax.nn.sigmoid(g)
        through = g * sig
        values[at, :] = jnp.sum(through * u * plain, axis=1, keepdims=True)
        scaled = weights[at, :] * plain
        gg = (scaled * u * sig * (1.0 + g * (1.0 - sig))).astype(BF)
        gu = (scaled * through).astype(BF)
        grad_gate[at, :] = gg
        grad_up[at, :] = gu
        sent[at, :] = (dot(gg, gate_w[theirs, :], LAST) + dot(gu, up_w[theirs, :], LAST)).astype(BF)

    eye = (lax.broadcasted_iota(I32, (tokens, tokens), 0)
           == lax.broadcasted_iota(I32, (tokens, tokens), 1))
    for k in range(lines):
        for first, size, tails in (
            (k * tokens, tokens, dense_tails),
            (lines * tokens + k * padded, padded, compact_tails),
        ):
            column = values[first:first + size, :]
            row = jnp.sum(jnp.where(eye[:size, :], column, 0.0), axis=0, keepdims=True)
            high = row.astype(BF).astype(F32)
            middle = (row - high).astype(BF).astype(F32)
            low = row - high - middle
            at = lax.broadcasted_iota(I32, (TAIL, tokens), 0)
            tails[k] = jnp.where(at == 0, high, jnp.where(at == 1, middle, jnp.where(at == 2, low, 0.0)))


def join_kernel(lines, tokens, padded, forward, info, came, *refs):
    width = came.shape[1]
    mine, _ = halves(info, width)
    if forward:
        scaled, down_w = refs[:2]
        dense, messages = refs[2], refs[3:]

        def product(at):
            return dot(scaled[at, :], down_w[:, mine], ROWS)
    else:
        grad_gate, grad_up, gate_w, up_w, tails = refs[:5]
        dense, messages = refs[5], refs[6:]

        def product(at):
            return dot(grad_gate[at, :], gate_w[mine, :], LAST) + dot(grad_up[at, :], up_w[mine, :], LAST)

    for k in range(lines):
        at = slice(lines * tokens + k * padded, lines * tokens + (k + 1) * padded)
        messages[k][:padded, :] = (product(at) + came[at, :].astype(F32)).astype(BF)
        if not forward:
            messages[k][padded:, :] = jnp.zeros((TAIL, width), BF)
            messages[k][padded:, :tokens] = tails[k].astype(BF)
    for k in range(lines):
        at = slice(k * tokens, (k + 1) * tokens)
        dense[k] = product(at) + came[at, :].astype(F32)


def home_kernel(k, tokens, padded, tailed, info, dense, back, place, *refs):
    message = refs[-1]
    block = dense[k] + dot(place[...], back[:padded, :], FIRST)
    message[:tokens, :] = block.astype(BF)
    if not tailed:
        return
    tails = refs[0]
    message[tokens:, :] = jnp.zeros((TAIL, message.shape[1]), BF)
    theirs = dot(back[padded:, :padded], place[...], ROWS)
    message[tokens:, :tokens] = jnp.concatenate([tails[k][:8], theirs[:8]], axis=0).astype(BF)


def per_device(tokens, expert_ids, router_weights, gate_weight, up_weight, down_weight, grad_out):
    token_count, half_width = tokens.shape
    hidden_half = gate_weight.shape[2]
    top_count = expert_ids.shape[1]
    experts = lax.axis_size("expert")
    capacity = min(token_count, 3 * token_count * top_count // (2 * experts))
    padded = -(-capacity // 16) * 16
    lines = experts // 2
    mine = lax.axis_index("expert")
    core = lax.axis_index("tensor")
    at_line = mine // 2
    peer = mine + 1 - 2 * (mine % 2)
    settle = lax.optimization_barrier

    def over_pair(x):
        return lax.ppermute(x, "expert", [(i, i + 1 - 2 * (i % 2)) for i in range(experts)])

    def over_line(x, k):
        return lax.ppermute(
            x, "expert",
            [(i, ((i // 2 + k) % lines) * 2 + i % 2) for i in range(experts)],
        )

    def over_core(x):
        return lax.ppermute(x, "tensor", [(0, 1), (1, 0)])

    chosen = expert_ids[:, :, None] == jnp.arange(experts, dtype=I32)[None, None, :]
    table = jnp.sum(jnp.where(chosen, router_weights[:, :, None], 0.0), axis=1).T
    part_rows = experts * token_count // half_width
    parts = jnp.concatenate([p.reshape(part_rows, half_width) for p in split_three(table)])
    tail = -(-3 * part_rows // TAIL) * TAIL
    parts = jnp.pad(parts, ((0, tail - 3 * part_rows), (0, 0)))
    first = jnp.concatenate([tokens, parts])

    info = jnp.stack([mine, peer, core]).astype(I32)
    sizes = (lines, token_count, padded)
    row_count = lines * (token_count + padded)
    half_rows = shape_of((row_count, half_width))
    hidden_rows = (row_count, hidden_half)
    gate_local = gate_weight[0]
    up_local = up_weight[0]
    down_local = down_weight[0]
    pieces, chunk = row_chunks(row_count)
    every = range(lines)
    by_reach = sorted(range(1, lines), key=lambda k: min(k, lines - k))

    blocks = {0: first}
    for k in by_reach:
        blocks[k] = over_line(first, k)
    compact, places, own_parts = {}, {}, {}
    for k in [0] + by_reach:
        packed, places[k], own_parts[k] = local_call(
            functools.partial(token_pack_kernel, token_count, part_rows, capacity, padded),
            (shape_of((padded + TAIL, half_width)), shape_of((padded, token_count)),
             shape_of((TAIL, token_count))),
            (info, blocks[k]),
            (pltpu.VMEM((tail, half_width), F32), pltpu.VMEM((TAIL, token_count), F32)),
        )
        compact[k] = over_pair(packed)

    held_grad, blocks = settle((grad_out, blocks))
    grad_blocks = {0: held_grad}
    for k in by_reach:
        grad_blocks[k] = over_line(held_grad, k)

    rows, weights = local_call(
        functools.partial(token_rows_kernel, *sizes),
        (half_rows, shape_of((row_count, 1), F32)),
        (info, *[blocks[k] for k in every], *[compact[k] for k in every], *[own_parts[k] for k in every]))
    rows_other = over_core(rows)
    gate, upward, scaled, sent = local_call(
        functools.partial(forward_kernel, pieces, chunk),
        (shape_of(hidden_rows, F32), shape_of(hidden_rows, F32), shape_of(hidden_rows), half_rows),
        (info, rows, rows_other, weights, gate_local, up_local, down_local))
    out_dense, *out_packed = local_call(
        functools.partial(join_kernel, *sizes, True),
        (shape_of((lines, token_count, half_width), F32),
         *[shape_of((padded, half_width)) for _ in every]),
        (info, over_core(sent), scaled, down_local))

    grad_compact = {}
    for k in [0] + by_reach:
        (packed,) = local_call(
            grad_pack_kernel, (shape_of((padded, half_width)),), (info, grad_blocks[k], places[k]))
        grad_compact[k] = over_pair(packed)
    out_back = {k: over_pair(out_packed[k]) for k in every}
    (grad_rows,) = local_call(
        functools.partial(grad_rows_kernel, *sizes), (half_rows,),
        (info, *[grad_blocks[k] for k in every], *[grad_compact[k] for k in every]))
    grad_rows, out_packed = settle((grad_rows, out_packed))
    grad_other = over_core(grad_rows)
    grad_gate, grad_up, sent, dense_tails, compact_tails = local_call(
        functools.partial(backward_kernel, pieces, chunk, *sizes),
        (shape_of(hidden_rows), shape_of(hidden_rows), half_rows,
         shape_of((lines, TAIL, token_count), F32), shape_of((lines, TAIL, token_count), F32)),
        (info, grad_rows, grad_other, weights, gate, upward, gate_local, up_local, down_local),
        (pltpu.VMEM((row_count, 1), F32),))
    sent, out_back = settle((sent, out_back))
    out_home = {}
    for k in by_reach[::-1] + [0]:
        (block,) = local_call(
            functools.partial(home_kernel, k, token_count, padded, False),
            (shape_of((token_count, half_width)),), (info, out_dense, out_back[k], places[k]))
        out_home[k] = over_line(block, lines - k) if k else block
    in_dense, *in_packed = local_call(
        functools.partial(join_kernel, *sizes, False),
        (shape_of((lines, token_count, half_width), F32),
         *[shape_of((padded + TAIL, half_width)) for _ in every]),
        (info, over_core(sent), grad_gate, grad_up, gate_local, up_local, compact_tails))
    in_packed, rows, rows_other, grad_rows, grad_other, scaled, grad_gate, grad_up = settle(
        (in_packed, rows, rows_other, grad_rows, grad_other, scaled, grad_gate, grad_up))
    in_back = {k: over_pair(in_packed[k]) for k in every}

    def summed(blocks):
        total = blocks[0][:token_count].astype(F32)
        for k in range(1, lines):
            total = total + blocks[k][:token_count].astype(F32)
        return total.astype(BF)

    layer_out = summed(out_home)
    in_back = {k: settle((in_back[k], layer_out))[0] for k in every}
    in_home = {}
    for k in by_reach[::-1] + [0]:
        (block,) = local_call(
            functools.partial(home_kernel, k, token_count, padded, True),
            (shape_of((token_count + TAIL, half_width)),),
            (info, in_dense, in_back[k], places[k], dense_tails))
        in_home[k] = over_line(block, lines - k) if k else block
    input_grad = summed(in_home)

    def whole(own, other):
        return jnp.concatenate(
            [jnp.where(core == 0, own, other), jnp.where(core == 0, other, own)], axis=1)

    rows = whole(rows, rows_other)
    grads = whole(grad_rows, grad_other)
    down_grad = dot(scaled, grads, FIRST).astype(BF)
    gate_grad = dot(rows, grad_gate, FIRST).astype(BF)
    up_grad = dot(rows, grad_up, FIRST).astype(BF)

    held = []
    for k in every:
        values = in_home[k][token_count:, :token_count].astype(F32)
        held.append(jnp.stack([jnp.sum(values[:8], axis=0), jnp.sum(values[8:], axis=0)]))
    flat = jnp.stack(held).reshape(experts, token_count)
    place = (expert_ids // 2 - at_line) % lines
    slot = place * 2 + ((expert_ids % 2) != (mine % 2)).astype(I32)
    match = slot[:, :, None] == jnp.arange(experts, dtype=I32)[None, None, :]
    half_value = jnp.sum(jnp.where(match, flat.T[:, None, :], 0.0), axis=2)
    weight_grad = half_value + over_core(half_value)
    return (layer_out, input_grad, weight_grad, gate_grad[None], up_grad[None], down_grad[None])


def solution(mesh):
    in_specs = (
        P(("group", "expert"), "tensor"),
        P(("group", "expert"), None),
        P(("group", "expert"), None),
        P("expert", None, "tensor"),
        P("expert", None, "tensor"),
        P("expert", "tensor", None),
        P(("group", "expert"), "tensor"),
    )
    out_specs = (
        P(("group", "expert"), "tensor"),
        P(("group", "expert"), "tensor"),
        P(("group", "expert"), None),
        P(("group", "expert"), None, "tensor"),
        P(("group", "expert"), None, "tensor"),
        P(("group", "expert"), "tensor", None),
    )
    return jax.shard_map(
        per_device, mesh=mesh, in_specs=in_specs, out_specs=out_specs, check_vma=False
    )
```

```python
import functools

import jax
import jax.numpy as jnp
import numpy as np
from jax import lax
from jax.experimental import pallas as pl
from jax.experimental.pallas import tpu as pltpu
from jax.sharding import PartitionSpec as P

BF = jnp.bfloat16
F32 = jnp.float32
I32 = jnp.int32
TAIL = 16
ROWS = ((1,), (0,))
LAST = ((1,), (1,))
FIRST = ((0,), (0,))

SMEM_SPEC = pl.BlockSpec(memory_space=pltpu.SMEM)
VMEM_SPEC = pl.BlockSpec(memory_space=pltpu.VMEM)


def dot(a, b, contract):
    return lax.dot_general(a, b, (contract, ((), ())), preferred_element_type=F32)


def split_three(values):
    high = lax.reduce_precision(values, 8, 7)
    rest = values - high
    middle = lax.reduce_precision(rest, 8, 7)
    low = rest - middle
    return [part.astype(BF) for part in (high, middle, low)]


def shape_of(shape, dtype=BF):
    return jax.ShapeDtypeStruct(shape, dtype)


def local_call(kernel, outs, args, scratch=()):
    total = sum(int(np.prod(x.shape)) * x.dtype.itemsize for x in tuple(args) + tuple(outs))
    return pl.pallas_call(
        kernel,
        out_shape=tuple(outs),
        in_specs=[SMEM_SPEC] + [VMEM_SPEC] * (len(args) - 1),
        out_specs=(VMEM_SPEC,) * len(outs),
        scratch_shapes=list(scratch),
        compiler_params=pltpu.CompilerParams(vmem_limit_bytes=int(total * 1.25) + 4 * 1024 * 1024),
        cost_estimate=pl.CostEstimate(flops=1000, bytes_accessed=1000, transcendentals=0),
    )(*args)


def row_chunks(count):
    pieces = -(-count // 512)
    if count % (16 * pieces):
        pieces = 1
    return pieces, count // pieces


def token_pack_kernel(tokens, part_rows, capacity, padded, info, block, compact, place, own_parts, table, parts):
    width = compact.shape[1]
    per_row = width // tokens
    table[...] = block[tokens:, :].astype(F32)

    def parts_of(expert):
        row, lane = expert // per_row, pl.multiple_of((expert % per_row) * tokens, tokens)
        parts[...] = jnp.zeros_like(parts)
        for p in range(3):
            found = lax.broadcasted_iota(I32, (table.shape[0], tokens), 0) == p * part_rows + row
            parts[p:p + 1, :] = jnp.sum(
                jnp.where(found, table[:, pl.ds(lane, tokens)], 0.0), axis=0, keepdims=True)
        return parts[...]

    own_parts[...] = parts_of(info[0]).astype(BF)
    theirs = parts_of(info[1])
    named = jnp.sum(theirs, axis=0, keepdims=True) > 0.0
    row_at = lax.broadcasted_iota(I32, (tokens, tokens), 0)
    column_at = lax.broadcasted_iota(I32, (tokens, tokens), 1)
    until = (row_at <= column_at).astype(F32).astype(BF)
    ones = jnp.broadcast_to(named.astype(F32), (TAIL, tokens)).astype(BF)
    rank = jnp.dot(ones, until, preferred_element_type=F32)[:1, :].astype(I32) - 1
    picked = ((row_at == rank) & named & (row_at < capacity)).astype(F32).astype(BF)
    place[...] = picked[:padded, :]
    compact[:padded, :] = dot(picked[:padded, :], block[:tokens, :], ROWS).astype(BF)
    compact[padded:, :] = jnp.zeros((TAIL, width), BF)
    compact[padded:, :tokens] = dot(theirs.astype(BF), picked, LAST).astype(BF)


def grad_pack_kernel(info, block, place, compact):
    compact[...] = dot(place[...], block[...], ROWS).astype(BF)


def lay_out(lines, tokens, padded, blocks, compact, rows):
    for k in range(lines):
        rows[k * tokens:(k + 1) * tokens, :] = blocks[k][:tokens, :]
        at = lines * tokens + k * padded
        rows[at:at + padded, :] = compact[k][:padded, :]


def token_rows_kernel(lines, tokens, padded, info, *refs):
    n = lines
    blocks, compact, own_parts = refs[:n], refs[n:2 * n], refs[2 * n:3 * n]
    rows, weights = refs[3 * n:]
    lay_out(n, tokens, padded, blocks, compact, rows)
    eye = (lax.broadcasted_iota(I32, (tokens, tokens), 0)
           == lax.broadcasted_iota(I32, (tokens, tokens), 1))
    for k in range(n):
        for first, size, tail in (
            (k * tokens, tokens, own_parts[k][...]),
            (n * tokens + k * padded, padded, compact[k][padded:, :tokens]),
        ):
            row = jnp.sum(tail.astype(F32), axis=0, keepdims=True)
            column = jnp.sum(jnp.where(eye, row, 0.0), axis=1, keepdims=True)
            weights[first:first + size, :] = column[:size]


def grad_rows_kernel(lines, tokens, padded, info, *refs):
    lay_out(lines, tokens, padded, refs[:lines], refs[lines:2 * lines], refs[2 * lines])


def halves(info, width):
    core = info[2]
    return pl.ds(pl.multiple_of(core * width, width), width), pl.ds(pl.multiple_of((1 - core) * width, width), width)


def forward_kernel(pieces, chunk, info, own, other, weights, gate_w, up_w, down_w, gate, upward, scaled, sent):
    mine, theirs = halves(info, own.shape[1])

    @pl.loop(0, pieces)
    def _(i):
        at = pl.ds(pl.multiple_of(i * chunk, 16), chunk)
        a, b = own[at, :], other[at, :]
        g = dot(a, gate_w[mine, :], ROWS) + dot(b, gate_w[theirs, :], ROWS)
        u = dot(a, up_w[mine, :], ROWS) + dot(b, up_w[theirs, :], ROWS)
        gate[at, :] = g
        upward[at, :] = u
        h = (weights[at, :] * (g * jax.nn.sigmoid(g) * u)).astype(BF)
        scaled[at, :] = h
        sent[at, :] = dot(h, down_w[:, theirs], ROWS).astype(BF)


def backward_kernel(pieces, chunk, lines, tokens, padded, info, own, other, weights, gate, upward, gate_w, up_w,
                    down_w, grad_gate, grad_up, sent, dense_tails, compact_tails, values):
    mine, theirs = halves(info, own.shape[1])

    @pl.loop(0, pieces)
    def _(i):
        at = pl.ds(pl.multiple_of(i * chunk, 16), chunk)
        plain = dot(own[at, :], down_w[:, mine], LAST) + dot(other[at, :], down_w[:, theirs], LAST)
        g, u = gate[at, :], upward[at, :]
        sig = jax.nn.sigmoid(g)
        through = g * sig
        values[at, :] = jnp.sum(through * u * plain, axis=1, keepdims=True)
        scaled = weights[at, :] * plain
        gg = (scaled * u * sig * (1.0 + g * (1.0 - sig))).astype(BF)
        gu = (scaled * through).astype(BF)
        grad_gate[at, :] = gg
        grad_up[at, :] = gu
        sent[at, :] = (dot(gg, gate_w[theirs, :], LAST) + dot(gu, up_w[theirs, :], LAST)).astype(BF)

    eye = (lax.broadcasted_iota(I32, (tokens, tokens), 0)
           == lax.broadcasted_iota(I32, (tokens, tokens), 1))
    for k in range(lines):
        for first, size, tails in (
            (k * tokens, tokens, dense_tails),
            (lines * tokens + k * padded, padded, compact_tails),
        ):
            column = values[first:first + size, :]
            row = jnp.sum(jnp.where(eye[:size, :], column, 0.0), axis=0, keepdims=True)
            high = row.astype(BF).astype(F32)
            middle = (row - high).astype(BF).astype(F32)
            low = row - high - middle
            at = lax.broadcasted_iota(I32, (TAIL, tokens), 0)
            tails[k] = jnp.where(at == 0, high, jnp.where(at == 1, middle, jnp.where(at == 2, low, 0.0)))


def join_kernel(lines, tokens, padded, forward, info, came, *refs):
    width = came.shape[1]
    mine, _ = halves(info, width)
    if forward:
        scaled, down_w = refs[:2]
        dense, messages = refs[2], refs[3:]

        def product(first, size):
            return dot(scaled[first:first + size, :], down_w[:, mine], ROWS)
    else:
        grad_gate, grad_up, gate_w, up_w, tails = refs[:5]
        dense, messages = refs[5], refs[6:]

        def product(first, size):
            at = slice(first, first + size)
            return dot(grad_gate[at, :], gate_w[mine, :], LAST) + dot(grad_up[at, :], up_w[mine, :], LAST)

    def joined(first, size):
        return product(first, size) + came[first:first + size, :].astype(F32)

    start = lines * tokens
    for first in range(0, lines, 4):
        count = min(4, lines - first)
        total = joined(start + first * padded, count * padded).astype(BF)
        for k in range(first, first + count):
            messages[k][:padded, :] = total[(k - first) * padded:(k - first + 1) * padded]
            if not forward:
                messages[k][padded:, :] = jnp.zeros((TAIL, width), BF)
                messages[k][padded:, :tokens] = tails[k].astype(BF)
    for first in range(0, lines, 4):
        count = min(4, lines - first)
        total = joined(first * tokens, count * tokens)
        for k in range(first, first + count):
            dense[k] = total[(k - first) * tokens:(k - first + 1) * tokens]


def home_kernel(k, tokens, padded, tailed, info, dense, back, place, *refs):
    message = refs[-1]
    block = dense[k] + dot(place[...], back[:padded, :], FIRST)
    message[:tokens, :] = block.astype(BF)
    if not tailed:
        return
    tails = refs[0]
    message[tokens:, :] = jnp.zeros((TAIL, message.shape[1]), BF)
    theirs = dot(back[padded:, :padded], place[...], ROWS)
    message[tokens:, :tokens] = jnp.concatenate([tails[k][:8], theirs[:8]], axis=0).astype(BF)


def per_device(tokens, expert_ids, router_weights, gate_weight, up_weight, down_weight, grad_out):
    token_count, half_width = tokens.shape
    hidden_half = gate_weight.shape[2]
    top_count = expert_ids.shape[1]
    experts = lax.axis_size("expert")
    capacity = min(token_count, 3 * token_count * top_count // (2 * experts))
    padded = -(-capacity // 16) * 16
    lines = experts // 2
    mine = lax.axis_index("expert")
    core = lax.axis_index("tensor")
    at_line = mine // 2
    peer = mine + 1 - 2 * (mine % 2)
    settle = lax.optimization_barrier

    def over_pair(x):
        return lax.ppermute(x, "expert", [(i, i + 1 - 2 * (i % 2)) for i in range(experts)])

    def over_line(x, k):
        return lax.ppermute(
            x, "expert",
            [(i, ((i // 2 + k) % lines) * 2 + i % 2) for i in range(experts)],
        )

    def over_core(x):
        return lax.ppermute(x, "tensor", [(0, 1), (1, 0)])

    chosen = expert_ids[:, :, None] == jnp.arange(experts, dtype=I32)[None, None, :]
    table = jnp.sum(jnp.where(chosen, router_weights[:, :, None], 0.0), axis=1).T
    part_rows = experts * token_count // half_width
    parts = jnp.concatenate([p.reshape(part_rows, half_width) for p in split_three(table)])
    tail = -(-3 * part_rows // TAIL) * TAIL
    parts = jnp.pad(parts, ((0, tail - 3 * part_rows), (0, 0)))
    first = jnp.concatenate([tokens, parts])

    info = jnp.stack([mine, peer, core]).astype(I32)
    sizes = (lines, token_count, padded)
    row_count = lines * (token_count + padded)
    half_rows = shape_of((row_count, half_width))
    hidden_rows = (row_count, hidden_half)
    gate_local = gate_weight[0]
    up_local = up_weight[0]
    down_local = down_weight[0]
    pieces, chunk = row_chunks(row_count)
    every = range(lines)
    by_reach = sorted(range(1, lines), key=lambda k: min(k, lines - k))

    blocks = {0: first}
    for k in by_reach:
        blocks[k] = over_line(first, k)
    compact, places, own_parts, early = {}, {}, {}, []
    for k in [0] + by_reach:
        packed, places[k], own_parts[k] = local_call(
            functools.partial(token_pack_kernel, token_count, part_rows, capacity, padded),
            (shape_of((padded + TAIL, half_width)), shape_of((padded, token_count)),
             shape_of((TAIL, token_count))),
            (info, blocks[k]),
            (pltpu.VMEM((tail, half_width), F32), pltpu.VMEM((TAIL, token_count), F32)),
        )
        if k != by_reach[-1]:
            early.append(packed)
        compact[k] = over_pair(packed)

    held_grad, blocks, early, compact[0] = settle((grad_out, blocks, early, compact[0]))
    grad_blocks = {0: held_grad}
    for k in by_reach:
        grad_blocks[k] = over_line(held_grad, k)

    grad_packed = {
        k: local_call(
            grad_pack_kernel, (shape_of((padded, half_width)),), (info, grad_blocks[k], places[k]))[0]
        for k in [0] + by_reach
    }
    grad_compact = {k: over_pair(grad_packed[k]) for k in [0] + by_reach}
    ahead = {k: grad_compact[k] for k in [0] + by_reach[:1]}
    compact, grad_blocks, grad_packed, ahead = settle((compact, grad_blocks, grad_packed, ahead))
    grad_compact.update(ahead)
    rows, weights = local_call(
        functools.partial(token_rows_kernel, *sizes),
        (half_rows, shape_of((row_count, 1), F32)),
        (info, *[blocks[k] for k in every], *[compact[k] for k in every], *[own_parts[k] for k in every]))
    rows_other = over_core(rows)
    ahead = {k: grad_compact[k] for k in by_reach[1:-1]}
    rows_other, ahead = settle((rows_other, ahead))
    grad_compact.update(ahead)
    gate, upward, scaled, sent = local_call(
        functools.partial(forward_kernel, pieces, chunk),
        (shape_of(hidden_rows, F32), shape_of(hidden_rows, F32), shape_of(hidden_rows), half_rows),
        (info, rows, rows_other, weights, gate_local, up_local, down_local))
    sent, grad_compact = settle((sent, grad_compact))
    out_dense, *out_packed = local_call(
        functools.partial(join_kernel, *sizes, True),
        (shape_of((lines, token_count, half_width), F32),
         *[shape_of((padded, half_width)) for _ in every]),
        (info, over_core(sent), scaled, down_local))

    outward = by_reach[::-1]
    out_back = {k: over_pair(out_packed[k]) for k in by_reach}
    last, _ = settle((out_packed[0], out_back[by_reach[0]]))
    out_back[0] = over_pair(last)
    (grad_rows,) = local_call(
        functools.partial(grad_rows_kernel, *sizes), (half_rows,),
        (info, *[grad_blocks[k] for k in every], *[grad_compact[k] for k in every]))
    grad_rows, out_packed = settle((grad_rows, out_packed))
    grad_other = over_core(grad_rows)
    grad_gate, grad_up, sent, dense_tails, compact_tails = local_call(
        functools.partial(backward_kernel, pieces, chunk, *sizes),
        (shape_of(hidden_rows), shape_of(hidden_rows), half_rows,
         shape_of((lines, TAIL, token_count), F32), shape_of((lines, TAIL, token_count), F32)),
        (info, grad_rows, grad_other, weights, gate, upward, gate_local, up_local, down_local),
        (pltpu.VMEM((row_count, 1), F32),))

    def to_home(k, dense, back, *tails):
        extra = TAIL if tails else 0
        return local_call(
            functools.partial(home_kernel, k, token_count, padded, bool(tails)),
            (shape_of((token_count + extra, half_width)),), (info, dense, back[k], places[k], *tails))[0]

    def summed(blocks):
        total = blocks[0][:token_count].astype(F32)
        for k in range(1, lines):
            total = total + blocks[k][:token_count].astype(F32)
        return total.astype(BF)

    sent, some = settle((sent, {k: out_back[k] for k in by_reach}))
    out_back.update(some)
    out_home = {k: to_home(k, out_dense, out_back) for k in by_reach + [0]}
    out_came = {k: over_line(out_home[k], lines - k) for k in by_reach}
    out_came[0] = out_home[0]
    in_dense, *in_packed = local_call(
        functools.partial(join_kernel, *sizes, False),
        (shape_of((lines, token_count, half_width), F32),
         *[shape_of((padded + TAIL, half_width)) for _ in every]),
        (info, over_core(sent), grad_gate, grad_up, gate_local, up_local, compact_tails))
    in_packed, early = settle((in_packed, {k: out_came[k] for k in by_reach[:-1]}))
    out_came.update(early)
    in_back, in_home, sequence = {}, {}, outward + [0]
    for i, k in enumerate(sequence):
        packed = in_packed[k]
        if i >= 2:
            packed, in_home[sequence[i - 2]] = settle((packed, in_home[sequence[i - 2]]))
        in_back[k] = over_pair(packed)
        in_home[k] = to_home(k, in_dense, in_back, dense_tails)
    in_home[outward[-1]], out_came = settle((in_home[outward[-1]], out_came))
    layer_out = summed(out_came)
    last_home, rows, rows_other, grad_rows, grad_other, scaled, grad_gate, grad_up = settle(
        ([in_home[k] for k in outward], rows, rows_other, grad_rows, grad_other, scaled, grad_gate, grad_up))
    in_home = {k: over_line(in_home[k], lines - k) if k else in_home[0] for k in every}
    input_grad = summed(in_home)

    def whole(own, other):
        return jnp.concatenate(
            [jnp.where(core == 0, own, other), jnp.where(core == 0, other, own)], axis=1)

    rows = whole(rows, rows_other)
    grads = whole(grad_rows, grad_other)
    down_grad = dot(scaled, grads, FIRST).astype(BF)
    gate_grad = dot(rows, grad_gate, FIRST).astype(BF)
    up_grad = dot(rows, grad_up, FIRST).astype(BF)

    held = []
    for k in every:
        values = in_home[k][token_count:, :token_count].astype(F32)
        held.append(jnp.stack([jnp.sum(values[:8], axis=0), jnp.sum(values[8:], axis=0)]))
    flat = jnp.stack(held).reshape(experts, token_count)
    place = (expert_ids // 2 - at_line) % lines
    slot = place * 2 + ((expert_ids % 2) != (mine % 2)).astype(I32)
    match = slot[:, :, None] == jnp.arange(experts, dtype=I32)[None, None, :]
    half_value = jnp.sum(jnp.where(match, flat.T[:, None, :], 0.0), axis=2)
    weight_grad = half_value + over_core(half_value)
    return (layer_out, input_grad, weight_grad, gate_grad[None], up_grad[None], down_grad[None])


def solution(mesh):
    in_specs = (
        P(("group", "expert"), "tensor"),
        P(("group", "expert"), None),
        P(("group", "expert"), None),
        P("expert", None, "tensor"),
        P("expert", None, "tensor"),
        P("expert", "tensor", None),
        P(("group", "expert"), "tensor"),
    )
    out_specs = (
        P(("group", "expert"), "tensor"),
        P(("group", "expert"), "tensor"),
        P(("group", "expert"), None),
        P(("group", "expert"), None, "tensor"),
        P(("group", "expert"), None, "tensor"),
        P(("group", "expert"), "tensor", None),
    )
    return jax.shard_map(
        per_device, mesh=mesh, in_specs=in_specs, out_specs=out_specs, check_vma=False
    )
```

```python
import functools

import jax
import jax.numpy as jnp
import numpy as np
from jax import lax
from jax.experimental import pallas as pl
from jax.experimental.pallas import tpu as pltpu
from jax.sharding import PartitionSpec as P

BF = jnp.bfloat16
F32 = jnp.float32
I32 = jnp.int32
TAIL = 16
ROWS = ((1,), (0,))
LAST = ((1,), (1,))
FIRST = ((0,), (0,))

SMEM_SPEC = pl.BlockSpec(memory_space=pltpu.SMEM)
VMEM_SPEC = pl.BlockSpec(memory_space=pltpu.VMEM)


def dot(a, b, contract):
    return lax.dot_general(a, b, (contract, ((), ())), preferred_element_type=F32)


def split_three(values):
    high = lax.reduce_precision(values, 8, 7)
    rest = values - high
    middle = lax.reduce_precision(rest, 8, 7)
    low = rest - middle
    return [part.astype(BF) for part in (high, middle, low)]


def shape_of(shape, dtype=BF):
    return jax.ShapeDtypeStruct(shape, dtype)


def local_call(kernel, outs, args, scratch=()):
    total = sum(int(np.prod(x.shape)) * x.dtype.itemsize for x in tuple(args) + tuple(outs))
    return pl.pallas_call(
        kernel,
        out_shape=tuple(outs),
        in_specs=[SMEM_SPEC] + [VMEM_SPEC] * (len(args) - 1),
        out_specs=(VMEM_SPEC,) * len(outs),
        scratch_shapes=list(scratch),
        compiler_params=pltpu.CompilerParams(vmem_limit_bytes=int(total * 1.25) + 4 * 1024 * 1024),
        cost_estimate=pl.CostEstimate(flops=1000, bytes_accessed=1000, transcendentals=0),
    )(*args)


def row_chunks(count):
    pieces = -(-count // 512)
    if count % (16 * pieces):
        pieces = 1
    return pieces, count // pieces


def token_pack_kernel(tokens, part_rows, capacity, padded, info, block, compact, place, own_parts, table, parts):
    width = compact.shape[1]
    per_row = width // tokens
    table[...] = block[tokens:, :].astype(F32)

    def parts_of(expert):
        row, lane = expert // per_row, pl.multiple_of((expert % per_row) * tokens, tokens)
        parts[...] = jnp.zeros_like(parts)
        for p in range(3):
            found = lax.broadcasted_iota(I32, (table.shape[0], tokens), 0) == p * part_rows + row
            parts[p:p + 1, :] = jnp.sum(
                jnp.where(found, table[:, pl.ds(lane, tokens)], 0.0), axis=0, keepdims=True)
        return parts[...]

    own_parts[...] = parts_of(info[0]).astype(BF)
    theirs = parts_of(info[1])
    named = jnp.sum(theirs, axis=0, keepdims=True) > 0.0
    row_at = lax.broadcasted_iota(I32, (tokens, tokens), 0)
    column_at = lax.broadcasted_iota(I32, (tokens, tokens), 1)
    until = (row_at <= column_at).astype(F32).astype(BF)
    ones = jnp.broadcast_to(named.astype(F32), (TAIL, tokens)).astype(BF)
    rank = jnp.dot(ones, until, preferred_element_type=F32)[:1, :].astype(I32) - 1
    picked = ((row_at == rank) & named & (row_at < capacity)).astype(F32).astype(BF)
    place[...] = picked[:padded, :]
    compact[:padded, :] = dot(picked[:padded, :], block[:tokens, :], ROWS).astype(BF)
    compact[padded:, :] = jnp.zeros((TAIL, width), BF)
    compact[padded:, :tokens] = dot(theirs.astype(BF), picked, LAST).astype(BF)


def grad_pack_kernel(info, block, place, compact):
    compact[...] = dot(place[...], block[...], ROWS).astype(BF)


def lay_out(lines, tokens, padded, blocks, compact, rows):
    for k in range(lines):
        rows[k * tokens:(k + 1) * tokens, :] = blocks[k][:tokens, :]
        at = lines * tokens + k * padded
        rows[at:at + padded, :] = compact[k][:padded, :]


def token_rows_kernel(lines, tokens, padded, info, *refs):
    n = lines
    blocks, compact, own_parts = refs[:n], refs[n:2 * n], refs[2 * n:3 * n]
    rows, weights = refs[3 * n:]
    lay_out(n, tokens, padded, blocks, compact, rows)
    eye = (lax.broadcasted_iota(I32, (tokens, tokens), 0)
           == lax.broadcasted_iota(I32, (tokens, tokens), 1))
    for k in range(n):
        for first, size, tail in (
            (k * tokens, tokens, own_parts[k][...]),
            (n * tokens + k * padded, padded, compact[k][padded:, :tokens]),
        ):
            row = jnp.sum(tail.astype(F32), axis=0, keepdims=True)
            column = jnp.sum(jnp.where(eye, row, 0.0), axis=1, keepdims=True)
            weights[first:first + size, :] = column[:size]


def grad_rows_kernel(lines, tokens, padded, info, *refs):
    lay_out(lines, tokens, padded, refs[:lines], refs[lines:2 * lines], refs[2 * lines])


def halves(info, width):
    core = info[2]
    return pl.ds(pl.multiple_of(core * width, width), width), pl.ds(pl.multiple_of((1 - core) * width, width), width)


def forward_kernel(pieces, chunk, info, own, other, weights, gate_w, up_w, down_w, gate, upward, scaled, sent):
    mine, theirs = halves(info, own.shape[1])

    @pl.loop(0, pieces)
    def _(i):
        at = pl.ds(pl.multiple_of(i * chunk, 16), chunk)
        a, b = own[at, :], other[at, :]
        g = dot(a, gate_w[mine, :], ROWS) + dot(b, gate_w[theirs, :], ROWS)
        u = dot(a, up_w[mine, :], ROWS) + dot(b, up_w[theirs, :], ROWS)
        gate[at, :] = g
        upward[at, :] = u
        h = (weights[at, :] * (g * jax.nn.sigmoid(g) * u)).astype(BF)
        scaled[at, :] = h
        sent[at, :] = dot(h, down_w[:, theirs], ROWS).astype(BF)


def backward_kernel(pieces, chunk, lines, tokens, padded, info, own, other, weights, gate, upward, gate_w, up_w,
                    down_w, grad_gate, grad_up, sent, dense_tails, compact_tails, values):
    mine, theirs = halves(info, own.shape[1])

    @pl.loop(0, pieces)
    def _(i):
        at = pl.ds(pl.multiple_of(i * chunk, 16), chunk)
        plain = dot(own[at, :], down_w[:, mine], LAST) + dot(other[at, :], down_w[:, theirs], LAST)
        g, u = gate[at, :], upward[at, :]
        sig = jax.nn.sigmoid(g)
        through = g * sig
        values[at, :] = jnp.sum(through * u * plain, axis=1, keepdims=True)
        scaled = weights[at, :] * plain
        gg = (scaled * u * sig * (1.0 + g * (1.0 - sig))).astype(BF)
        gu = (scaled * through).astype(BF)
        grad_gate[at, :] = gg
        grad_up[at, :] = gu
        sent[at, :] = (dot(gg, gate_w[theirs, :], LAST) + dot(gu, up_w[theirs, :], LAST)).astype(BF)

    eye = (lax.broadcasted_iota(I32, (tokens, tokens), 0)
           == lax.broadcasted_iota(I32, (tokens, tokens), 1))
    for k in range(lines):
        for first, size, tails in (
            (k * tokens, tokens, dense_tails),
            (lines * tokens + k * padded, padded, compact_tails),
        ):
            column = values[first:first + size, :]
            row = jnp.sum(jnp.where(eye[:size, :], column, 0.0), axis=0, keepdims=True)
            high = row.astype(BF).astype(F32)
            middle = (row - high).astype(BF).astype(F32)
            low = row - high - middle
            at = lax.broadcasted_iota(I32, (TAIL, tokens), 0)
            tails[k] = jnp.where(at == 0, high, jnp.where(at == 1, middle, jnp.where(at == 2, low, 0.0)))


def join_kernel(lines, tokens, padded, forward, info, came, *refs):
    width = came.shape[1]
    mine, _ = halves(info, width)
    if forward:
        scaled, down_w = refs[:2]
        dense, messages = refs[2], refs[3:]

        def product(first, size):
            return dot(scaled[first:first + size, :], down_w[:, mine], ROWS)
    else:
        grad_gate, grad_up, gate_w, up_w, tails = refs[:5]
        dense, messages = refs[5], refs[6:]

        def product(first, size):
            at = slice(first, first + size)
            return dot(grad_gate[at, :], gate_w[mine, :], LAST) + dot(grad_up[at, :], up_w[mine, :], LAST)

    def joined(first, size):
        return product(first, size) + came[first:first + size, :].astype(F32)

    start = lines * tokens
    for first in range(0, lines, 4):
        count = min(4, lines - first)
        total = joined(start + first * padded, count * padded).astype(BF)
        for k in range(first, first + count):
            messages[k][:padded, :] = total[(k - first) * padded:(k - first + 1) * padded]
            if not forward:
                messages[k][padded:, :] = jnp.zeros((TAIL, width), BF)
                messages[k][padded:, :tokens] = tails[k].astype(BF)
    for first in range(0, lines, 4):
        count = min(4, lines - first)
        total = joined(first * tokens, count * tokens)
        for k in range(first, first + count):
            dense[k] = total[(k - first) * tokens:(k - first + 1) * tokens]


def home_kernel(k, tokens, padded, tailed, info, dense, back, place, *refs):
    message = refs[-1]
    block = dense[k] + dot(place[...], back[:padded, :], FIRST)
    message[:tokens, :] = block.astype(BF)
    if not tailed:
        return
    tails = refs[0]
    message[tokens:, :] = jnp.zeros((TAIL, message.shape[1]), BF)
    theirs = dot(back[padded:, :padded], place[...], ROWS)
    message[tokens:, :tokens] = jnp.concatenate([tails[k][:8], theirs[:8]], axis=0).astype(BF)


def per_device(tokens, expert_ids, router_weights, gate_weight, up_weight, down_weight, grad_out):
    token_count, half_width = tokens.shape
    hidden_half = gate_weight.shape[2]
    top_count = expert_ids.shape[1]
    experts = lax.axis_size("expert")
    capacity = min(token_count, 3 * token_count * top_count // (2 * experts))
    padded = -(-capacity // 16) * 16
    lines = experts // 2
    mine = lax.axis_index("expert")
    core = lax.axis_index("tensor")
    at_line = mine // 2
    peer = mine + 1 - 2 * (mine % 2)
    settle = lax.optimization_barrier

    def over_pair(x):
        return lax.ppermute(x, "expert", [(i, i + 1 - 2 * (i % 2)) for i in range(experts)])

    def over_line(x, k):
        return lax.ppermute(
            x, "expert",
            [(i, ((i // 2 + k) % lines) * 2 + i % 2) for i in range(experts)],
        )

    def over_core(x):
        return lax.ppermute(x, "tensor", [(0, 1), (1, 0)])

    chosen = expert_ids[:, :, None] == jnp.arange(experts, dtype=I32)[None, None, :]
    table = jnp.sum(jnp.where(chosen, router_weights[:, :, None], 0.0), axis=1).T
    part_rows = experts * token_count // half_width
    parts = jnp.concatenate([p.reshape(part_rows, half_width) for p in split_three(table)])
    tail = -(-3 * part_rows // TAIL) * TAIL
    parts = jnp.pad(parts, ((0, tail - 3 * part_rows), (0, 0)))
    first = jnp.concatenate([tokens, parts])

    info = jnp.stack([mine, peer, core]).astype(I32)
    sizes = (lines, token_count, padded)
    row_count = lines * (token_count + padded)
    half_rows = shape_of((row_count, half_width))
    hidden_rows = (row_count, hidden_half)
    gate_local = gate_weight[0]
    up_local = up_weight[0]
    down_local = down_weight[0]
    pieces, chunk = row_chunks(row_count)
    every = range(lines)
    by_reach = sorted(range(1, lines), key=lambda k: min(k, lines - k))

    blocks = {0: first}
    for k in by_reach:
        blocks[k] = over_line(first, k)
    compact, places, own_parts, early = {}, {}, {}, []
    for k in [0] + by_reach:
        packed, places[k], own_parts[k] = local_call(
            functools.partial(token_pack_kernel, token_count, part_rows, capacity, padded),
            (shape_of((padded + TAIL, half_width)), shape_of((padded, token_count)),
             shape_of((TAIL, token_count))),
            (info, blocks[k]),
            (pltpu.VMEM((tail, half_width), F32), pltpu.VMEM((TAIL, token_count), F32)),
        )
        if k != by_reach[-1]:
            early.append(packed)
        compact[k] = over_pair(packed)

    (first_packed,) = local_call(
        grad_pack_kernel, (shape_of((padded, half_width)),), (info, grad_out, places[0]))
    grad_first = over_pair(first_packed)
    soon = {k: compact[k] for k in [0] + by_reach[:1]}
    held_grad, blocks, early, soon, grad_first = settle((grad_out, blocks, early, soon, grad_first))
    compact.update(soon)
    grad_blocks = {0: held_grad}
    for k in by_reach:
        grad_blocks[k] = over_line(held_grad, k)

    grad_packed = {
        k: local_call(
            grad_pack_kernel, (shape_of((padded, half_width)),), (info, grad_blocks[k], places[k]))[0]
        for k in by_reach
    }
    grad_compact = {k: over_pair(grad_packed[k]) for k in by_reach}
    grad_compact[0] = grad_first
    ahead = {k: grad_compact[k] for k in by_reach[:1]}
    compact, grad_blocks, grad_packed, ahead = settle((compact, grad_blocks, grad_packed, ahead))
    grad_compact.update(ahead)
    rows, weights = local_call(
        functools.partial(token_rows_kernel, *sizes),
        (half_rows, shape_of((row_count, 1), F32)),
        (info, *[blocks[k] for k in every], *[compact[k] for k in every], *[own_parts[k] for k in every]))
    rows_other = over_core(rows)
    ahead = {k: grad_compact[k] for k in by_reach[1:-1]}
    rows_other, ahead = settle((rows_other, ahead))
    grad_compact.update(ahead)
    gate, upward, scaled, sent = local_call(
        functools.partial(forward_kernel, pieces, chunk),
        (shape_of(hidden_rows, F32), shape_of(hidden_rows, F32), shape_of(hidden_rows), half_rows),
        (info, rows, rows_other, weights, gate_local, up_local, down_local))
    sent, grad_compact = settle((sent, grad_compact))
    out_dense, *out_packed = local_call(
        functools.partial(join_kernel, *sizes, True),
        (shape_of((lines, token_count, half_width), F32),
         *[shape_of((padded, half_width)) for _ in every]),
        (info, over_core(sent), scaled, down_local))

    outward = by_reach[::-1]
    out_back = {k: over_pair(out_packed[k]) for k in every}
    (grad_rows,) = local_call(
        functools.partial(grad_rows_kernel, *sizes), (half_rows,),
        (info, *[grad_blocks[k] for k in every], *[grad_compact[k] for k in every]))
    grad_rows, out_packed = settle((grad_rows, out_packed))
    grad_other = over_core(grad_rows)
    grad_gate, grad_up, sent, dense_tails, compact_tails = local_call(
        functools.partial(backward_kernel, pieces, chunk, *sizes),
        (shape_of(hidden_rows), shape_of(hidden_rows), half_rows,
         shape_of((lines, TAIL, token_count), F32), shape_of((lines, TAIL, token_count), F32)),
        (info, grad_rows, grad_other, weights, gate, upward, gate_local, up_local, down_local),
        (pltpu.VMEM((row_count, 1), F32),))

    def to_home(k, dense, back, *tails):
        extra = TAIL if tails else 0
        return local_call(
            functools.partial(home_kernel, k, token_count, padded, bool(tails)),
            (shape_of((token_count + extra, half_width)),), (info, dense, back[k], places[k], *tails))[0]

    def summed(blocks):
        total = blocks[0][:token_count].astype(F32)
        for k in range(1, lines):
            total = total + blocks[k][:token_count].astype(F32)
        return total.astype(BF)

    sent, some = settle((sent, {k: out_back[k] for k in by_reach}))
    out_back.update(some)
    out_home = {k: to_home(k, out_dense, out_back) for k in by_reach + [0]}
    out_came = {k: over_line(out_home[k], lines - k) for k in by_reach}
    out_came[0] = out_home[0]
    in_dense, *in_packed = local_call(
        functools.partial(join_kernel, *sizes, False),
        (shape_of((lines, token_count, half_width), F32),
         *[shape_of((padded + TAIL, half_width)) for _ in every]),
        (info, over_core(sent), grad_gate, grad_up, gate_local, up_local, compact_tails))
    in_packed, out_came[0] = settle((in_packed, out_came[0]))
    in_back, in_home, sequence = {}, {}, outward + [0]
    for i, k in enumerate(sequence):
        packed = in_packed[k]
        if i >= 2:
            packed, _ = settle((packed, in_home[sequence[i - 2]]))
        in_back[k] = over_pair(packed)
        in_home[k] = to_home(k, in_dense, in_back, dense_tails)
    in_home[sequence[0]], out_came = settle((in_home[sequence[0]], out_came))
    layer_out = summed(out_came)
    last_home, rows, rows_other, grad_rows, grad_other, scaled, grad_gate, grad_up = settle(
        ([in_home[k] for k in outward], rows, rows_other, grad_rows, grad_other, scaled, grad_gate, grad_up))
    in_home = {k: over_line(in_home[k], lines - k) if k else in_home[0] for k in every}
    input_grad = summed(in_home)

    def whole(own, other):
        return jnp.concatenate(
            [jnp.where(core == 0, own, other), jnp.where(core == 0, other, own)], axis=1)

    rows = whole(rows, rows_other)
    grads = whole(grad_rows, grad_other)
    down_grad = dot(scaled, grads, FIRST).astype(BF)
    gate_grad = dot(rows, grad_gate, FIRST).astype(BF)
    up_grad = dot(rows, grad_up, FIRST).astype(BF)

    held = []
    for k in every:
        values = in_home[k][token_count:, :token_count].astype(F32)
        held.append(jnp.stack([jnp.sum(values[:8], axis=0), jnp.sum(values[8:], axis=0)]))
    flat = jnp.stack(held).reshape(experts, token_count)
    place = (expert_ids // 2 - at_line) % lines
    slot = place * 2 + ((expert_ids % 2) != (mine % 2)).astype(I32)
    match = slot[:, :, None] == jnp.arange(experts, dtype=I32)[None, None, :]
    half_value = jnp.sum(jnp.where(match, flat.T[:, None, :], 0.0), axis=2)
    weight_grad = half_value + over_core(half_value)
    return (layer_out, input_grad, weight_grad, gate_grad[None], up_grad[None], down_grad[None])


def solution(mesh):
    in_specs = (
        P(("group", "expert"), "tensor"),
        P(("group", "expert"), None),
        P(("group", "expert"), None),
        P("expert", None, "tensor"),
        P("expert", None, "tensor"),
        P("expert", "tensor", None),
        P(("group", "expert"), "tensor"),
    )
    out_specs = (
        P(("group", "expert"), "tensor"),
        P(("group", "expert"), "tensor"),
        P(("group", "expert"), None),
        P(("group", "expert"), None, "tensor"),
        P(("group", "expert"), None, "tensor"),
        P(("group", "expert"), "tensor", None),
    )
    return jax.shard_map(
        per_device, mesh=mesh, in_specs=in_specs, out_specs=out_specs, check_vma=False
    )
```

```python
import functools

import jax
import jax.numpy as jnp
import numpy as np
from jax import lax
from jax.experimental import pallas as pl
from jax.experimental.pallas import tpu as pltpu
from jax.sharding import PartitionSpec as P

BF = jnp.bfloat16
F32 = jnp.float32
I32 = jnp.int32
TAIL = 16
ROWS = ((1,), (0,))
LAST = ((1,), (1,))
FIRST = ((0,), (0,))

SMEM_SPEC = pl.BlockSpec(memory_space=pltpu.SMEM)
VMEM_SPEC = pl.BlockSpec(memory_space=pltpu.VMEM)


def dot(a, b, contract):
    return lax.dot_general(a, b, (contract, ((), ())), preferred_element_type=F32)


def split_three(values):
    high = lax.reduce_precision(values, 8, 7)
    rest = values - high
    middle = lax.reduce_precision(rest, 8, 7)
    low = rest - middle
    return [part.astype(BF) for part in (high, middle, low)]


def shape_of(shape, dtype=BF):
    return jax.ShapeDtypeStruct(shape, dtype)


def local_call(kernel, outs, args, scratch=()):
    total = sum(int(np.prod(x.shape)) * x.dtype.itemsize for x in tuple(args) + tuple(outs))
    return pl.pallas_call(
        kernel,
        out_shape=tuple(outs),
        in_specs=[SMEM_SPEC] + [VMEM_SPEC] * (len(args) - 1),
        out_specs=(VMEM_SPEC,) * len(outs),
        scratch_shapes=list(scratch),
        compiler_params=pltpu.CompilerParams(vmem_limit_bytes=int(total * 1.25) + 4 * 1024 * 1024),
        cost_estimate=pl.CostEstimate(flops=1000, bytes_accessed=1000, transcendentals=0),
    )(*args)


def row_chunks(count):
    pieces = -(-count // 512)
    if count % (16 * pieces):
        pieces = 1
    return pieces, count // pieces


def token_pack_kernel(tokens, part_rows, capacity, padded, info, block, compact, place, own_parts, table, parts):
    width = compact.shape[1]
    per_row = width // tokens
    table[...] = block[tokens:, :].astype(F32)

    def parts_of(expert):
        row, lane = expert // per_row, pl.multiple_of((expert % per_row) * tokens, tokens)
        parts[...] = jnp.zeros_like(parts)
        for p in range(3):
            found = lax.broadcasted_iota(I32, (table.shape[0], tokens), 0) == p * part_rows + row
            parts[p:p + 1, :] = jnp.sum(
                jnp.where(found, table[:, pl.ds(lane, tokens)], 0.0), axis=0, keepdims=True)
        return parts[...]

    own_parts[...] = parts_of(info[0]).astype(BF)
    theirs = parts_of(info[1])
    named = jnp.sum(theirs, axis=0, keepdims=True) > 0.0
    row_at = lax.broadcasted_iota(I32, (tokens, tokens), 0)
    column_at = lax.broadcasted_iota(I32, (tokens, tokens), 1)
    until = (row_at <= column_at).astype(F32).astype(BF)
    ones = jnp.broadcast_to(named.astype(F32), (TAIL, tokens)).astype(BF)
    rank = jnp.dot(ones, until, preferred_element_type=F32)[:1, :].astype(I32) - 1
    picked = ((row_at == rank) & named & (row_at < capacity)).astype(F32).astype(BF)
    place[...] = picked[:padded, :]
    compact[:padded, :] = dot(picked[:padded, :], block[:tokens, :], ROWS).astype(BF)
    compact[padded:, :] = jnp.zeros((TAIL, width), BF)
    compact[padded:, :tokens] = dot(theirs.astype(BF), picked, LAST).astype(BF)


def grad_pack_kernel(info, block, place, compact):
    compact[...] = dot(place[...], block[...], ROWS).astype(BF)


def lay_out(lines, tokens, padded, blocks, compact, rows):
    for k in range(lines):
        rows[k * tokens:(k + 1) * tokens, :] = blocks[k][:tokens, :]
        at = lines * tokens + k * padded
        rows[at:at + padded, :] = compact[k][:padded, :]


def token_rows_kernel(lines, tokens, padded, info, *refs):
    n = lines
    blocks, compact, own_parts = refs[:n], refs[n:2 * n], refs[2 * n:3 * n]
    rows, weights = refs[3 * n:]
    lay_out(n, tokens, padded, blocks, compact, rows)
    eye = (lax.broadcasted_iota(I32, (tokens, tokens), 0)
           == lax.broadcasted_iota(I32, (tokens, tokens), 1))
    for k in range(n):
        for first, size, tail in (
            (k * tokens, tokens, own_parts[k][...]),
            (n * tokens + k * padded, padded, compact[k][padded:, :tokens]),
        ):
            row = jnp.sum(tail.astype(F32), axis=0, keepdims=True)
            column = jnp.sum(jnp.where(eye, row, 0.0), axis=1, keepdims=True)
            weights[first:first + size, :] = column[:size]


def grad_rows_kernel(lines, tokens, padded, info, *refs):
    lay_out(lines, tokens, padded, refs[:lines], refs[lines:2 * lines], refs[2 * lines])


def halves(info, width):
    core = info[2]
    return pl.ds(pl.multiple_of(core * width, width), width), pl.ds(pl.multiple_of((1 - core) * width, width), width)


def forward_kernel(pieces, chunk, info, own, other, weights, gate_w, up_w, down_w, gate, upward, scaled, sent):
    mine, theirs = halves(info, own.shape[1])

    @pl.loop(0, pieces)
    def _(i):
        at = pl.ds(pl.multiple_of(i * chunk, 16), chunk)
        a, b = own[at, :], other[at, :]
        g = dot(a, gate_w[mine, :], ROWS) + dot(b, gate_w[theirs, :], ROWS)
        u = dot(a, up_w[mine, :], ROWS) + dot(b, up_w[theirs, :], ROWS)
        gate[at, :] = g
        upward[at, :] = u
        h = (weights[at, :] * (g * jax.nn.sigmoid(g) * u)).astype(BF)
        scaled[at, :] = h
        sent[at, :] = dot(h, down_w[:, theirs], ROWS).astype(BF)


def backward_kernel(pieces, chunk, lines, tokens, padded, info, own, other, weights, gate, upward, gate_w, up_w,
                    down_w, grad_gate, grad_up, sent, dense_tails, compact_tails, values):
    mine, theirs = halves(info, own.shape[1])

    @pl.loop(0, pieces)
    def _(i):
        at = pl.ds(pl.multiple_of(i * chunk, 16), chunk)
        plain = dot(own[at, :], down_w[:, mine], LAST) + dot(other[at, :], down_w[:, theirs], LAST)
        g, u = gate[at, :], upward[at, :]
        sig = jax.nn.sigmoid(g)
        through = g * sig
        values[at, :] = jnp.sum(through * u * plain, axis=1, keepdims=True)
        scaled = weights[at, :] * plain
        gg = (scaled * u * sig * (1.0 + g * (1.0 - sig))).astype(BF)
        gu = (scaled * through).astype(BF)
        grad_gate[at, :] = gg
        grad_up[at, :] = gu
        sent[at, :] = (dot(gg, gate_w[theirs, :], LAST) + dot(gu, up_w[theirs, :], LAST)).astype(BF)

    eye = (lax.broadcasted_iota(I32, (tokens, tokens), 0)
           == lax.broadcasted_iota(I32, (tokens, tokens), 1))
    for k in range(lines):
        for first, size, tails in (
            (k * tokens, tokens, dense_tails),
            (lines * tokens + k * padded, padded, compact_tails),
        ):
            column = values[first:first + size, :]
            row = jnp.sum(jnp.where(eye[:size, :], column, 0.0), axis=0, keepdims=True)
            high = row.astype(BF).astype(F32)
            middle = (row - high).astype(BF).astype(F32)
            low = row - high - middle
            at = lax.broadcasted_iota(I32, (TAIL, tokens), 0)
            tails[k] = jnp.where(at == 0, high, jnp.where(at == 1, middle, jnp.where(at == 2, low, 0.0)))


def join_kernel(lines, tokens, padded, forward, info, came, *refs):
    width = came.shape[1]
    mine, _ = halves(info, width)
    if forward:
        scaled, down_w = refs[:2]
        dense, messages = refs[2], refs[3:]

        def product(first, size):
            return dot(scaled[first:first + size, :], down_w[:, mine], ROWS)
    else:
        grad_gate, grad_up, gate_w, up_w, tails = refs[:5]
        dense, messages = refs[5], refs[6:]

        def product(first, size):
            at = slice(first, first + size)
            return dot(grad_gate[at, :], gate_w[mine, :], LAST) + dot(grad_up[at, :], up_w[mine, :], LAST)

    def joined(first, size):
        return product(first, size) + came[first:first + size, :].astype(F32)

    start = lines * tokens
    for first in range(0, lines, 4):
        count = min(4, lines - first)
        total = joined(start + first * padded, count * padded).astype(BF)
        for k in range(first, first + count):
            messages[k][:padded, :] = total[(k - first) * padded:(k - first + 1) * padded]
            if not forward:
                messages[k][padded:, :] = jnp.zeros((TAIL, width), BF)
                messages[k][padded:, :tokens] = tails[k].astype(BF)
    for first in range(0, lines, 4):
        count = min(4, lines - first)
        total = joined(first * tokens, count * tokens)
        for k in range(first, first + count):
            dense[k] = total[(k - first) * tokens:(k - first + 1) * tokens]


def home_kernel(k, tokens, padded, tailed, info, dense, back, place, *refs):
    message = refs[-1]
    block = dense[k] + dot(place[...], back[:padded, :], FIRST)
    message[:tokens, :] = block.astype(BF)
    if not tailed:
        return
    tails = refs[0]
    message[tokens:, :] = jnp.zeros((TAIL, message.shape[1]), BF)
    theirs = dot(back[padded:, :padded], place[...], ROWS)
    message[tokens:, :tokens] = jnp.concatenate([tails[k][:8], theirs[:8]], axis=0).astype(BF)


def per_device(tokens, expert_ids, router_weights, gate_weight, up_weight, down_weight, grad_out):
    token_count, half_width = tokens.shape
    hidden_half = gate_weight.shape[2]
    top_count = expert_ids.shape[1]
    experts = lax.axis_size("expert")
    capacity = min(token_count, 3 * token_count * top_count // (2 * experts))
    padded = -(-capacity // 16) * 16
    lines = experts // 2
    mine = lax.axis_index("expert")
    core = lax.axis_index("tensor")
    at_line = mine // 2
    peer = mine + 1 - 2 * (mine % 2)
    settle = lax.optimization_barrier

    def over_pair(x):
        return lax.ppermute(x, "expert", [(i, i + 1 - 2 * (i % 2)) for i in range(experts)])

    def over_line(x, k):
        return lax.ppermute(
            x, "expert",
            [(i, ((i // 2 + k) % lines) * 2 + i % 2) for i in range(experts)],
        )

    def over_core(x):
        return lax.ppermute(x, "tensor", [(0, 1), (1, 0)])

    chosen = expert_ids[:, :, None] == jnp.arange(experts, dtype=I32)[None, None, :]
    table = jnp.sum(jnp.where(chosen, router_weights[:, :, None], 0.0), axis=1).T
    part_rows = experts * token_count // half_width
    parts = jnp.concatenate([p.reshape(part_rows, half_width) for p in split_three(table)])
    tail = -(-3 * part_rows // TAIL) * TAIL
    parts = jnp.pad(parts, ((0, tail - 3 * part_rows), (0, 0)))
    first = jnp.concatenate([tokens, parts])

    info = jnp.stack([mine, peer, core]).astype(I32)
    sizes = (lines, token_count, padded)
    row_count = lines * (token_count + padded)
    half_rows = shape_of((row_count, half_width))
    hidden_rows = (row_count, hidden_half)
    gate_local = gate_weight[0]
    up_local = up_weight[0]
    down_local = down_weight[0]
    pieces, chunk = row_chunks(row_count)
    every = range(lines)
    by_reach = sorted(range(1, lines), key=lambda k: min(k, lines - k))

    blocks = {0: first}
    for k in by_reach:
        blocks[k] = over_line(first, k)
    compact, places, own_parts, early = {}, {}, {}, []
    for k in [0] + by_reach:
        packed, places[k], own_parts[k] = local_call(
            functools.partial(token_pack_kernel, token_count, part_rows, capacity, padded),
            (shape_of((padded + TAIL, half_width)), shape_of((padded, token_count)),
             shape_of((TAIL, token_count))),
            (info, blocks[k]),
            (pltpu.VMEM((tail, half_width), F32), pltpu.VMEM((TAIL, token_count), F32)),
        )
        if k != by_reach[-1]:
            early.append(packed)
        compact[k] = over_pair(packed)

    (first_packed,) = local_call(
        grad_pack_kernel, (shape_of((padded, half_width)),), (info, grad_out, places[0]))
    grad_first = over_pair(first_packed)
    soon = {k: compact[k] for k in [0] + by_reach[:-1]}
    held_grad, blocks, early, soon, grad_first = settle((grad_out, blocks, early, soon, grad_first))
    compact.update(soon)
    grad_blocks = {0: held_grad}
    for k in by_reach:
        grad_blocks[k] = over_line(held_grad, k)

    def grad_pack(k):
        return local_call(
            grad_pack_kernel, (shape_of((padded, half_width)),), (info, grad_blocks[k], places[k]))[0]

    near, far = by_reach[:-1], by_reach[-1]
    grad_packed = {k: grad_pack(k) for k in near}
    grad_compact = {k: over_pair(grad_packed[k]) for k in near}
    grad_compact[0] = grad_first
    compact, near_blocks, near_packed = settle(
        (compact, {k: grad_blocks[k] for k in near}, {k: grad_packed[k] for k in near}))
    grad_blocks.update(near_blocks)
    rows, weights = local_call(
        functools.partial(token_rows_kernel, *sizes),
        (half_rows, shape_of((row_count, 1), F32)),
        (info, *[blocks[k] for k in every], *[compact[k] for k in every], *[own_parts[k] for k in every]))
    rows_other = over_core(rows)
    gate, upward, scaled, sent = local_call(
        functools.partial(forward_kernel, pieces, chunk),
        (shape_of(hidden_rows, F32), shape_of(hidden_rows, F32), shape_of(hidden_rows), half_rows),
        (info, rows, rows_other, weights, gate_local, up_local, down_local))
    sent, grad_compact, grad_blocks = settle((sent, grad_compact, grad_blocks))
    grad_compact[far] = over_pair(grad_pack(far))
    out_dense, *out_packed = local_call(
        functools.partial(join_kernel, *sizes, True),
        (shape_of((lines, token_count, half_width), F32),
         *[shape_of((padded, half_width)) for _ in every]),
        (info, over_core(sent), scaled, down_local))

    outward = by_reach[::-1]
    out_back = {k: over_pair(out_packed[k]) for k in near}
    (grad_rows,) = local_call(
        functools.partial(grad_rows_kernel, *sizes), (half_rows,),
        (info, *[grad_blocks[k] for k in every], *[grad_compact[k] for k in every]))
    grad_rows, out_packed = settle((grad_rows, out_packed))
    grad_other = over_core(grad_rows)
    grad_gate, grad_up, sent, dense_tails, compact_tails = local_call(
        functools.partial(backward_kernel, pieces, chunk, *sizes),
        (shape_of(hidden_rows), shape_of(hidden_rows), half_rows,
         shape_of((lines, TAIL, token_count), F32), shape_of((lines, TAIL, token_count), F32)),
        (info, grad_rows, grad_other, weights, gate, upward, gate_local, up_local, down_local),
        (pltpu.VMEM((row_count, 1), F32),))

    def to_home(k, dense, back, *tails):
        extra = TAIL if tails else 0
        return local_call(
            functools.partial(home_kernel, k, token_count, padded, bool(tails)),
            (shape_of((token_count + extra, half_width)),), (info, dense, back[k], places[k], *tails))[0]

    def summed(blocks):
        total = blocks[0][:token_count].astype(F32)
        for k in range(1, lines):
            total = total + blocks[k][:token_count].astype(F32)
        return total.astype(BF)

    sent, out_back = settle((sent, out_back))
    out_home = {k: to_home(k, out_dense, out_back) for k in near}
    last, first_home = settle((out_packed[far], out_home[near[0]]))
    out_back[far] = over_pair(last)
    out_home[near[0]] = first_home
    last, out_back[far] = settle((out_packed[0], out_back[far]))
    out_back[0] = over_pair(last)
    for k in (far, 0):
        out_home[k] = to_home(k, out_dense, out_back)

    def whole(own, other):
        return jnp.concatenate(
            [jnp.where(core == 0, own, other), jnp.where(core == 0, other, own)], axis=1)

    came = over_core(sent)
    out_came = {k: over_line(out_home[k], lines - k) for k in by_reach}
    out_came[0] = out_home[0]
    in_dense, *in_packed = local_call(
        functools.partial(join_kernel, *sizes, False),
        (shape_of((lines, token_count, half_width), F32),
         *[shape_of((padded + TAIL, half_width)) for _ in every]),
        (info, came, grad_gate, grad_up, gate_local, up_local, compact_tails))
    in_packed, ahead = settle((in_packed, {k: out_came[k] for k in near}))
    out_came.update(ahead)
    in_back, in_home, sequence = {}, {}, outward + [0]
    for i, k in enumerate(sequence):
        packed = in_packed[k]
        if i >= 2:
            packed, _ = settle((packed, in_home[sequence[i - 2]]))
        in_back[k] = over_pair(packed)
        in_home[k] = to_home(k, in_dense, in_back, dense_tails)
    ready, out_came = settle(({k: in_home[k] for k in sequence[:2]}, out_came))
    in_home.update(ready)
    layer_out = summed(out_came)
    rows, rows_other, grad_rows, _ = settle((rows, rows_other, grad_rows, in_packed))
    rows = whole(rows, rows_other)
    gate_grad = dot(rows, grad_gate, FIRST).astype(BF)
    down_grad = dot(scaled, whole(grad_rows, grad_other), FIRST).astype(BF)
    in_home[sequence[0]], gate_grad = settle((in_home[sequence[0]], gate_grad))
    in_home[sequence[1]], down_grad = settle((in_home[sequence[1]], down_grad))
    last_home, rows, grad_up = settle(([in_home[k] for k in outward], rows, grad_up))
    in_home = {k: over_line(in_home[k], lines - k) if k else in_home[0] for k in every}
    input_grad = summed(in_home)

    up_grad = dot(rows, grad_up, FIRST).astype(BF)

    held = []
    for k in every:
        values = in_home[k][token_count:, :token_count].astype(F32)
        held.append(jnp.stack([jnp.sum(values[:8], axis=0), jnp.sum(values[8:], axis=0)]))
    flat = jnp.stack(held).reshape(experts, token_count)
    place = (expert_ids // 2 - at_line) % lines
    slot = place * 2 + ((expert_ids % 2) != (mine % 2)).astype(I32)
    match = slot[:, :, None] == jnp.arange(experts, dtype=I32)[None, None, :]
    half_value = jnp.sum(jnp.where(match, flat.T[:, None, :], 0.0), axis=2)
    weight_grad = half_value + over_core(half_value)
    return (layer_out, input_grad, weight_grad, gate_grad[None], up_grad[None], down_grad[None])


def solution(mesh):
    in_specs = (
        P(("group", "expert"), "tensor"),
        P(("group", "expert"), None),
        P(("group", "expert"), None),
        P("expert", None, "tensor"),
        P("expert", None, "tensor"),
        P("expert", "tensor", None),
        P(("group", "expert"), "tensor"),
    )
    out_specs = (
        P(("group", "expert"), "tensor"),
        P(("group", "expert"), "tensor"),
        P(("group", "expert"), None),
        P(("group", "expert"), None, "tensor"),
        P(("group", "expert"), None, "tensor"),
        P(("group", "expert"), "tensor", None),
    )
    return jax.shard_map(
        per_device, mesh=mesh, in_specs=in_specs, out_specs=out_specs, check_vma=False
    )
```

```python
import functools

import jax
import jax.numpy as jnp
import numpy as np
from jax import lax
from jax.experimental import pallas as pl
from jax.experimental.pallas import tpu as pltpu
from jax.sharding import PartitionSpec as P

BF = jnp.bfloat16
F32 = jnp.float32
I32 = jnp.int32
TAIL = 16
ROWS = ((1,), (0,))
LAST = ((1,), (1,))
FIRST = ((0,), (0,))

SMEM_SPEC = pl.BlockSpec(memory_space=pltpu.SMEM)
VMEM_SPEC = pl.BlockSpec(memory_space=pltpu.VMEM)


def dot(a, b, contract):
    return lax.dot_general(a, b, (contract, ((), ())), preferred_element_type=F32)


def split_three(values):
    high = lax.reduce_precision(values, 8, 7)
    rest = values - high
    middle = lax.reduce_precision(rest, 8, 7)
    low = rest - middle
    return [part.astype(BF) for part in (high, middle, low)]


def shape_of(shape, dtype=BF):
    return jax.ShapeDtypeStruct(shape, dtype)


def local_call(kernel, outs, args, scratch=()):
    total = sum(int(np.prod(x.shape)) * x.dtype.itemsize for x in tuple(args) + tuple(outs))
    return pl.pallas_call(
        kernel,
        out_shape=tuple(outs),
        in_specs=[SMEM_SPEC] + [VMEM_SPEC] * (len(args) - 1),
        out_specs=(VMEM_SPEC,) * len(outs),
        scratch_shapes=list(scratch),
        compiler_params=pltpu.CompilerParams(vmem_limit_bytes=int(total * 1.25) + 4 * 1024 * 1024),
        cost_estimate=pl.CostEstimate(flops=1000, bytes_accessed=1000, transcendentals=0),
    )(*args)


def row_chunks(count):
    pieces = -(-count // 512)
    if count % (16 * pieces):
        pieces = 1
    return pieces, count // pieces


def token_pack_kernel(tokens, part_rows, capacity, padded, info, block, compact, place, own_parts, table, parts):
    width = compact.shape[1]
    per_row = width // tokens
    table[...] = block[tokens:, :].astype(F32)

    def parts_of(expert):
        row, lane = expert // per_row, pl.multiple_of((expert % per_row) * tokens, tokens)
        parts[...] = jnp.zeros_like(parts)
        for p in range(3):
            found = lax.broadcasted_iota(I32, (table.shape[0], tokens), 0) == p * part_rows + row
            parts[p:p + 1, :] = jnp.sum(
                jnp.where(found, table[:, pl.ds(lane, tokens)], 0.0), axis=0, keepdims=True)
        return parts[...]

    own_parts[...] = parts_of(info[0]).astype(BF)
    theirs = parts_of(info[1])
    named = jnp.sum(theirs, axis=0, keepdims=True) > 0.0
    row_at = lax.broadcasted_iota(I32, (tokens, tokens), 0)
    column_at = lax.broadcasted_iota(I32, (tokens, tokens), 1)
    until = (row_at <= column_at).astype(F32).astype(BF)
    ones = jnp.broadcast_to(named.astype(F32), (TAIL, tokens)).astype(BF)
    rank = jnp.dot(ones, until, preferred_element_type=F32)[:1, :].astype(I32) - 1
    picked = ((row_at == rank) & named & (row_at < capacity)).astype(F32).astype(BF)
    place[...] = picked[:padded, :]
    compact[:padded, :] = dot(picked[:padded, :], block[:tokens, :], ROWS).astype(BF)
    compact[padded:, :] = jnp.zeros((TAIL, width), BF)
    compact[padded:, :tokens] = dot(theirs.astype(BF), picked, LAST).astype(BF)


def grad_pack_kernel(info, block, place, compact):
    compact[...] = dot(place[...], block[...], ROWS).astype(BF)


def lay_out(lines, tokens, padded, blocks, compact, rows):
    for k in range(lines):
        rows[k * tokens:(k + 1) * tokens, :] = blocks[k][:tokens, :]
        at = lines * tokens + k * padded
        rows[at:at + padded, :] = compact[k][:padded, :]


def token_rows_kernel(lines, tokens, padded, info, *refs):
    n = lines
    blocks, compact, own_parts = refs[:n], refs[n:2 * n], refs[2 * n:3 * n]
    rows, weights = refs[3 * n:]
    lay_out(n, tokens, padded, blocks, compact, rows)
    eye = (lax.broadcasted_iota(I32, (tokens, tokens), 0)
           == lax.broadcasted_iota(I32, (tokens, tokens), 1))
    for k in range(n):
        for first, size, tail in (
            (k * tokens, tokens, own_parts[k][...]),
            (n * tokens + k * padded, padded, compact[k][padded:, :tokens]),
        ):
            row = jnp.sum(tail.astype(F32), axis=0, keepdims=True)
            column = jnp.sum(jnp.where(eye, row, 0.0), axis=1, keepdims=True)
            weights[first:first + size, :] = column[:size]


def grad_rows_kernel(lines, tokens, padded, info, *refs):
    lay_out(lines, tokens, padded, refs[:lines], refs[lines:2 * lines], refs[2 * lines])


def halves(info, width):
    core = info[2]
    return pl.ds(pl.multiple_of(core * width, width), width), pl.ds(pl.multiple_of((1 - core) * width, width), width)


def forward_kernel(pieces, chunk, info, own, other, weights, gate_w, up_w, down_w, gate, upward, scaled, sent):
    mine, theirs = halves(info, own.shape[1])

    @pl.loop(0, pieces)
    def _(i):
        at = pl.ds(pl.multiple_of(i * chunk, 16), chunk)
        a, b = own[at, :], other[at, :]
        g = dot(a, gate_w[mine, :], ROWS) + dot(b, gate_w[theirs, :], ROWS)
        u = dot(a, up_w[mine, :], ROWS) + dot(b, up_w[theirs, :], ROWS)
        gate[at, :] = g
        upward[at, :] = u
        h = (weights[at, :] * (g * jax.nn.sigmoid(g) * u)).astype(BF)
        scaled[at, :] = h
        sent[at, :] = dot(h, down_w[:, theirs], ROWS).astype(BF)


def backward_kernel(pieces, chunk, lines, tokens, padded, info, own, other, weights, gate, upward, gate_w, up_w,
                    down_w, grad_gate, grad_up, sent, dense_tails, compact_tails, values):
    mine, theirs = halves(info, own.shape[1])

    @pl.loop(0, pieces)
    def _(i):
        at = pl.ds(pl.multiple_of(i * chunk, 16), chunk)
        plain = dot(own[at, :], down_w[:, mine], LAST) + dot(other[at, :], down_w[:, theirs], LAST)
        g, u = gate[at, :], upward[at, :]
        sig = jax.nn.sigmoid(g)
        through = g * sig
        values[at, :] = jnp.sum(through * u * plain, axis=1, keepdims=True)
        scaled = weights[at, :] * plain
        gg = (scaled * u * sig * (1.0 + g * (1.0 - sig))).astype(BF)
        gu = (scaled * through).astype(BF)
        grad_gate[at, :] = gg
        grad_up[at, :] = gu
        sent[at, :] = (dot(gg, gate_w[theirs, :], LAST) + dot(gu, up_w[theirs, :], LAST)).astype(BF)

    eye = (lax.broadcasted_iota(I32, (tokens, tokens), 0)
           == lax.broadcasted_iota(I32, (tokens, tokens), 1))
    for k in range(lines):
        for first, size, tails in (
            (k * tokens, tokens, dense_tails),
            (lines * tokens + k * padded, padded, compact_tails),
        ):
            column = values[first:first + size, :]
            row = jnp.sum(jnp.where(eye[:size, :], column, 0.0), axis=0, keepdims=True)
            high = row.astype(BF).astype(F32)
            middle = (row - high).astype(BF).astype(F32)
            low = row - high - middle
            at = lax.broadcasted_iota(I32, (TAIL, tokens), 0)
            tails[k] = jnp.where(at == 0, high, jnp.where(at == 1, middle, jnp.where(at == 2, low, 0.0)))


def join_kernel(lines, tokens, padded, forward, info, came, *refs):
    width = came.shape[1]
    mine, _ = halves(info, width)
    if forward:
        scaled, down_w = refs[:2]
        dense, messages = refs[2], refs[3:]

        def product(first, size):
            return dot(scaled[first:first + size, :], down_w[:, mine], ROWS)
    else:
        grad_gate, grad_up, gate_w, up_w, tails = refs[:5]
        dense, messages = refs[5], refs[6:]

        def product(first, size):
            at = slice(first, first + size)
            return dot(grad_gate[at, :], gate_w[mine, :], LAST) + dot(grad_up[at, :], up_w[mine, :], LAST)

    def joined(first, size):
        return product(first, size) + came[first:first + size, :].astype(F32)

    start = lines * tokens
    for first in range(0, lines, 4):
        count = min(4, lines - first)
        total = joined(start + first * padded, count * padded).astype(BF)
        for k in range(first, first + count):
            messages[k][:padded, :] = total[(k - first) * padded:(k - first + 1) * padded]
            if not forward:
                messages[k][padded:, :] = jnp.zeros((TAIL, width), BF)
                messages[k][padded:, :tokens] = tails[k].astype(BF)
    for first in range(0, lines, 4):
        count = min(4, lines - first)
        total = joined(first * tokens, count * tokens)
        for k in range(first, first + count):
            dense[k] = total[(k - first) * tokens:(k - first + 1) * tokens]


def home_kernel(k, tokens, padded, tailed, info, dense, back, place, *refs):
    message = refs[-1]
    block = dense[k] + dot(place[...], back[:padded, :], FIRST)
    message[:tokens, :] = block.astype(BF)
    if not tailed:
        return
    tails = refs[0]
    message[tokens:, :] = jnp.zeros((TAIL, message.shape[1]), BF)
    theirs = dot(back[padded:, :padded], place[...], ROWS)
    message[tokens:, :tokens] = jnp.concatenate([tails[k][:8], theirs[:8]], axis=0).astype(BF)


def per_device(tokens, expert_ids, router_weights, gate_weight, up_weight, down_weight, grad_out):
    token_count, half_width = tokens.shape
    hidden_half = gate_weight.shape[2]
    top_count = expert_ids.shape[1]
    experts = lax.axis_size("expert")
    capacity = min(token_count, 3 * token_count * top_count // (2 * experts))
    padded = -(-capacity // 16) * 16
    lines = experts // 2
    mine = lax.axis_index("expert")
    core = lax.axis_index("tensor")
    at_line = mine // 2
    peer = mine + 1 - 2 * (mine % 2)
    settle = lax.optimization_barrier

    def over_pair(x):
        return lax.ppermute(x, "expert", [(i, i + 1 - 2 * (i % 2)) for i in range(experts)])

    def over_line(x, k):
        return lax.ppermute(
            x, "expert",
            [(i, ((i // 2 + k) % lines) * 2 + i % 2) for i in range(experts)],
        )

    def over_core(x):
        return lax.ppermute(x, "tensor", [(0, 1), (1, 0)])

    chosen = expert_ids[:, :, None] == jnp.arange(experts, dtype=I32)[None, None, :]
    table = jnp.sum(jnp.where(chosen, router_weights[:, :, None], 0.0), axis=1).T
    part_rows = experts * token_count // half_width
    parts = jnp.concatenate([p.reshape(part_rows, half_width) for p in split_three(table)])
    tail = -(-3 * part_rows // TAIL) * TAIL
    parts = jnp.pad(parts, ((0, tail - 3 * part_rows), (0, 0)))
    first = jnp.concatenate([tokens, parts])

    info = jnp.stack([mine, peer, core]).astype(I32)
    sizes = (lines, token_count, padded)
    row_count = lines * (token_count + padded)
    half_rows = shape_of((row_count, half_width))
    hidden_rows = (row_count, hidden_half)
    gate_local = gate_weight[0]
    up_local = up_weight[0]
    down_local = down_weight[0]
    pieces, chunk = row_chunks(row_count)
    every = range(lines)
    by_reach = sorted(range(1, lines), key=lambda k: min(k, lines - k))

    blocks = {0: first}
    for k in by_reach:
        blocks[k] = over_line(first, k)
    compact, places, own_parts, early = {}, {}, {}, []
    for k in [0] + by_reach:
        packed, places[k], own_parts[k] = local_call(
            functools.partial(token_pack_kernel, token_count, part_rows, capacity, padded),
            (shape_of((padded + TAIL, half_width)), shape_of((padded, token_count)),
             shape_of((TAIL, token_count))),
            (info, blocks[k]),
            (pltpu.VMEM((tail, half_width), F32), pltpu.VMEM((TAIL, token_count), F32)),
        )
        if k != by_reach[-1]:
            early.append(packed)
        compact[k] = over_pair(packed)

    (first_packed,) = local_call(
        grad_pack_kernel, (shape_of((padded, half_width)),), (info, grad_out, places[0]))
    grad_first = over_pair(first_packed)
    soon = {k: compact[k] for k in [0] + by_reach[:-1]}
    held_grad, blocks, early, soon, grad_first = settle((grad_out, blocks, early, soon, grad_first))
    compact.update(soon)
    grad_blocks = {0: held_grad}
    for k in by_reach:
        grad_blocks[k] = over_line(held_grad, k)

    def grad_pack(k):
        return local_call(
            grad_pack_kernel, (shape_of((padded, half_width)),), (info, grad_blocks[k], places[k]))[0]

    near, far = by_reach[:-1], by_reach[-1]
    grad_packed = {k: grad_pack(k) for k in by_reach}
    grad_compact = {k: over_pair(grad_packed[k]) for k in by_reach}
    grad_compact[0] = grad_first
    ahead = {k: grad_compact[k] for k in near[:1]}
    compact, grad_blocks, grad_packed, ahead = settle((compact, grad_blocks, grad_packed, ahead))
    grad_compact.update(ahead)
    rows, weights = local_call(
        functools.partial(token_rows_kernel, *sizes),
        (half_rows, shape_of((row_count, 1), F32)),
        (info, *[blocks[k] for k in every], *[compact[k] for k in every], *[own_parts[k] for k in every]))
    rows_other = over_core(rows)
    gate, upward, scaled, sent = local_call(
        functools.partial(forward_kernel, pieces, chunk),
        (shape_of(hidden_rows, F32), shape_of(hidden_rows, F32), shape_of(hidden_rows), half_rows),
        (info, rows, rows_other, weights, gate_local, up_local, down_local))
    sent, grad_compact = settle((sent, grad_compact))
    out_dense, *out_packed = local_call(
        functools.partial(join_kernel, *sizes, True),
        (shape_of((lines, token_count, half_width), F32),
         *[shape_of((padded, half_width)) for _ in every]),
        (info, over_core(sent), scaled, down_local))

    outward = by_reach[::-1]
    out_back = {k: over_pair(out_packed[k]) for k in near}
    (grad_rows,) = local_call(
        functools.partial(grad_rows_kernel, *sizes), (half_rows,),
        (info, *[grad_blocks[k] for k in every], *[grad_compact[k] for k in every]))
    grad_rows, out_packed = settle((grad_rows, out_packed))
    grad_other = over_core(grad_rows)
    grad_gate, grad_up, sent, dense_tails, compact_tails = local_call(
        functools.partial(backward_kernel, pieces, chunk, *sizes),
        (shape_of(hidden_rows), shape_of(hidden_rows), half_rows,
         shape_of((lines, TAIL, token_count), F32), shape_of((lines, TAIL, token_count), F32)),
        (info, grad_rows, grad_other, weights, gate, upward, gate_local, up_local, down_local),
        (pltpu.VMEM((row_count, 1), F32),))

    def to_home(k, dense, back, *tails):
        extra = TAIL if tails else 0
        return local_call(
            functools.partial(home_kernel, k, token_count, padded, bool(tails)),
            (shape_of((token_count + extra, half_width)),), (info, dense, back[k], places[k], *tails))[0]

    def summed(blocks):
        total = blocks[0][:token_count].astype(F32)
        for k in range(1, lines):
            total = total + blocks[k][:token_count].astype(F32)
        return total.astype(BF)

    sent, out_back = settle((sent, out_back))
    out_home = {k: to_home(k, out_dense, out_back) for k in near}
    last, first_home = settle((out_packed[far], out_home[near[0]]))
    out_back[far] = over_pair(last)
    out_home[near[0]] = first_home

    def whole(own, other):
        return jnp.concatenate(
            [jnp.where(core == 0, own, other), jnp.where(core == 0, other, own)], axis=1)

    came = over_core(sent)
    out_came = {k: over_line(out_home[k], lines - k) for k in near}
    in_dense, *in_packed = local_call(
        functools.partial(join_kernel, *sizes, False),
        (shape_of((lines, token_count, half_width), F32),
         *[shape_of((padded + TAIL, half_width)) for _ in every]),
        (info, came, grad_gate, grad_up, gate_local, up_local, compact_tails))
    in_packed, out_back[far], out_came = settle((in_packed, out_back[far], out_came))
    far_home = to_home(far, out_dense, out_back)
    out_came[far] = over_line(far_home, lines - far)
    in_back, in_home, sequence = {}, {}, outward + [0]
    for i, k in enumerate(sequence):
        packed = in_packed[k]
        if i >= 2:
            packed, _ = settle((packed, in_home[sequence[i - 2]]))
        in_back[k] = over_pair(packed)
        in_home[k] = to_home(k, in_dense, in_back, dense_tails)
    last, _ = settle((out_packed[0], in_back[sequence[2]]))
    out_back[0] = over_pair(last)
    ready, out_came = settle(({k: in_home[k] for k in sequence[:2]}, out_came))
    out_came[0] = to_home(0, out_dense, out_back)
    in_home.update(ready)
    layer_out = summed(out_came)
    rows, rows_other, grad_rows, _ = settle((rows, rows_other, grad_rows, far_home))
    rows = whole(rows, rows_other)
    gate_grad = dot(rows, grad_gate, FIRST).astype(BF)
    down_grad = dot(scaled, whole(grad_rows, grad_other), FIRST).astype(BF)
    in_home[sequence[0]], gate_grad = settle((in_home[sequence[0]], gate_grad))
    in_home[sequence[1]], down_grad = settle((in_home[sequence[1]], down_grad))
    last_home, rows, grad_up = settle(([in_home[k] for k in outward], rows, grad_up))
    in_home = {k: over_line(in_home[k], lines - k) if k else in_home[0] for k in every}
    input_grad = summed(in_home)

    up_grad = dot(rows, grad_up, FIRST).astype(BF)

    held = []
    for k in every:
        values = in_home[k][token_count:, :token_count].astype(F32)
        held.append(jnp.stack([jnp.sum(values[:8], axis=0), jnp.sum(values[8:], axis=0)]))
    flat = jnp.stack(held).reshape(experts, token_count)
    place = (expert_ids // 2 - at_line) % lines
    slot = place * 2 + ((expert_ids % 2) != (mine % 2)).astype(I32)
    match = slot[:, :, None] == jnp.arange(experts, dtype=I32)[None, None, :]
    half_value = jnp.sum(jnp.where(match, flat.T[:, None, :], 0.0), axis=2)
    weight_grad = half_value + over_core(half_value)
    return (layer_out, input_grad, weight_grad, gate_grad[None], up_grad[None], down_grad[None])


def solution(mesh):
    in_specs = (
        P(("group", "expert"), "tensor"),
        P(("group", "expert"), None),
        P(("group", "expert"), None),
        P("expert", None, "tensor"),
        P("expert", None, "tensor"),
        P("expert", "tensor", None),
        P(("group", "expert"), "tensor"),
    )
    out_specs = (
        P(("group", "expert"), "tensor"),
        P(("group", "expert"), "tensor"),
        P(("group", "expert"), None),
        P(("group", "expert"), None, "tensor"),
        P(("group", "expert"), None, "tensor"),
        P(("group", "expert"), "tensor", None),
    )
    return jax.shard_map(
        per_device, mesh=mesh, in_specs=in_specs, out_specs=out_specs, check_vma=False
    )
```

```python
import functools

import jax
import jax.numpy as jnp
import numpy as np
from jax import lax
from jax.experimental import pallas as pl
from jax.experimental.pallas import tpu as pltpu
from jax.sharding import PartitionSpec as P

BF = jnp.bfloat16
F32 = jnp.float32
I32 = jnp.int32
TAIL = 16
ROWS = ((1,), (0,))
LAST = ((1,), (1,))
FIRST = ((0,), (0,))

SMEM_SPEC = pl.BlockSpec(memory_space=pltpu.SMEM)
VMEM_SPEC = pl.BlockSpec(memory_space=pltpu.VMEM)


def dot(a, b, contract):
    return lax.dot_general(a, b, (contract, ((), ())), preferred_element_type=F32)


def split_three(values):
    high = lax.reduce_precision(values, 8, 7)
    rest = values - high
    middle = lax.reduce_precision(rest, 8, 7)
    low = rest - middle
    return [part.astype(BF) for part in (high, middle, low)]


def shape_of(shape, dtype=BF):
    return jax.ShapeDtypeStruct(shape, dtype)


def local_call(kernel, outs, args, scratch=()):
    total = sum(int(np.prod(x.shape)) * x.dtype.itemsize for x in tuple(args) + tuple(outs))
    return pl.pallas_call(
        kernel,
        out_shape=tuple(outs),
        in_specs=[SMEM_SPEC] + [VMEM_SPEC] * (len(args) - 1),
        out_specs=(VMEM_SPEC,) * len(outs),
        scratch_shapes=list(scratch),
        compiler_params=pltpu.CompilerParams(vmem_limit_bytes=int(total * 1.25) + 4 * 1024 * 1024),
        cost_estimate=pl.CostEstimate(flops=1000, bytes_accessed=1000, transcendentals=0),
    )(*args)


def row_chunks(count):
    pieces = -(-count // 512)
    if count % (16 * pieces):
        pieces = 1
    return pieces, count // pieces


def token_pack_kernel(tokens, part_rows, capacity, padded, info, block, compact, place, own_parts, table, parts):
    width = compact.shape[1]
    per_row = width // tokens
    table[...] = block[tokens:, :].astype(F32)

    def parts_of(expert):
        row, lane = expert // per_row, pl.multiple_of((expert % per_row) * tokens, tokens)
        parts[...] = jnp.zeros_like(parts)
        for p in range(3):
            found = lax.broadcasted_iota(I32, (table.shape[0], tokens), 0) == p * part_rows + row
            parts[p:p + 1, :] = jnp.sum(
                jnp.where(found, table[:, pl.ds(lane, tokens)], 0.0), axis=0, keepdims=True)
        return parts[...]

    own_parts[...] = parts_of(info[0]).astype(BF)
    theirs = parts_of(info[1])
    named = jnp.sum(theirs, axis=0, keepdims=True) > 0.0
    row_at = lax.broadcasted_iota(I32, (tokens, tokens), 0)
    column_at = lax.broadcasted_iota(I32, (tokens, tokens), 1)
    until = (row_at <= column_at).astype(F32).astype(BF)
    ones = jnp.broadcast_to(named.astype(F32), (TAIL, tokens)).astype(BF)
    rank = jnp.dot(ones, until, preferred_element_type=F32)[:1, :].astype(I32) - 1
    picked = ((row_at == rank) & named & (row_at < capacity)).astype(F32).astype(BF)
    place[...] = picked[:padded, :]
    compact[:padded, :] = dot(picked[:padded, :], block[:tokens, :], ROWS).astype(BF)
    compact[padded:, :] = jnp.zeros((TAIL, width), BF)
    compact[padded:, :tokens] = dot(theirs.astype(BF), picked, LAST).astype(BF)


def grad_pack_kernel(info, block, place, compact):
    compact[...] = dot(place[...], block[...], ROWS).astype(BF)


def lay_out(lines, tokens, padded, blocks, compact, rows):
    for k in range(lines):
        rows[k * tokens:(k + 1) * tokens, :] = blocks[k][:tokens, :]
        at = lines * tokens + k * padded
        rows[at:at + padded, :] = compact[k][:padded, :]


def token_rows_kernel(lines, tokens, padded, info, *refs):
    n = lines
    blocks, compact, own_parts = refs[:n], refs[n:2 * n], refs[2 * n:3 * n]
    rows, weights = refs[3 * n:]
    lay_out(n, tokens, padded, blocks, compact, rows)
    eye = (lax.broadcasted_iota(I32, (tokens, tokens), 0)
           == lax.broadcasted_iota(I32, (tokens, tokens), 1))
    for k in range(n):
        for first, size, tail in (
            (k * tokens, tokens, own_parts[k][...]),
            (n * tokens + k * padded, padded, compact[k][padded:, :tokens]),
        ):
            row = jnp.sum(tail.astype(F32), axis=0, keepdims=True)
            column = jnp.sum(jnp.where(eye, row, 0.0), axis=1, keepdims=True)
            weights[first:first + size, :] = column[:size]


def grad_rows_kernel(lines, tokens, padded, info, *refs):
    lay_out(lines, tokens, padded, refs[:lines], refs[lines:2 * lines], refs[2 * lines])


def halves(info, width):
    core = info[2]
    return pl.ds(pl.multiple_of(core * width, width), width), pl.ds(pl.multiple_of((1 - core) * width, width), width)


def forward_kernel(pieces, chunk, info, own, other, weights, gate_w, up_w, down_w, gate, upward, scaled, sent):
    mine, theirs = halves(info, own.shape[1])

    @pl.loop(0, pieces)
    def _(i):
        at = pl.ds(pl.multiple_of(i * chunk, 16), chunk)
        a, b = own[at, :], other[at, :]
        g = dot(a, gate_w[mine, :], ROWS) + dot(b, gate_w[theirs, :], ROWS)
        u = dot(a, up_w[mine, :], ROWS) + dot(b, up_w[theirs, :], ROWS)
        gate[at, :] = g
        upward[at, :] = u
        h = (weights[at, :] * (g * jax.nn.sigmoid(g) * u)).astype(BF)
        scaled[at, :] = h
        sent[at, :] = dot(h, down_w[:, theirs], ROWS).astype(BF)


def backward_kernel(pieces, chunk, lines, tokens, padded, info, own, other, weights, gate, upward, gate_w, up_w,
                    down_w, grad_gate, grad_up, sent, dense_tails, compact_tails, values):
    mine, theirs = halves(info, own.shape[1])

    @pl.loop(0, pieces)
    def _(i):
        at = pl.ds(pl.multiple_of(i * chunk, 16), chunk)
        plain = dot(own[at, :], down_w[:, mine], LAST) + dot(other[at, :], down_w[:, theirs], LAST)
        g, u = gate[at, :], upward[at, :]
        sig = jax.nn.sigmoid(g)
        through = g * sig
        values[at, :] = jnp.sum(through * u * plain, axis=1, keepdims=True)
        scaled = weights[at, :] * plain
        gg = (scaled * u * sig * (1.0 + g * (1.0 - sig))).astype(BF)
        gu = (scaled * through).astype(BF)
        grad_gate[at, :] = gg
        grad_up[at, :] = gu
        sent[at, :] = (dot(gg, gate_w[theirs, :], LAST) + dot(gu, up_w[theirs, :], LAST)).astype(BF)

    eye = (lax.broadcasted_iota(I32, (tokens, tokens), 0)
           == lax.broadcasted_iota(I32, (tokens, tokens), 1))
    for k in range(lines):
        for first, size, tails in (
            (k * tokens, tokens, dense_tails),
            (lines * tokens + k * padded, padded, compact_tails),
        ):
            column = values[first:first + size, :]
            row = jnp.sum(jnp.where(eye[:size, :], column, 0.0), axis=0, keepdims=True)
            high = row.astype(BF).astype(F32)
            middle = (row - high).astype(BF).astype(F32)
            low = row - high - middle
            at = lax.broadcasted_iota(I32, (TAIL, tokens), 0)
            tails[k] = jnp.where(at == 0, high, jnp.where(at == 1, middle, jnp.where(at == 2, low, 0.0)))


def join_kernel(lines, tokens, padded, forward, info, came, *refs):
    width = came.shape[1]
    mine, _ = halves(info, width)
    if forward:
        scaled, down_w = refs[:2]
        dense, messages = refs[2], refs[3:]

        def product(first, size):
            return dot(scaled[first:first + size, :], down_w[:, mine], ROWS)
    else:
        grad_gate, grad_up, gate_w, up_w, tails = refs[:5]
        dense, messages = refs[5], refs[6:]

        def product(first, size):
            at = slice(first, first + size)
            return dot(grad_gate[at, :], gate_w[mine, :], LAST) + dot(grad_up[at, :], up_w[mine, :], LAST)

    def joined(first, size):
        return product(first, size) + came[first:first + size, :].astype(F32)

    start = lines * tokens
    for first in range(0, lines, 4):
        count = min(4, lines - first)
        total = joined(start + first * padded, count * padded).astype(BF)
        for k in range(first, first + count):
            messages[k][:padded, :] = total[(k - first) * padded:(k - first + 1) * padded]
            if not forward:
                messages[k][padded:, :] = jnp.zeros((TAIL, width), BF)
                messages[k][padded:, :tokens] = tails[k].astype(BF)
    for first in range(0, lines, 4):
        count = min(4, lines - first)
        total = joined(first * tokens, count * tokens)
        for k in range(first, first + count):
            dense[k] = total[(k - first) * tokens:(k - first + 1) * tokens]


def home_kernel(k, tokens, padded, tailed, info, dense, back, place, *refs):
    message = refs[-1]
    block = dense[k] + dot(place[...], back[:padded, :], FIRST)
    message[:tokens, :] = block.astype(BF)
    if not tailed:
        return
    tails = refs[0]
    message[tokens:, :] = jnp.zeros((TAIL, message.shape[1]), BF)
    theirs = dot(back[padded:, :padded], place[...], ROWS)
    message[tokens:, :tokens] = jnp.concatenate([tails[k][:8], theirs[:8]], axis=0).astype(BF)


def per_device(tokens, expert_ids, router_weights, gate_weight, up_weight, down_weight, grad_out):
    token_count, half_width = tokens.shape
    hidden_half = gate_weight.shape[2]
    top_count = expert_ids.shape[1]
    experts = lax.axis_size("expert")
    capacity = min(token_count, 3 * token_count * top_count // (2 * experts))
    padded = -(-capacity // 16) * 16
    lines = experts // 2
    mine = lax.axis_index("expert")
    core = lax.axis_index("tensor")
    at_line = mine // 2
    peer = mine + 1 - 2 * (mine % 2)
    settle = lax.optimization_barrier

    def over_pair(x):
        return lax.ppermute(x, "expert", [(i, i + 1 - 2 * (i % 2)) for i in range(experts)])

    def over_line(x, k):
        return lax.ppermute(
            x, "expert",
            [(i, ((i // 2 + k) % lines) * 2 + i % 2) for i in range(experts)],
        )

    def over_core(x):
        return lax.ppermute(x, "tensor", [(0, 1), (1, 0)])

    chosen = expert_ids[:, :, None] == jnp.arange(experts, dtype=I32)[None, None, :]
    table = jnp.sum(jnp.where(chosen, router_weights[:, :, None], 0.0), axis=1).T
    part_rows = experts * token_count // half_width
    parts = jnp.concatenate([p.reshape(part_rows, half_width) for p in split_three(table)])
    tail = -(-3 * part_rows // TAIL) * TAIL
    parts = jnp.pad(parts, ((0, tail - 3 * part_rows), (0, 0)))
    first = jnp.concatenate([tokens, parts])

    info = jnp.stack([mine, peer, core]).astype(I32)
    sizes = (lines, token_count, padded)
    row_count = lines * (token_count + padded)
    half_rows = shape_of((row_count, half_width))
    hidden_rows = (row_count, hidden_half)
    gate_local = gate_weight[0]
    up_local = up_weight[0]
    down_local = down_weight[0]
    pieces, chunk = row_chunks(row_count)
    every = range(lines)
    by_reach = sorted(range(1, lines), key=lambda k: min(k, lines - k))

    blocks = {0: first}
    for k in by_reach:
        blocks[k] = over_line(first, k)
    compact, places, own_parts, early = {}, {}, {}, []
    for k in [0] + by_reach:
        packed, places[k], own_parts[k] = local_call(
            functools.partial(token_pack_kernel, token_count, part_rows, capacity, padded),
            (shape_of((padded + TAIL, half_width)), shape_of((padded, token_count)),
             shape_of((TAIL, token_count))),
            (info, blocks[k]),
            (pltpu.VMEM((tail, half_width), F32), pltpu.VMEM((TAIL, token_count), F32)),
        )
        if k != by_reach[-1]:
            early.append(packed)
        compact[k] = over_pair(packed)

    (first_packed,) = local_call(
        grad_pack_kernel, (shape_of((padded, half_width)),), (info, grad_out, places[0]))
    grad_first = over_pair(first_packed)
    soon = {k: compact[k] for k in [0] + by_reach[:-1]}
    held_grad, blocks, early, soon, grad_first = settle((grad_out, blocks, early, soon, grad_first))
    compact.update(soon)
    grad_blocks = {0: held_grad}
    for k in by_reach:
        grad_blocks[k] = over_line(held_grad, k)

    def grad_pack(k):
        return local_call(
            grad_pack_kernel, (shape_of((padded, half_width)),), (info, grad_blocks[k], places[k]))[0]

    near, far = by_reach[:-1], by_reach[-1]
    grad_packed = {k: grad_pack(k) for k in by_reach}
    grad_compact = {k: over_pair(grad_packed[k]) for k in by_reach}
    grad_compact[0] = grad_first
    ahead = {k: grad_compact[k] for k in near[:1]}
    compact, grad_blocks, grad_packed, ahead = settle((compact, grad_blocks, grad_packed, ahead))
    grad_compact.update(ahead)
    rows, weights = local_call(
        functools.partial(token_rows_kernel, *sizes),
        (half_rows, shape_of((row_count, 1), F32)),
        (info, *[blocks[k] for k in every], *[compact[k] for k in every], *[own_parts[k] for k in every]))
    rows_other = over_core(rows)
    gate, upward, scaled, sent = local_call(
        functools.partial(forward_kernel, pieces, chunk),
        (shape_of(hidden_rows, F32), shape_of(hidden_rows, F32), shape_of(hidden_rows), half_rows),
        (info, rows, rows_other, weights, gate_local, up_local, down_local))
    sent, grad_compact = settle((sent, grad_compact))
    out_dense, *out_packed = local_call(
        functools.partial(join_kernel, *sizes, True),
        (shape_of((lines, token_count, half_width), F32),
         *[shape_of((padded, half_width)) for _ in every]),
        (info, over_core(sent), scaled, down_local))

    outward = by_reach[::-1]
    out_back = {k: over_pair(out_packed[k]) for k in near}
    (grad_rows,) = local_call(
        functools.partial(grad_rows_kernel, *sizes), (half_rows,),
        (info, *[grad_blocks[k] for k in every], *[grad_compact[k] for k in every]))
    grad_other, out_packed = settle((over_core(grad_rows), out_packed))
    grad_gate, grad_up, sent, dense_tails, compact_tails = local_call(
        functools.partial(backward_kernel, pieces, chunk, *sizes),
        (shape_of(hidden_rows), shape_of(hidden_rows), half_rows,
         shape_of((lines, TAIL, token_count), F32), shape_of((lines, TAIL, token_count), F32)),
        (info, grad_rows, grad_other, weights, gate, upward, gate_local, up_local, down_local),
        (pltpu.VMEM((row_count, 1), F32),))

    def to_home(k, dense, back, *tails):
        extra = TAIL if tails else 0
        return local_call(
            functools.partial(home_kernel, k, token_count, padded, bool(tails)),
            (shape_of((token_count + extra, half_width)),), (info, dense, back[k], places[k], *tails))[0]

    def summed(blocks):
        total = blocks[0][:token_count].astype(F32)
        for k in range(1, lines):
            total = total + blocks[k][:token_count].astype(F32)
        return total.astype(BF)

    sent, out_back = settle((sent, out_back))
    out_home = {k: to_home(k, out_dense, out_back) for k in near}
    out_back[far] = over_pair(out_packed[far])

    def whole(own, other):
        return jnp.concatenate(
            [jnp.where(core == 0, own, other), jnp.where(core == 0, other, own)], axis=1)

    came, out_back[far] = settle((over_core(sent), out_back[far]))
    out_came = {k: over_line(out_home[k], lines - k) for k in near}
    in_dense, *in_packed = local_call(
        functools.partial(join_kernel, *sizes, False),
        (shape_of((lines, token_count, half_width), F32),
         *[shape_of((padded + TAIL, half_width)) for _ in every]),
        (info, came, grad_gate, grad_up, gate_local, up_local, compact_tails))
    in_packed, out_came = settle((in_packed, out_came))
    far_home = to_home(far, out_dense, out_back)
    out_came[far] = over_line(far_home, lines - far)
    in_back, in_home, sequence = {}, {}, outward + [0]
    for i, k in enumerate(sequence):
        packed = in_packed[k]
        if i >= 2:
            packed, _ = settle((packed, in_home[sequence[i - 2]]))
        in_back[k] = over_pair(packed)
        in_home[k] = to_home(k, in_dense, in_back, dense_tails)
    last, _ = settle((out_packed[0], in_back[sequence[1]]))
    out_back[0] = over_pair(last)
    ready, out_came = settle(({k: in_home[k] for k in sequence[:2]}, out_came))
    out_came[0] = to_home(0, out_dense, out_back)
    in_home.update(ready)
    layer_out = summed(out_came)
    rows, rows_other, grad_rows, _ = settle((rows, rows_other, grad_rows, far_home))
    rows = whole(rows, rows_other)
    gate_grad = dot(rows, grad_gate, FIRST).astype(BF)
    down_grad = dot(scaled, whole(grad_rows, grad_other), FIRST).astype(BF)
    in_home[sequence[0]], gate_grad = settle((in_home[sequence[0]], gate_grad))
    in_home[sequence[1]], down_grad = settle((in_home[sequence[1]], down_grad))
    last_home, layer_out, rows, grad_up = settle(([in_home[k] for k in outward], layer_out, rows, grad_up))
    in_home = {k: over_line(in_home[k], lines - k) if k else in_home[0] for k in every}
    input_grad = summed(in_home)

    up_grad = dot(rows, grad_up, FIRST).astype(BF)

    held = []
    for k in every:
        values = in_home[k][token_count:, :token_count].astype(F32)
        held.append(jnp.stack([jnp.sum(values[:8], axis=0), jnp.sum(values[8:], axis=0)]))
    flat = jnp.stack(held).reshape(experts, token_count)
    place = (expert_ids // 2 - at_line) % lines
    slot = place * 2 + ((expert_ids % 2) != (mine % 2)).astype(I32)
    match = slot[:, :, None] == jnp.arange(experts, dtype=I32)[None, None, :]
    half_value = jnp.sum(jnp.where(match, flat.T[:, None, :], 0.0), axis=2)
    weight_grad = half_value + over_core(half_value)
    return (layer_out, input_grad, weight_grad, gate_grad[None], up_grad[None], down_grad[None])


def solution(mesh):
    in_specs = (
        P(("group", "expert"), "tensor"),
        P(("group", "expert"), None),
        P(("group", "expert"), None),
        P("expert", None, "tensor"),
        P("expert", None, "tensor"),
        P("expert", "tensor", None),
        P(("group", "expert"), "tensor"),
    )
    out_specs = (
        P(("group", "expert"), "tensor"),
        P(("group", "expert"), "tensor"),
        P(("group", "expert"), None),
        P(("group", "expert"), None, "tensor"),
        P(("group", "expert"), None, "tensor"),
        P(("group", "expert"), "tensor", None),
    )
    return jax.shard_map(
        per_device, mesh=mesh, in_specs=in_specs, out_specs=out_specs, check_vma=False
    )
```

```python
import functools

import jax
import jax.numpy as jnp
import numpy as np
from jax import lax
from jax.experimental import pallas as pl
from jax.experimental.pallas import tpu as pltpu
from jax.sharding import PartitionSpec as P

BF = jnp.bfloat16
F32 = jnp.float32
I32 = jnp.int32
TAIL = 16
ROWS = ((1,), (0,))
LAST = ((1,), (1,))
FIRST = ((0,), (0,))

SMEM_SPEC = pl.BlockSpec(memory_space=pltpu.SMEM)
VMEM_SPEC = pl.BlockSpec(memory_space=pltpu.VMEM)


def dot(a, b, contract):
    return lax.dot_general(a, b, (contract, ((), ())), preferred_element_type=F32)


def split_three(values):
    high = lax.reduce_precision(values, 8, 7)
    rest = values - high
    middle = lax.reduce_precision(rest, 8, 7)
    low = rest - middle
    return [part.astype(BF) for part in (high, middle, low)]


def shape_of(shape, dtype=BF):
    return jax.ShapeDtypeStruct(shape, dtype)


def local_call(kernel, outs, args, scratch=()):
    total = sum(int(np.prod(x.shape)) * x.dtype.itemsize for x in tuple(args) + tuple(outs))
    return pl.pallas_call(
        kernel,
        out_shape=tuple(outs),
        in_specs=[SMEM_SPEC] + [VMEM_SPEC] * (len(args) - 1),
        out_specs=(VMEM_SPEC,) * len(outs),
        scratch_shapes=list(scratch),
        compiler_params=pltpu.CompilerParams(vmem_limit_bytes=int(total * 1.25) + 4 * 1024 * 1024),
        cost_estimate=pl.CostEstimate(flops=1000, bytes_accessed=1000, transcendentals=0),
    )(*args)


def row_chunks(count):
    pieces = -(-count // 512)
    if count % (16 * pieces):
        pieces = 1
    return pieces, count // pieces


def token_pack_kernel(tokens, part_rows, capacity, padded, info, block, compact, place, own_parts, table, parts):
    width = compact.shape[1]
    per_row = width // tokens
    table[...] = block[tokens:, :].astype(F32)

    def parts_of(expert):
        row, lane = expert // per_row, pl.multiple_of((expert % per_row) * tokens, tokens)
        parts[...] = jnp.zeros_like(parts)
        for p in range(3):
            found = lax.broadcasted_iota(I32, (table.shape[0], tokens), 0) == p * part_rows + row
            parts[p:p + 1, :] = jnp.sum(
                jnp.where(found, table[:, pl.ds(lane, tokens)], 0.0), axis=0, keepdims=True)
        return parts[...]

    own_parts[...] = parts_of(info[0]).astype(BF)
    theirs = parts_of(info[1])
    named = jnp.sum(theirs, axis=0, keepdims=True) > 0.0
    row_at = lax.broadcasted_iota(I32, (tokens, tokens), 0)
    column_at = lax.broadcasted_iota(I32, (tokens, tokens), 1)
    until = (row_at <= column_at).astype(F32).astype(BF)
    ones = jnp.broadcast_to(named.astype(F32), (TAIL, tokens)).astype(BF)
    rank = jnp.dot(ones, until, preferred_element_type=F32)[:1, :].astype(I32) - 1
    picked = ((row_at == rank) & named & (row_at < capacity)).astype(F32).astype(BF)
    place[...] = picked[:padded, :]
    compact[:padded, :] = dot(picked[:padded, :], block[:tokens, :], ROWS).astype(BF)
    compact[padded:, :] = jnp.zeros((TAIL, width), BF)
    compact[padded:, :tokens] = dot(theirs.astype(BF), picked, LAST).astype(BF)


def grad_pack_kernel(info, block, place, compact):
    compact[...] = dot(place[...], block[...], ROWS).astype(BF)


def lay_out(lines, tokens, padded, blocks, compact, rows):
    for k in range(lines):
        rows[k * tokens:(k + 1) * tokens, :] = blocks[k][:tokens, :]
        at = lines * tokens + k * padded
        rows[at:at + padded, :] = compact[k][:padded, :]


def token_rows_kernel(lines, tokens, padded, info, *refs):
    n = lines
    blocks, compact, own_parts = refs[:n], refs[n:2 * n], refs[2 * n:3 * n]
    rows, weights = refs[3 * n:]
    lay_out(n, tokens, padded, blocks, compact, rows)
    eye = (lax.broadcasted_iota(I32, (tokens, tokens), 0)
           == lax.broadcasted_iota(I32, (tokens, tokens), 1))
    for k in range(n):
        for first, size, tail in (
            (k * tokens, tokens, own_parts[k][...]),
            (n * tokens + k * padded, padded, compact[k][padded:, :tokens]),
        ):
            row = jnp.sum(tail.astype(F32), axis=0, keepdims=True)
            column = jnp.sum(jnp.where(eye, row, 0.0), axis=1, keepdims=True)
            weights[first:first + size, :] = column[:size]


def grad_rows_kernel(lines, tokens, padded, info, *refs):
    lay_out(lines, tokens, padded, refs[:lines], refs[lines:2 * lines], refs[2 * lines])


def halves(info, width):
    core = info[2]
    return pl.ds(pl.multiple_of(core * width, width), width), pl.ds(pl.multiple_of((1 - core) * width, width), width)


def forward_kernel(pieces, chunk, info, own, other, weights, gate_w, up_w, down_w, gate, upward, scaled, sent):
    mine, theirs = halves(info, own.shape[1])

    @pl.loop(0, pieces)
    def _(i):
        at = pl.ds(pl.multiple_of(i * chunk, 16), chunk)
        a, b = own[at, :], other[at, :]
        g = dot(a, gate_w[mine, :], ROWS) + dot(b, gate_w[theirs, :], ROWS)
        u = dot(a, up_w[mine, :], ROWS) + dot(b, up_w[theirs, :], ROWS)
        gate[at, :] = g
        upward[at, :] = u
        h = (weights[at, :] * (g * jax.nn.sigmoid(g) * u)).astype(BF)
        scaled[at, :] = h
        sent[at, :] = dot(h, down_w[:, theirs], ROWS).astype(BF)


def backward_kernel(pieces, chunk, lines, tokens, padded, info, own, other, weights, gate, upward, gate_w, up_w,
                    down_w, grad_gate, grad_up, sent, dense_tails, compact_tails, values):
    mine, theirs = halves(info, own.shape[1])

    @pl.loop(0, pieces)
    def _(i):
        at = pl.ds(pl.multiple_of(i * chunk, 16), chunk)
        plain = dot(own[at, :], down_w[:, mine], LAST) + dot(other[at, :], down_w[:, theirs], LAST)
        g, u = gate[at, :], upward[at, :]
        sig = jax.nn.sigmoid(g)
        through = g * sig
        values[at, :] = jnp.sum(through * u * plain, axis=1, keepdims=True)
        scaled = weights[at, :] * plain
        gg = (scaled * u * sig * (1.0 + g * (1.0 - sig))).astype(BF)
        gu = (scaled * through).astype(BF)
        grad_gate[at, :] = gg
        grad_up[at, :] = gu
        sent[at, :] = (dot(gg, gate_w[theirs, :], LAST) + dot(gu, up_w[theirs, :], LAST)).astype(BF)

    eye = (lax.broadcasted_iota(I32, (tokens, tokens), 0)
           == lax.broadcasted_iota(I32, (tokens, tokens), 1))
    for k in range(lines):
        for first, size, tails in (
            (k * tokens, tokens, dense_tails),
            (lines * tokens + k * padded, padded, compact_tails),
        ):
            column = values[first:first + size, :]
            row = jnp.sum(jnp.where(eye[:size, :], column, 0.0), axis=0, keepdims=True)
            high = row.astype(BF).astype(F32)
            middle = (row - high).astype(BF).astype(F32)
            low = row - high - middle
            at = lax.broadcasted_iota(I32, (TAIL, tokens), 0)
            tails[k] = jnp.where(at == 0, high, jnp.where(at == 1, middle, jnp.where(at == 2, low, 0.0)))


def join_kernel(lines, tokens, padded, forward, info, came, *refs):
    width = came.shape[1]
    mine, _ = halves(info, width)
    if forward:
        scaled, down_w = refs[:2]
        dense, messages = refs[2], refs[3:]

        def product(first, size):
            return dot(scaled[first:first + size, :], down_w[:, mine], ROWS)
    else:
        grad_gate, grad_up, gate_w, up_w, tails = refs[:5]
        dense, messages = refs[5], refs[6:]

        def product(first, size):
            at = slice(first, first + size)
            return dot(grad_gate[at, :], gate_w[mine, :], LAST) + dot(grad_up[at, :], up_w[mine, :], LAST)

    def joined(first, size):
        return product(first, size) + came[first:first + size, :].astype(F32)

    start = lines * tokens
    for first in range(0, lines, 4):
        count = min(4, lines - first)
        total = joined(start + first * padded, count * padded).astype(BF)
        for k in range(first, first + count):
            messages[k][:padded, :] = total[(k - first) * padded:(k - first + 1) * padded]
            if not forward:
                messages[k][padded:, :] = jnp.zeros((TAIL, width), BF)
                messages[k][padded:, :tokens] = tails[k].astype(BF)
    for first in range(0, lines, 4):
        count = min(4, lines - first)
        total = joined(first * tokens, count * tokens)
        for k in range(first, first + count):
            dense[k] = total[(k - first) * tokens:(k - first + 1) * tokens]


def home_kernel(k, tokens, padded, tailed, info, dense, back, place, *refs):
    message = refs[-1]
    block = dense[k] + dot(place[...], back[:padded, :], FIRST)
    message[:tokens, :] = block.astype(BF)
    if not tailed:
        return
    tails = refs[0]
    message[tokens:, :] = jnp.zeros((TAIL, message.shape[1]), BF)
    theirs = dot(back[padded:, :padded], place[...], ROWS)
    message[tokens:, :tokens] = jnp.concatenate([tails[k][:8], theirs[:8]], axis=0).astype(BF)


def per_device(tokens, expert_ids, router_weights, gate_weight, up_weight, down_weight, grad_out):
    token_count, half_width = tokens.shape
    hidden_half = gate_weight.shape[2]
    top_count = expert_ids.shape[1]
    experts = lax.axis_size("expert")
    capacity = min(token_count, 3 * token_count * top_count // (2 * experts))
    padded = -(-capacity // 16) * 16
    lines = experts // 2
    mine = lax.axis_index("expert")
    core = lax.axis_index("tensor")
    at_line = mine // 2
    peer = mine + 1 - 2 * (mine % 2)
    settle = lax.optimization_barrier

    def over_pair(x):
        return lax.ppermute(x, "expert", [(i, i + 1 - 2 * (i % 2)) for i in range(experts)])

    def over_line(x, k):
        return lax.ppermute(
            x, "expert",
            [(i, ((i // 2 + k) % lines) * 2 + i % 2) for i in range(experts)],
        )

    def over_core(x):
        return lax.ppermute(x, "tensor", [(0, 1), (1, 0)])

    chosen = expert_ids[:, :, None] == jnp.arange(experts, dtype=I32)[None, None, :]
    table = jnp.sum(jnp.where(chosen, router_weights[:, :, None], 0.0), axis=1).T
    part_rows = experts * token_count // half_width
    parts = jnp.concatenate([p.reshape(part_rows, half_width) for p in split_three(table)])
    tail = -(-3 * part_rows // TAIL) * TAIL
    parts = jnp.pad(parts, ((0, tail - 3 * part_rows), (0, 0)))
    first = jnp.concatenate([tokens, parts])

    info = jnp.stack([mine, peer, core]).astype(I32)
    sizes = (lines, token_count, padded)
    row_count = lines * (token_count + padded)
    half_rows = shape_of((row_count, half_width))
    hidden_rows = (row_count, hidden_half)
    gate_local = gate_weight[0]
    up_local = up_weight[0]
    down_local = down_weight[0]
    pieces, chunk = row_chunks(row_count)
    every = range(lines)
    by_reach = sorted(range(1, lines), key=lambda k: min(k, lines - k))

    blocks = {0: first}
    for k in by_reach:
        blocks[k] = over_line(first, k)
    compact, places, own_parts, early = {}, {}, {}, []
    for k in [0] + by_reach:
        packed, places[k], own_parts[k] = local_call(
            functools.partial(token_pack_kernel, token_count, part_rows, capacity, padded),
            (shape_of((padded + TAIL, half_width)), shape_of((padded, token_count)),
             shape_of((TAIL, token_count))),
            (info, blocks[k]),
            (pltpu.VMEM((tail, half_width), F32), pltpu.VMEM((TAIL, token_count), F32)),
        )
        if k != by_reach[-1]:
            early.append(packed)
        compact[k] = over_pair(packed)

    (first_packed,) = local_call(
        grad_pack_kernel, (shape_of((padded, half_width)),), (info, grad_out, places[0]))
    grad_first = over_pair(first_packed)
    soon = {k: compact[k] for k in [0] + by_reach[:-1]}
    held_grad, blocks, early, soon, grad_first = settle((grad_out, blocks, early, soon, grad_first))
    compact.update(soon)
    grad_blocks = {0: held_grad}
    for k in by_reach:
        grad_blocks[k] = over_line(held_grad, k)

    def grad_pack(k):
        return local_call(
            grad_pack_kernel, (shape_of((padded, half_width)),), (info, grad_blocks[k], places[k]))[0]

    near, far = by_reach[:-1], by_reach[-1]
    grad_packed = {k: grad_pack(k) for k in near}
    grad_compact = {k: over_pair(grad_packed[k]) for k in near}
    grad_compact[0] = grad_first
    compact, near_blocks, near_packed = settle(
        (compact, {k: grad_blocks[k] for k in near}, grad_packed))
    grad_blocks.update(near_blocks)
    rows, weights = local_call(
        functools.partial(token_rows_kernel, *sizes),
        (half_rows, shape_of((row_count, 1), F32)),
        (info, *[blocks[k] for k in every], *[compact[k] for k in every], *[own_parts[k] for k in every]))
    rows_other = over_core(rows)
    gate, upward, scaled, sent = local_call(
        functools.partial(forward_kernel, pieces, chunk),
        (shape_of(hidden_rows, F32), shape_of(hidden_rows, F32), shape_of(hidden_rows), half_rows),
        (info, rows, rows_other, weights, gate_local, up_local, down_local))
    sent, grad_compact = settle((sent, grad_compact))
    out_dense, *out_packed = local_call(
        functools.partial(join_kernel, *sizes, True),
        (shape_of((lines, token_count, half_width), F32),
         *[shape_of((padded, half_width)) for _ in every]),
        (info, over_core(sent), scaled, down_local))

    outward = by_reach[::-1]
    out_back = {k: over_pair(out_packed[k]) for k in near}
    grad_blocks[far], out_back = settle((grad_blocks[far], out_back))
    grad_compact[far] = over_pair(grad_pack(far))
    (grad_rows,) = local_call(
        functools.partial(grad_rows_kernel, *sizes), (half_rows,),
        (info, *[grad_blocks[k] for k in every], *[grad_compact[k] for k in every]))
    grad_other, out_packed = settle((over_core(grad_rows), out_packed))
    grad_gate, grad_up, sent, dense_tails, compact_tails = local_call(
        functools.partial(backward_kernel, pieces, chunk, *sizes),
        (shape_of(hidden_rows), shape_of(hidden_rows), half_rows,
         shape_of((lines, TAIL, token_count), F32), shape_of((lines, TAIL, token_count), F32)),
        (info, grad_rows, grad_other, weights, gate, upward, gate_local, up_local, down_local),
        (pltpu.VMEM((row_count, 1), F32),))

    def to_home(k, dense, back, *tails):
        extra = TAIL if tails else 0
        return local_call(
            functools.partial(home_kernel, k, token_count, padded, bool(tails)),
            (shape_of((token_count + extra, half_width)),), (info, dense, back[k], places[k], *tails))[0]

    def summed(blocks):
        total = blocks[0][:token_count].astype(F32)
        for k in range(1, lines):
            total = total + blocks[k][:token_count].astype(F32)
        return total.astype(BF)

    out_home = {k: to_home(k, out_dense, out_back) for k in near}
    out_came = {k: over_line(out_home[k], lines - k) for k in near}
    sent, out_came = settle((sent, out_came))
    out_back[far] = over_pair(out_packed[far])

    def whole(own, other):
        return jnp.concatenate(
            [jnp.where(core == 0, own, other), jnp.where(core == 0, other, own)], axis=1)

    came, out_back[far] = settle((over_core(sent), out_back[far]))
    out_came = {k: over_line(out_home[k], lines - k) for k in near}
    in_dense, *in_packed = local_call(
        functools.partial(join_kernel, *sizes, False),
        (shape_of((lines, token_count, half_width), F32),
         *[shape_of((padded + TAIL, half_width)) for _ in every]),
        (info, came, grad_gate, grad_up, gate_local, up_local, compact_tails))
    in_packed, out_came = settle((in_packed, out_came))
    far_home = to_home(far, out_dense, out_back)
    out_came[far] = over_line(far_home, lines - far)
    in_back, in_home, sequence = {}, {}, outward + [0]
    for i, k in enumerate(sequence):
        packed = in_packed[k]
        if i >= 2:
            packed, _ = settle((packed, in_home[sequence[i - 2]]))
        in_back[k] = over_pair(packed)
        in_home[k] = to_home(k, in_dense, in_back, dense_tails)
    last, _ = settle((out_packed[0], in_back[sequence[1]]))
    out_back[0] = over_pair(last)
    ready, out_came = settle(({k: in_home[k] for k in sequence[:2]}, out_came))
    out_came[0] = to_home(0, out_dense, out_back)
    in_home.update(ready)
    layer_out = summed(out_came)
    rows, rows_other, grad_rows, _ = settle((rows, rows_other, grad_rows, far_home))
    rows = whole(rows, rows_other)
    gate_grad = dot(rows, grad_gate, FIRST).astype(BF)
    down_grad = dot(scaled, whole(grad_rows, grad_other), FIRST).astype(BF)
    in_home[sequence[0]], gate_grad = settle((in_home[sequence[0]], gate_grad))
    in_home[sequence[1]], down_grad = settle((in_home[sequence[1]], down_grad))
    last_home, layer_out, rows, grad_up = settle(([in_home[k] for k in outward], layer_out, rows, grad_up))
    in_home = {k: over_line(in_home[k], lines - k) if k else in_home[0] for k in every}
    input_grad = summed(in_home)

    up_grad = dot(rows, grad_up, FIRST).astype(BF)

    held = []
    for k in every:
        values = in_home[k][token_count:, :token_count].astype(F32)
        held.append(jnp.stack([jnp.sum(values[:8], axis=0), jnp.sum(values[8:], axis=0)]))
    flat = jnp.stack(held).reshape(experts, token_count)
    place = (expert_ids // 2 - at_line) % lines
    slot = place * 2 + ((expert_ids % 2) != (mine % 2)).astype(I32)
    match = slot[:, :, None] == jnp.arange(experts, dtype=I32)[None, None, :]
    half_value = jnp.sum(jnp.where(match, flat.T[:, None, :], 0.0), axis=2)
    weight_grad = half_value + over_core(half_value)
    return (layer_out, input_grad, weight_grad, gate_grad[None], up_grad[None], down_grad[None])


def solution(mesh):
    in_specs = (
        P(("group", "expert"), "tensor"),
        P(("group", "expert"), None),
        P(("group", "expert"), None),
        P("expert", None, "tensor"),
        P("expert", None, "tensor"),
        P("expert", "tensor", None),
        P(("group", "expert"), "tensor"),
    )
    out_specs = (
        P(("group", "expert"), "tensor"),
        P(("group", "expert"), "tensor"),
        P(("group", "expert"), None),
        P(("group", "expert"), None, "tensor"),
        P(("group", "expert"), None, "tensor"),
        P(("group", "expert"), "tensor", None),
    )
    return jax.shard_map(
        per_device, mesh=mesh, in_specs=in_specs, out_specs=out_specs, check_vma=False
    )
```

```python
import functools

import jax
import jax.numpy as jnp
import numpy as np
from jax import lax
from jax.experimental import pallas as pl
from jax.experimental.pallas import tpu as pltpu
from jax.sharding import PartitionSpec as P

BF = jnp.bfloat16
F32 = jnp.float32
I32 = jnp.int32
TAIL = 16
ROWS = ((1,), (0,))
LAST = ((1,), (1,))
FIRST = ((0,), (0,))

SMEM_SPEC = pl.BlockSpec(memory_space=pltpu.SMEM)
VMEM_SPEC = pl.BlockSpec(memory_space=pltpu.VMEM)


def dot(a, b, contract):
    return lax.dot_general(a, b, (contract, ((), ())), preferred_element_type=F32)


def split_three(values):
    high = lax.reduce_precision(values, 8, 7)
    rest = values - high
    middle = lax.reduce_precision(rest, 8, 7)
    low = rest - middle
    return [part.astype(BF) for part in (high, middle, low)]


def shape_of(shape, dtype=BF):
    return jax.ShapeDtypeStruct(shape, dtype)


def local_call(kernel, outs, args, scratch=()):
    total = sum(int(np.prod(x.shape)) * x.dtype.itemsize for x in tuple(args) + tuple(outs))
    return pl.pallas_call(
        kernel,
        out_shape=tuple(outs),
        in_specs=[SMEM_SPEC] + [VMEM_SPEC] * (len(args) - 1),
        out_specs=(VMEM_SPEC,) * len(outs),
        scratch_shapes=list(scratch),
        compiler_params=pltpu.CompilerParams(vmem_limit_bytes=int(total * 1.25) + 4 * 1024 * 1024),
        cost_estimate=pl.CostEstimate(flops=1000, bytes_accessed=1000, transcendentals=0),
    )(*args)


def row_chunks(count):
    pieces = -(-count // 512)
    if count % (16 * pieces):
        pieces = 1
    return pieces, count // pieces


def token_pack_kernel(tokens, part_rows, capacity, padded, info, block, compact, place, own_parts, table, parts):
    width = compact.shape[1]
    per_row = width // tokens
    table[...] = block[tokens:, :].astype(F32)

    def parts_of(expert):
        row, lane = expert // per_row, pl.multiple_of((expert % per_row) * tokens, tokens)
        parts[...] = jnp.zeros_like(parts)
        for p in range(3):
            found = lax.broadcasted_iota(I32, (table.shape[0], tokens), 0) == p * part_rows + row
            parts[p:p + 1, :] = jnp.sum(
                jnp.where(found, table[:, pl.ds(lane, tokens)], 0.0), axis=0, keepdims=True)
        return parts[...]

    own_parts[...] = parts_of(info[0]).astype(BF)
    theirs = parts_of(info[1])
    named = jnp.sum(theirs, axis=0, keepdims=True) > 0.0
    row_at = lax.broadcasted_iota(I32, (tokens, tokens), 0)
    column_at = lax.broadcasted_iota(I32, (tokens, tokens), 1)
    until = (row_at <= column_at).astype(F32).astype(BF)
    ones = jnp.broadcast_to(named.astype(F32), (TAIL, tokens)).astype(BF)
    rank = jnp.dot(ones, until, preferred_element_type=F32)[:1, :].astype(I32) - 1
    picked = ((row_at == rank) & named & (row_at < capacity)).astype(F32).astype(BF)
    place[...] = picked[:padded, :]
    compact[:padded, :] = dot(picked[:padded, :], block[:tokens, :], ROWS).astype(BF)
    compact[padded:, :] = jnp.zeros((TAIL, width), BF)
    compact[padded:, :tokens] = dot(theirs.astype(BF), picked, LAST).astype(BF)


def grad_pack_kernel(info, block, place, compact):
    compact[...] = dot(place[...], block[...], ROWS).astype(BF)


def lay_out(lines, tokens, padded, blocks, compact, rows):
    for k in range(lines):
        rows[k * tokens:(k + 1) * tokens, :] = blocks[k][:tokens, :]
        at = lines * tokens + k * padded
        rows[at:at + padded, :] = compact[k][:padded, :]


def token_rows_kernel(lines, tokens, padded, info, *refs):
    n = lines
    blocks, compact, own_parts = refs[:n], refs[n:2 * n], refs[2 * n:3 * n]
    rows, weights = refs[3 * n:]
    lay_out(n, tokens, padded, blocks, compact, rows)
    eye = (lax.broadcasted_iota(I32, (tokens, tokens), 0)
           == lax.broadcasted_iota(I32, (tokens, tokens), 1))
    for k in range(n):
        for first, size, tail in (
            (k * tokens, tokens, own_parts[k][...]),
            (n * tokens + k * padded, padded, compact[k][padded:, :tokens]),
        ):
            row = jnp.sum(tail.astype(F32), axis=0, keepdims=True)
            column = jnp.sum(jnp.where(eye, row, 0.0), axis=1, keepdims=True)
            weights[first:first + size, :] = column[:size]


def grad_rows_kernel(lines, tokens, padded, info, *refs):
    lay_out(lines, tokens, padded, refs[:lines], refs[lines:2 * lines], refs[2 * lines])


def halves(info, width):
    core = info[2]
    return pl.ds(pl.multiple_of(core * width, width), width), pl.ds(pl.multiple_of((1 - core) * width, width), width)


def forward_kernel(pieces, chunk, info, own, other, weights, gate_w, up_w, down_w, gate, upward, scaled, sent):
    mine, theirs = halves(info, own.shape[1])

    @pl.loop(0, pieces)
    def _(i):
        at = pl.ds(pl.multiple_of(i * chunk, 16), chunk)
        a, b = own[at, :], other[at, :]
        g = dot(a, gate_w[mine, :], ROWS) + dot(b, gate_w[theirs, :], ROWS)
        u = dot(a, up_w[mine, :], ROWS) + dot(b, up_w[theirs, :], ROWS)
        gate[at, :] = g
        upward[at, :] = u
        h = (weights[at, :] * (g * jax.nn.sigmoid(g) * u)).astype(BF)
        scaled[at, :] = h
        sent[at, :] = dot(h, down_w[:, theirs], ROWS).astype(BF)


def backward_kernel(pieces, chunk, lines, tokens, padded, info, own, other, weights, gate, upward, gate_w, up_w,
                    down_w, grad_gate, grad_up, sent, dense_tails, compact_tails, values):
    mine, theirs = halves(info, own.shape[1])

    @pl.loop(0, pieces)
    def _(i):
        at = pl.ds(pl.multiple_of(i * chunk, 16), chunk)
        plain = dot(own[at, :], down_w[:, mine], LAST) + dot(other[at, :], down_w[:, theirs], LAST)
        g, u = gate[at, :], upward[at, :]
        sig = jax.nn.sigmoid(g)
        through = g * sig
        values[at, :] = jnp.sum(through * u * plain, axis=1, keepdims=True)
        scaled = weights[at, :] * plain
        gg = (scaled * u * sig * (1.0 + g * (1.0 - sig))).astype(BF)
        gu = (scaled * through).astype(BF)
        grad_gate[at, :] = gg
        grad_up[at, :] = gu
        sent[at, :] = (dot(gg, gate_w[theirs, :], LAST) + dot(gu, up_w[theirs, :], LAST)).astype(BF)

    eye = (lax.broadcasted_iota(I32, (tokens, tokens), 0)
           == lax.broadcasted_iota(I32, (tokens, tokens), 1))
    for k in range(lines):
        for first, size, tails in (
            (k * tokens, tokens, dense_tails),
            (lines * tokens + k * padded, padded, compact_tails),
        ):
            column = values[first:first + size, :]
            row = jnp.sum(jnp.where(eye[:size, :], column, 0.0), axis=0, keepdims=True)
            high = row.astype(BF).astype(F32)
            middle = (row - high).astype(BF).astype(F32)
            low = row - high - middle
            at = lax.broadcasted_iota(I32, (TAIL, tokens), 0)
            tails[k] = jnp.where(at == 0, high, jnp.where(at == 1, middle, jnp.where(at == 2, low, 0.0)))


def join_kernel(lines, tokens, padded, forward, info, came, *refs):
    width = came.shape[1]
    mine, _ = halves(info, width)
    if forward:
        scaled, down_w = refs[:2]
        dense, messages = refs[2], refs[3:]

        def product(first, size):
            return dot(scaled[first:first + size, :], down_w[:, mine], ROWS)
    else:
        grad_gate, grad_up, gate_w, up_w, tails = refs[:5]
        dense, messages = refs[5], refs[6:]

        def product(first, size):
            at = slice(first, first + size)
            return dot(grad_gate[at, :], gate_w[mine, :], LAST) + dot(grad_up[at, :], up_w[mine, :], LAST)

    def joined(first, size):
        return product(first, size) + came[first:first + size, :].astype(F32)

    start = lines * tokens
    for first in range(0, lines, 4):
        count = min(4, lines - first)
        total = joined(start + first * padded, count * padded).astype(BF)
        for k in range(first, first + count):
            messages[k][:padded, :] = total[(k - first) * padded:(k - first + 1) * padded]
            if not forward:
                messages[k][padded:, :] = jnp.zeros((TAIL, width), BF)
                messages[k][padded:, :tokens] = tails[k].astype(BF)
    for first in range(0, lines, 4):
        count = min(4, lines - first)
        total = joined(first * tokens, count * tokens)
        for k in range(first, first + count):
            dense[k] = total[(k - first) * tokens:(k - first + 1) * tokens]


def home_kernel(k, tokens, padded, tailed, info, dense, back, place, *refs):
    message = refs[-1]
    block = dense[k] + dot(place[...], back[:padded, :], FIRST)
    message[:tokens, :] = block.astype(BF)
    if not tailed:
        return
    tails = refs[0]
    message[tokens:, :] = jnp.zeros((TAIL, message.shape[1]), BF)
    theirs = dot(back[padded:, :padded], place[...], ROWS)
    message[tokens:, :tokens] = jnp.concatenate([tails[k][:8], theirs[:8]], axis=0).astype(BF)


def per_device(tokens, expert_ids, router_weights, gate_weight, up_weight, down_weight, grad_out):
    token_count, half_width = tokens.shape
    hidden_half = gate_weight.shape[2]
    top_count = expert_ids.shape[1]
    experts = lax.axis_size("expert")
    capacity = min(token_count, 3 * token_count * top_count // (2 * experts))
    padded = -(-capacity // 16) * 16
    lines = experts // 2
    mine = lax.axis_index("expert")
    core = lax.axis_index("tensor")
    at_line = mine // 2
    peer = mine + 1 - 2 * (mine % 2)
    settle = lax.optimization_barrier

    def over_pair(x):
        return lax.ppermute(x, "expert", [(i, i + 1 - 2 * (i % 2)) for i in range(experts)])

    def over_line(x, k):
        return lax.ppermute(
            x, "expert",
            [(i, ((i // 2 + k) % lines) * 2 + i % 2) for i in range(experts)],
        )

    def over_core(x):
        return lax.ppermute(x, "tensor", [(0, 1), (1, 0)])

    chosen = expert_ids[:, :, None] == jnp.arange(experts, dtype=I32)[None, None, :]
    table = jnp.sum(jnp.where(chosen, router_weights[:, :, None], 0.0), axis=1).T
    part_rows = experts * token_count // half_width
    parts = jnp.concatenate([p.reshape(part_rows, half_width) for p in split_three(table)])
    tail = -(-3 * part_rows // TAIL) * TAIL
    parts = jnp.pad(parts, ((0, tail - 3 * part_rows), (0, 0)))
    first = jnp.concatenate([tokens, parts])

    info = jnp.stack([mine, peer, core]).astype(I32)
    sizes = (lines, token_count, padded)
    row_count = lines * (token_count + padded)
    half_rows = shape_of((row_count, half_width))
    hidden_rows = (row_count, hidden_half)
    gate_local = gate_weight[0]
    up_local = up_weight[0]
    down_local = down_weight[0]
    pieces, chunk = row_chunks(row_count)
    every = range(lines)
    by_reach = sorted(range(1, lines), key=lambda k: min(k, lines - k))

    blocks = {0: first}
    for k in by_reach:
        blocks[k] = over_line(first, k)
    compact, places, own_parts, early = {}, {}, {}, []
    for k in [0] + by_reach:
        packed, places[k], own_parts[k] = local_call(
            functools.partial(token_pack_kernel, token_count, part_rows, capacity, padded),
            (shape_of((padded + TAIL, half_width)), shape_of((padded, token_count)),
             shape_of((TAIL, token_count))),
            (info, blocks[k]),
            (pltpu.VMEM((tail, half_width), F32), pltpu.VMEM((TAIL, token_count), F32)),
        )
        if k != by_reach[-1]:
            early.append(packed)
        compact[k] = over_pair(packed)

    (first_packed,) = local_call(
        grad_pack_kernel, (shape_of((padded, half_width)),), (info, grad_out, places[0]))
    grad_first = over_pair(first_packed)
    soon = {k: compact[k] for k in [0] + by_reach[:-1]}
    held_grad, blocks, early, soon, grad_first = settle((grad_out, blocks, early, soon, grad_first))
    compact.update(soon)
    grad_blocks = {0: held_grad}
    for k in by_reach:
        grad_blocks[k] = over_line(held_grad, k)

    def grad_pack(k):
        return local_call(
            grad_pack_kernel, (shape_of((padded, half_width)),), (info, grad_blocks[k], places[k]))[0]

    near, far = by_reach[:-1], by_reach[-1]
    grad_packed = {k: grad_pack(k) for k in by_reach}
    grad_compact = {k: over_pair(grad_packed[k]) for k in by_reach}
    grad_compact[0] = grad_first
    ahead = {k: grad_compact[k] for k in near[:1]}
    compact, grad_blocks, grad_packed, ahead = settle((compact, grad_blocks, grad_packed, ahead))
    grad_compact.update(ahead)
    rows, weights = local_call(
        functools.partial(token_rows_kernel, *sizes),
        (half_rows, shape_of((row_count, 1), F32)),
        (info, *[blocks[k] for k in every], *[compact[k] for k in every], *[own_parts[k] for k in every]))
    rows_other = over_core(rows)
    gate, upward, scaled, sent = local_call(
        functools.partial(forward_kernel, pieces, chunk),
        (shape_of(hidden_rows, F32), shape_of(hidden_rows, F32), shape_of(hidden_rows), half_rows),
        (info, rows, rows_other, weights, gate_local, up_local, down_local))
    sent, grad_compact = settle((sent, grad_compact))
    out_dense, *out_packed = local_call(
        functools.partial(join_kernel, *sizes, True),
        (shape_of((lines, token_count, half_width), F32),
         *[shape_of((padded, half_width)) for _ in every]),
        (info, over_core(sent), scaled, down_local))

    outward = by_reach[::-1]
    leading, trailing = outward[:-1], outward[-1]
    out_back = {k: over_pair(out_packed[k]) for k in leading}
    (grad_rows,) = local_call(
        functools.partial(grad_rows_kernel, *sizes), (half_rows,),
        (info, *[grad_blocks[k] for k in every], *[grad_compact[k] for k in every]))
    grad_other, out_packed = settle((over_core(grad_rows), out_packed))
    grad_gate, grad_up, sent, dense_tails, compact_tails = local_call(
        functools.partial(backward_kernel, pieces, chunk, *sizes),
        (shape_of(hidden_rows), shape_of(hidden_rows), half_rows,
         shape_of((lines, TAIL, token_count), F32), shape_of((lines, TAIL, token_count), F32)),
        (info, grad_rows, grad_other, weights, gate, upward, gate_local, up_local, down_local),
        (pltpu.VMEM((row_count, 1), F32),))

    def to_home(k, dense, back, *tails):
        extra = TAIL if tails else 0
        return local_call(
            functools.partial(home_kernel, k, token_count, padded, bool(tails)),
            (shape_of((token_count + extra, half_width)),), (info, dense, back[k], places[k], *tails))[0]

    def summed(blocks):
        total = blocks[0][:token_count].astype(F32)
        for k in range(1, lines):
            total = total + blocks[k][:token_count].astype(F32)
        return total.astype(BF)

    sent, out_back = settle((sent, out_back))
    out_home = {k: to_home(k, out_dense, out_back) for k in leading}
    out_back[trailing] = over_pair(out_packed[trailing])

    def whole(own, other):
        return jnp.concatenate(
            [jnp.where(core == 0, own, other), jnp.where(core == 0, other, own)], axis=1)

    came = over_core(sent)
    out_came = {k: over_line(out_home[k], lines - k) for k in leading}
    in_dense, *in_packed = local_call(
        functools.partial(join_kernel, *sizes, False),
        (shape_of((lines, token_count, half_width), F32),
         *[shape_of((padded + TAIL, half_width)) for _ in every]),
        (info, came, grad_gate, grad_up, gate_local, up_local, compact_tails))
    in_packed, out_back[trailing], out_came = settle((in_packed, out_back[trailing], out_came))
    trailing_home = to_home(trailing, out_dense, out_back)
    out_came[trailing] = over_line(trailing_home, lines - trailing)
    in_back, in_home, sequence = {}, {}, outward + [0]
    for i, k in enumerate(sequence):
        packed = in_packed[k]
        if i >= 2:
            packed, _ = settle((packed, in_home[sequence[i - 2]]))
        in_back[k] = over_pair(packed)
        in_home[k] = to_home(k, in_dense, in_back, dense_tails)
    last, _ = settle((out_packed[0], in_back[sequence[1]]))
    out_back[0] = over_pair(last)
    ready, out_came = settle(({k: in_home[k] for k in sequence[:2]}, out_came))
    out_came[0] = to_home(0, out_dense, out_back)
    in_home.update(ready)
    layer_out = summed(out_came)
    last_home, layer_out, rows, rows_other, grad_rows, grad_up = settle(
        ([in_home[k] for k in outward], layer_out, rows, rows_other, grad_rows, grad_up))
    rows = whole(rows, rows_other)
    gate_grad = dot(rows, grad_gate, FIRST).astype(BF)
    down_grad = dot(scaled, whole(grad_rows, grad_other), FIRST).astype(BF)
    in_home = {k: over_line(in_home[k], lines - k) if k else in_home[0] for k in every}
    input_grad = summed(in_home)

    up_grad = dot(rows, grad_up, FIRST).astype(BF)

    held = []
    for k in every:
        values = in_home[k][token_count:, :token_count].astype(F32)
        held.append(jnp.stack([jnp.sum(values[:8], axis=0), jnp.sum(values[8:], axis=0)]))
    flat = jnp.stack(held).reshape(experts, token_count)
    place = (expert_ids // 2 - at_line) % lines
    slot = place * 2 + ((expert_ids % 2) != (mine % 2)).astype(I32)
    match = slot[:, :, None] == jnp.arange(experts, dtype=I32)[None, None, :]
    half_value = jnp.sum(jnp.where(match, flat.T[:, None, :], 0.0), axis=2)
    weight_grad = half_value + over_core(half_value)
    return (layer_out, input_grad, weight_grad, gate_grad[None], up_grad[None], down_grad[None])


def solution(mesh):
    in_specs = (
        P(("group", "expert"), "tensor"),
        P(("group", "expert"), None),
        P(("group", "expert"), None),
        P("expert", None, "tensor"),
        P("expert", None, "tensor"),
        P("expert", "tensor", None),
        P(("group", "expert"), "tensor"),
    )
    out_specs = (
        P(("group", "expert"), "tensor"),
        P(("group", "expert"), "tensor"),
        P(("group", "expert"), None),
        P(("group", "expert"), None, "tensor"),
        P(("group", "expert"), None, "tensor"),
        P(("group", "expert"), "tensor", None),
    )
    return jax.shard_map(
        per_device, mesh=mesh, in_specs=in_specs, out_specs=out_specs, check_vma=False
    )
```

```python
import functools

import jax
import jax.numpy as jnp
import numpy as np
from jax import lax
from jax.experimental import pallas as pl
from jax.experimental.pallas import tpu as pltpu
from jax.sharding import PartitionSpec as P

BF = jnp.bfloat16
F32 = jnp.float32
I32 = jnp.int32
TAIL = 16
ROWS = ((1,), (0,))
LAST = ((1,), (1,))
FIRST = ((0,), (0,))

SMEM_SPEC = pl.BlockSpec(memory_space=pltpu.SMEM)
VMEM_SPEC = pl.BlockSpec(memory_space=pltpu.VMEM)


def dot(a, b, contract):
    return lax.dot_general(a, b, (contract, ((), ())), preferred_element_type=F32)


def split_three(values):
    high = lax.reduce_precision(values, 8, 7)
    rest = values - high
    middle = lax.reduce_precision(rest, 8, 7)
    low = rest - middle
    return [part.astype(BF) for part in (high, middle, low)]


def shape_of(shape, dtype=BF):
    return jax.ShapeDtypeStruct(shape, dtype)


def local_call(kernel, outs, args, scratch=()):
    total = sum(int(np.prod(x.shape)) * x.dtype.itemsize for x in tuple(args) + tuple(outs))
    return pl.pallas_call(
        kernel,
        out_shape=tuple(outs),
        in_specs=[SMEM_SPEC] + [VMEM_SPEC] * (len(args) - 1),
        out_specs=(VMEM_SPEC,) * len(outs),
        scratch_shapes=list(scratch),
        compiler_params=pltpu.CompilerParams(vmem_limit_bytes=int(total * 1.25) + 4 * 1024 * 1024),
        cost_estimate=pl.CostEstimate(flops=1000, bytes_accessed=1000, transcendentals=0),
    )(*args)


def row_chunks(count):
    pieces = -(-count // 512)
    if count % (16 * pieces):
        pieces = 1
    return pieces, count // pieces


def token_pack_kernel(tokens, part_rows, capacity, padded, info, block, compact, place, own_parts, table, parts):
    width = compact.shape[1]
    per_row = width // tokens
    table[...] = block[tokens:, :].astype(F32)

    def parts_of(expert):
        row, lane = expert // per_row, pl.multiple_of((expert % per_row) * tokens, tokens)
        parts[...] = jnp.zeros_like(parts)
        for p in range(3):
            found = lax.broadcasted_iota(I32, (table.shape[0], tokens), 0) == p * part_rows + row
            parts[p:p + 1, :] = jnp.sum(
                jnp.where(found, table[:, pl.ds(lane, tokens)], 0.0), axis=0, keepdims=True)
        return parts[...]

    own_parts[...] = parts_of(info[0]).astype(BF)
    theirs = parts_of(info[1])
    named = jnp.sum(theirs, axis=0, keepdims=True) > 0.0
    row_at = lax.broadcasted_iota(I32, (tokens, tokens), 0)
    column_at = lax.broadcasted_iota(I32, (tokens, tokens), 1)
    until = (row_at <= column_at).astype(F32).astype(BF)
    ones = jnp.broadcast_to(named.astype(F32), (TAIL, tokens)).astype(BF)
    rank = jnp.dot(ones, until, preferred_element_type=F32)[:1, :].astype(I32) - 1
    picked = ((row_at == rank) & named & (row_at < capacity)).astype(F32).astype(BF)
    place[...] = picked[:padded, :]
    compact[:padded, :] = dot(picked[:padded, :], block[:tokens, :], ROWS).astype(BF)
    compact[padded:, :] = jnp.zeros((TAIL, width), BF)
    compact[padded:, :tokens] = dot(theirs.astype(BF), picked, LAST).astype(BF)


def grad_pack_kernel(info, block, place, compact):
    compact[...] = dot(place[...], block[...], ROWS).astype(BF)


def lay_out(lines, tokens, padded, blocks, compact, rows):
    for k in range(lines):
        rows[k * tokens:(k + 1) * tokens, :] = blocks[k][:tokens, :]
        at = lines * tokens + k * padded
        rows[at:at + padded, :] = compact[k][:padded, :]


def token_rows_kernel(lines, tokens, padded, info, *refs):
    n = lines
    blocks, compact, own_parts = refs[:n], refs[n:2 * n], refs[2 * n:3 * n]
    rows, weights = refs[3 * n:]
    lay_out(n, tokens, padded, blocks, compact, rows)
    eye = (lax.broadcasted_iota(I32, (tokens, tokens), 0)
           == lax.broadcasted_iota(I32, (tokens, tokens), 1))
    for k in range(n):
        for first, size, tail in (
            (k * tokens, tokens, own_parts[k][...]),
            (n * tokens + k * padded, padded, compact[k][padded:, :tokens]),
        ):
            row = jnp.sum(tail.astype(F32), axis=0, keepdims=True)
            column = jnp.sum(jnp.where(eye, row, 0.0), axis=1, keepdims=True)
            weights[first:first + size, :] = column[:size]


def grad_rows_kernel(lines, tokens, padded, info, *refs):
    lay_out(lines, tokens, padded, refs[:lines], refs[lines:2 * lines], refs[2 * lines])


def halves(info, width):
    core = info[2]
    return pl.ds(pl.multiple_of(core * width, width), width), pl.ds(pl.multiple_of((1 - core) * width, width), width)


def forward_kernel(pieces, chunk, info, own, other, weights, gate_w, up_w, down_w, gate, upward, scaled, sent):
    mine, theirs = halves(info, own.shape[1])

    @pl.loop(0, pieces)
    def _(i):
        at = pl.ds(pl.multiple_of(i * chunk, 16), chunk)
        a, b = own[at, :], other[at, :]
        g = dot(a, gate_w[mine, :], ROWS) + dot(b, gate_w[theirs, :], ROWS)
        u = dot(a, up_w[mine, :], ROWS) + dot(b, up_w[theirs, :], ROWS)
        gate[at, :] = g
        upward[at, :] = u
        h = (weights[at, :] * (g * jax.nn.sigmoid(g) * u)).astype(BF)
        scaled[at, :] = h
        sent[at, :] = dot(h, down_w[:, theirs], ROWS).astype(BF)


def backward_kernel(pieces, chunk, lines, tokens, padded, info, own, other, weights, gate, upward, gate_w, up_w,
                    down_w, grad_gate, grad_up, sent, dense_tails, compact_tails, values):
    mine, theirs = halves(info, own.shape[1])

    @pl.loop(0, pieces)
    def _(i):
        at = pl.ds(pl.multiple_of(i * chunk, 16), chunk)
        plain = dot(own[at, :], down_w[:, mine], LAST) + dot(other[at, :], down_w[:, theirs], LAST)
        g, u = gate[at, :], upward[at, :]
        sig = jax.nn.sigmoid(g)
        through = g * sig
        values[at, :] = jnp.sum(through * u * plain, axis=1, keepdims=True)
        scaled = weights[at, :] * plain
        gg = (scaled * u * sig * (1.0 + g * (1.0 - sig))).astype(BF)
        gu = (scaled * through).astype(BF)
        grad_gate[at, :] = gg
        grad_up[at, :] = gu
        sent[at, :] = (dot(gg, gate_w[theirs, :], LAST) + dot(gu, up_w[theirs, :], LAST)).astype(BF)

    eye = (lax.broadcasted_iota(I32, (tokens, tokens), 0)
           == lax.broadcasted_iota(I32, (tokens, tokens), 1))
    for k in range(lines):
        for first, size, tails in (
            (k * tokens, tokens, dense_tails),
            (lines * tokens + k * padded, padded, compact_tails),
        ):
            column = values[first:first + size, :]
            row = jnp.sum(jnp.where(eye[:size, :], column, 0.0), axis=0, keepdims=True)
            high = row.astype(BF).astype(F32)
            middle = (row - high).astype(BF).astype(F32)
            low = row - high - middle
            at = lax.broadcasted_iota(I32, (TAIL, tokens), 0)
            tails[k] = jnp.where(at == 0, high, jnp.where(at == 1, middle, jnp.where(at == 2, low, 0.0)))


def join_kernel(lines, tokens, padded, forward, info, came, *refs):
    width = came.shape[1]
    mine, _ = halves(info, width)
    if forward:
        scaled, down_w = refs[:2]
        dense, messages = refs[2], refs[3:]

        def product(first, size):
            return dot(scaled[first:first + size, :], down_w[:, mine], ROWS)
    else:
        grad_gate, grad_up, gate_w, up_w, tails = refs[:5]
        dense, messages = refs[5], refs[6:]

        def product(first, size):
            at = slice(first, first + size)
            return dot(grad_gate[at, :], gate_w[mine, :], LAST) + dot(grad_up[at, :], up_w[mine, :], LAST)

    def joined(first, size):
        return product(first, size) + came[first:first + size, :].astype(F32)

    start = lines * tokens
    for first in range(0, lines, 4):
        count = min(4, lines - first)
        total = joined(start + first * padded, count * padded).astype(BF)
        for k in range(first, first + count):
            messages[k][:padded, :] = total[(k - first) * padded:(k - first + 1) * padded]
            if not forward:
                messages[k][padded:, :] = jnp.zeros((TAIL, width), BF)
                messages[k][padded:, :tokens] = tails[k].astype(BF)
    for first in range(0, lines, 4):
        count = min(4, lines - first)
        total = joined(first * tokens, count * tokens)
        for k in range(first, first + count):
            dense[k] = total[(k - first) * tokens:(k - first + 1) * tokens]


def home_kernel(k, tokens, padded, tailed, info, dense, back, place, *refs):
    message = refs[-1]
    block = dense[k] + dot(place[...], back[:padded, :], FIRST)
    message[:tokens, :] = block.astype(BF)
    if not tailed:
        return
    tails = refs[0]
    message[tokens:, :] = jnp.zeros((TAIL, message.shape[1]), BF)
    theirs = dot(back[padded:, :padded], place[...], ROWS)
    message[tokens:, :tokens] = jnp.concatenate([tails[k][:8], theirs[:8]], axis=0).astype(BF)


def per_device(tokens, expert_ids, router_weights, gate_weight, up_weight, down_weight, grad_out):
    token_count, half_width = tokens.shape
    hidden_half = gate_weight.shape[2]
    top_count = expert_ids.shape[1]
    experts = lax.axis_size("expert")
    capacity = min(token_count, 3 * token_count * top_count // (2 * experts))
    padded = -(-capacity // 16) * 16
    lines = experts // 2
    mine = lax.axis_index("expert")
    core = lax.axis_index("tensor")
    at_line = mine // 2
    peer = mine + 1 - 2 * (mine % 2)
    settle = lax.optimization_barrier

    def over_pair(x):
        return lax.ppermute(x, "expert", [(i, i + 1 - 2 * (i % 2)) for i in range(experts)])

    def over_line(x, k):
        return lax.ppermute(
            x, "expert",
            [(i, ((i // 2 + k) % lines) * 2 + i % 2) for i in range(experts)],
        )

    def over_core(x):
        return lax.ppermute(x, "tensor", [(0, 1), (1, 0)])

    chosen = expert_ids[:, :, None] == jnp.arange(experts, dtype=I32)[None, None, :]
    table = jnp.sum(jnp.where(chosen, router_weights[:, :, None], 0.0), axis=1).T
    part_rows = experts * token_count // half_width
    parts = jnp.concatenate([p.reshape(part_rows, half_width) for p in split_three(table)])
    tail = -(-3 * part_rows // TAIL) * TAIL
    parts = jnp.pad(parts, ((0, tail - 3 * part_rows), (0, 0)))
    first = jnp.concatenate([tokens, parts])

    info = jnp.stack([mine, peer, core]).astype(I32)
    sizes = (lines, token_count, padded)
    row_count = lines * (token_count + padded)
    half_rows = shape_of((row_count, half_width))
    hidden_rows = (row_count, hidden_half)
    gate_local = gate_weight[0]
    up_local = up_weight[0]
    down_local = down_weight[0]
    pieces, chunk = row_chunks(row_count)
    every = range(lines)
    by_reach = sorted(range(1, lines), key=lambda k: min(k, lines - k))

    blocks = {0: first}
    for k in by_reach:
        blocks[k] = over_line(first, k)
    compact, places, own_parts, early = {}, {}, {}, []
    for k in [0] + by_reach:
        packed, places[k], own_parts[k] = local_call(
            functools.partial(token_pack_kernel, token_count, part_rows, capacity, padded),
            (shape_of((padded + TAIL, half_width)), shape_of((padded, token_count)),
             shape_of((TAIL, token_count))),
            (info, blocks[k]),
            (pltpu.VMEM((tail, half_width), F32), pltpu.VMEM((TAIL, token_count), F32)),
        )
        if k != by_reach[-1]:
            early.append(packed)
        compact[k] = over_pair(packed)

    (first_packed,) = local_call(
        grad_pack_kernel, (shape_of((padded, half_width)),), (info, grad_out, places[0]))
    grad_first = over_pair(first_packed)
    soon = {k: compact[k] for k in [0] + by_reach[:-1]}
    held_grad, blocks, early, soon, grad_first = settle((grad_out, blocks, early, soon, grad_first))
    compact.update(soon)
    grad_blocks = {0: held_grad}
    for k in by_reach:
        grad_blocks[k] = over_line(held_grad, k)

    def grad_pack(k):
        return local_call(
            grad_pack_kernel, (shape_of((padded, half_width)),), (info, grad_blocks[k], places[k]))[0]

    near, far = by_reach[:-1], by_reach[-1]
    grad_packed = {k: grad_pack(k) for k in by_reach}
    grad_compact = {k: over_pair(grad_packed[k]) for k in by_reach}
    grad_compact[0] = grad_first
    ahead = {k: grad_compact[k] for k in near[:1]}
    compact, grad_blocks, grad_packed, ahead = settle((compact, grad_blocks, grad_packed, ahead))
    grad_compact.update(ahead)
    rows, weights = local_call(
        functools.partial(token_rows_kernel, *sizes),
        (half_rows, shape_of((row_count, 1), F32)),
        (info, *[blocks[k] for k in every], *[compact[k] for k in every], *[own_parts[k] for k in every]))
    rows_other = over_core(rows)
    gate, upward, scaled, sent = local_call(
        functools.partial(forward_kernel, pieces, chunk),
        (shape_of(hidden_rows, F32), shape_of(hidden_rows, F32), shape_of(hidden_rows), half_rows),
        (info, rows, rows_other, weights, gate_local, up_local, down_local))
    sent, grad_compact = settle((sent, grad_compact))
    out_dense, *out_packed = local_call(
        functools.partial(join_kernel, *sizes, True),
        (shape_of((lines, token_count, half_width), F32),
         *[shape_of((padded, half_width)) for _ in every]),
        (info, over_core(sent), scaled, down_local))

    outward = by_reach[::-1]
    leading, trailing = outward[:-1], outward[-1]
    out_back = {k: over_pair(out_packed[k]) for k in leading}
    (grad_rows,) = local_call(
        functools.partial(grad_rows_kernel, *sizes), (half_rows,),
        (info, *[grad_blocks[k] for k in every], *[grad_compact[k] for k in every]))
    grad_other, out_packed = settle((over_core(grad_rows), out_packed))
    grad_gate, grad_up, sent, dense_tails, compact_tails = local_call(
        functools.partial(backward_kernel, pieces, chunk, *sizes),
        (shape_of(hidden_rows), shape_of(hidden_rows), half_rows,
         shape_of((lines, TAIL, token_count), F32), shape_of((lines, TAIL, token_count), F32)),
        (info, grad_rows, grad_other, weights, gate, upward, gate_local, up_local, down_local),
        (pltpu.VMEM((row_count, 1), F32),))

    def to_home(k, dense, back, *tails):
        extra = TAIL if tails else 0
        return local_call(
            functools.partial(home_kernel, k, token_count, padded, bool(tails)),
            (shape_of((token_count + extra, half_width)),), (info, dense, back[k], places[k], *tails))[0]

    def summed(blocks):
        total = blocks[0][:token_count].astype(F32)
        for k in range(1, lines):
            total = total + blocks[k][:token_count].astype(F32)
        return total.astype(BF)

    sent, out_back = settle((sent, out_back))
    out_home = {k: to_home(k, out_dense, out_back) for k in leading}
    out_back[trailing] = over_pair(out_packed[trailing])

    def whole(own, other):
        return jnp.concatenate(
            [jnp.where(core == 0, own, other), jnp.where(core == 0, other, own)], axis=1)

    came = over_core(sent)
    out_came = {k: over_line(out_home[k], lines - k) for k in leading}
    in_dense, *in_packed = local_call(
        functools.partial(join_kernel, *sizes, False),
        (shape_of((lines, token_count, half_width), F32),
         *[shape_of((padded + TAIL, half_width)) for _ in every]),
        (info, came, grad_gate, grad_up, gate_local, up_local, compact_tails))
    distant = out_came.pop(outward[0])
    in_packed, out_back[trailing], out_came = settle((in_packed, out_back[trailing], out_came))
    trailing_home = to_home(trailing, out_dense, out_back)
    later, out_came[outward[0]], _ = settle(
        (in_packed[:outward[0]] + in_packed[outward[0] + 1:], distant, trailing_home))
    in_packed = later[:outward[0]] + [in_packed[outward[0]]] + later[outward[0]:]
    out_came[trailing] = over_line(trailing_home, lines - trailing)
    in_back, in_home, sequence = {}, {}, outward + [0]
    for i, k in enumerate(sequence):
        packed = in_packed[k]
        if i >= 2:
            packed, _ = settle((packed, in_home[sequence[i - 2]]))
        in_back[k] = over_pair(packed)
        in_home[k] = to_home(k, in_dense, in_back, dense_tails)
    last, _ = settle((out_packed[0], in_back[sequence[1]]))
    out_back[0] = over_pair(last)
    ready, out_came = settle(({k: in_home[k] for k in sequence[:2]}, out_came))
    out_came[0] = to_home(0, out_dense, out_back)
    in_home.update(ready)
    layer_out = summed(out_came)
    last_home, layer_out, rows, rows_other, grad_rows, grad_up = settle(
        ([in_home[k] for k in outward], layer_out, rows, rows_other, grad_rows, grad_up))
    rows = whole(rows, rows_other)
    gate_grad = dot(rows, grad_gate, FIRST).astype(BF)
    down_grad = dot(scaled, whole(grad_rows, grad_other), FIRST).astype(BF)
    in_home = {k: over_line(in_home[k], lines - k) if k else in_home[0] for k in every}
    input_grad = summed(in_home)

    up_grad = dot(rows, grad_up, FIRST).astype(BF)

    held = []
    for k in every:
        values = in_home[k][token_count:, :token_count].astype(F32)
        held.append(jnp.stack([jnp.sum(values[:8], axis=0), jnp.sum(values[8:], axis=0)]))
    flat = jnp.stack(held).reshape(experts, token_count)
    place = (expert_ids // 2 - at_line) % lines
    slot = place * 2 + ((expert_ids % 2) != (mine % 2)).astype(I32)
    match = slot[:, :, None] == jnp.arange(experts, dtype=I32)[None, None, :]
    half_value = jnp.sum(jnp.where(match, flat.T[:, None, :], 0.0), axis=2)
    weight_grad = half_value + over_core(half_value)
    return (layer_out, input_grad, weight_grad, gate_grad[None], up_grad[None], down_grad[None])


def solution(mesh):
    in_specs = (
        P(("group", "expert"), "tensor"),
        P(("group", "expert"), None),
        P(("group", "expert"), None),
        P("expert", None, "tensor"),
        P("expert", None, "tensor"),
        P("expert", "tensor", None),
        P(("group", "expert"), "tensor"),
    )
    out_specs = (
        P(("group", "expert"), "tensor"),
        P(("group", "expert"), "tensor"),
        P(("group", "expert"), None),
        P(("group", "expert"), None, "tensor"),
        P(("group", "expert"), None, "tensor"),
        P(("group", "expert"), "tensor", None),
    )
    return jax.shard_map(
        per_device, mesh=mesh, in_specs=in_specs, out_specs=out_specs, check_vma=False
    )
```

```python
import functools

import jax
import jax.numpy as jnp
import numpy as np
from jax import lax
from jax.experimental import pallas as pl
from jax.experimental.pallas import tpu as pltpu
from jax.sharding import PartitionSpec as P

BF = jnp.bfloat16
F32 = jnp.float32
I32 = jnp.int32
TAIL = 16
ROWS = ((1,), (0,))
LAST = ((1,), (1,))
FIRST = ((0,), (0,))

SMEM_SPEC = pl.BlockSpec(memory_space=pltpu.SMEM)
VMEM_SPEC = pl.BlockSpec(memory_space=pltpu.VMEM)


def dot(a, b, contract):
    return lax.dot_general(a, b, (contract, ((), ())), preferred_element_type=F32)


def split_three(values):
    high = lax.reduce_precision(values, 8, 7)
    rest = values - high
    middle = lax.reduce_precision(rest, 8, 7)
    low = rest - middle
    return [part.astype(BF) for part in (high, middle, low)]


def shape_of(shape, dtype=BF):
    return jax.ShapeDtypeStruct(shape, dtype)


def local_call(kernel, outs, args, scratch=()):
    total = sum(int(np.prod(x.shape)) * x.dtype.itemsize for x in tuple(args) + tuple(outs))
    return pl.pallas_call(
        kernel,
        out_shape=tuple(outs),
        in_specs=[SMEM_SPEC] + [VMEM_SPEC] * (len(args) - 1),
        out_specs=(VMEM_SPEC,) * len(outs),
        scratch_shapes=list(scratch),
        compiler_params=pltpu.CompilerParams(vmem_limit_bytes=int(total * 1.25) + 4 * 1024 * 1024),
        cost_estimate=pl.CostEstimate(flops=1000, bytes_accessed=1000, transcendentals=0),
    )(*args)


def row_chunks(count):
    pieces = -(-count // 512)
    if count % (16 * pieces):
        pieces = 1
    return pieces, count // pieces


def token_pack_kernel(tokens, part_rows, capacity, padded, info, block, compact, place, own_parts, table, parts):
    width = compact.shape[1]
    per_row = width // tokens
    table[...] = block[tokens:, :].astype(F32)

    def parts_of(expert):
        row, lane = expert // per_row, pl.multiple_of((expert % per_row) * tokens, tokens)
        parts[...] = jnp.zeros_like(parts)
        for p in range(3):
            found = lax.broadcasted_iota(I32, (table.shape[0], tokens), 0) == p * part_rows + row
            parts[p:p + 1, :] = jnp.sum(
                jnp.where(found, table[:, pl.ds(lane, tokens)], 0.0), axis=0, keepdims=True)
        return parts[...]

    own_parts[...] = parts_of(info[0]).astype(BF)
    theirs = parts_of(info[1])
    named = jnp.sum(theirs, axis=0, keepdims=True) > 0.0
    row_at = lax.broadcasted_iota(I32, (tokens, tokens), 0)
    column_at = lax.broadcasted_iota(I32, (tokens, tokens), 1)
    until = (row_at <= column_at).astype(F32).astype(BF)
    ones = jnp.broadcast_to(named.astype(F32), (TAIL, tokens)).astype(BF)
    rank = jnp.dot(ones, until, preferred_element_type=F32)[:1, :].astype(I32) - 1
    picked = ((row_at == rank) & named & (row_at < capacity)).astype(F32).astype(BF)
    place[...] = picked[:padded, :]
    compact[:padded, :] = dot(picked[:padded, :], block[:tokens, :], ROWS).astype(BF)
    compact[padded:, :] = jnp.zeros((TAIL, width), BF)
    compact[padded:, :tokens] = dot(theirs.astype(BF), picked, LAST).astype(BF)


def grad_pack_kernel(info, block, place, compact):
    compact[...] = dot(place[...], block[...], ROWS).astype(BF)


def lay_out(lines, tokens, padded, blocks, compact, rows):
    for k in range(lines):
        rows[k * tokens:(k + 1) * tokens, :] = blocks[k][:tokens, :]
        at = lines * tokens + k * padded
        rows[at:at + padded, :] = compact[k][:padded, :]


def token_rows_kernel(lines, tokens, padded, info, *refs):
    n = lines
    blocks, compact, own_parts = refs[:n], refs[n:2 * n], refs[2 * n:3 * n]
    rows, weights = refs[3 * n:]
    lay_out(n, tokens, padded, blocks, compact, rows)
    eye = (lax.broadcasted_iota(I32, (tokens, tokens), 0)
           == lax.broadcasted_iota(I32, (tokens, tokens), 1))
    for k in range(n):
        for first, size, tail in (
            (k * tokens, tokens, own_parts[k][...]),
            (n * tokens + k * padded, padded, compact[k][padded:, :tokens]),
        ):
            row = jnp.sum(tail.astype(F32), axis=0, keepdims=True)
            column = jnp.sum(jnp.where(eye, row, 0.0), axis=1, keepdims=True)
            weights[first:first + size, :] = column[:size]


def grad_rows_kernel(lines, tokens, padded, info, *refs):
    lay_out(lines, tokens, padded, refs[:lines], refs[lines:2 * lines], refs[2 * lines])


def halves(info, width):
    core = info[2]
    return pl.ds(pl.multiple_of(core * width, width), width), pl.ds(pl.multiple_of((1 - core) * width, width), width)


def forward_kernel(pieces, chunk, info, own, other, weights, gate_w, up_w, down_w, gate, upward, scaled, sent):
    mine, theirs = halves(info, own.shape[1])

    @pl.loop(0, pieces)
    def _(i):
        at = pl.ds(pl.multiple_of(i * chunk, 16), chunk)
        a, b = own[at, :], other[at, :]
        g = dot(a, gate_w[mine, :], ROWS) + dot(b, gate_w[theirs, :], ROWS)
        u = dot(a, up_w[mine, :], ROWS) + dot(b, up_w[theirs, :], ROWS)
        gate[at, :] = g
        upward[at, :] = u
        h = (weights[at, :] * (g * jax.nn.sigmoid(g) * u)).astype(BF)
        scaled[at, :] = h
        sent[at, :] = dot(h, down_w[:, theirs], ROWS).astype(BF)


def backward_kernel(pieces, chunk, lines, tokens, padded, info, own, other, weights, gate, upward, gate_w, up_w,
                    down_w, grad_gate, grad_up, sent, dense_tails, compact_tails, values):
    mine, theirs = halves(info, own.shape[1])

    @pl.loop(0, pieces)
    def _(i):
        at = pl.ds(pl.multiple_of(i * chunk, 16), chunk)
        plain = dot(own[at, :], down_w[:, mine], LAST) + dot(other[at, :], down_w[:, theirs], LAST)
        g, u = gate[at, :], upward[at, :]
        sig = jax.nn.sigmoid(g)
        through = g * sig
        values[at, :] = jnp.sum(through * u * plain, axis=1, keepdims=True)
        scaled = weights[at, :] * plain
        gg = (scaled * u * sig * (1.0 + g * (1.0 - sig))).astype(BF)
        gu = (scaled * through).astype(BF)
        grad_gate[at, :] = gg
        grad_up[at, :] = gu
        sent[at, :] = (dot(gg, gate_w[theirs, :], LAST) + dot(gu, up_w[theirs, :], LAST)).astype(BF)

    eye = (lax.broadcasted_iota(I32, (tokens, tokens), 0)
           == lax.broadcasted_iota(I32, (tokens, tokens), 1))
    for k in range(lines):
        for first, size, tails in (
            (k * tokens, tokens, dense_tails),
            (lines * tokens + k * padded, padded, compact_tails),
        ):
            column = values[first:first + size, :]
            row = jnp.sum(jnp.where(eye[:size, :], column, 0.0), axis=0, keepdims=True)
            high = row.astype(BF).astype(F32)
            middle = (row - high).astype(BF).astype(F32)
            low = row - high - middle
            at = lax.broadcasted_iota(I32, (TAIL, tokens), 0)
            tails[k] = jnp.where(at == 0, high, jnp.where(at == 1, middle, jnp.where(at == 2, low, 0.0)))


def join_kernel(lines, tokens, padded, forward, info, came, *refs):
    width = came.shape[1]
    mine, _ = halves(info, width)
    if forward:
        scaled, down_w = refs[:2]
        dense, messages = refs[2], refs[3:]

        def product(first, size):
            return dot(scaled[first:first + size, :], down_w[:, mine], ROWS)
    else:
        grad_gate, grad_up, gate_w, up_w, tails = refs[:5]
        dense, messages = refs[5], refs[6:]

        def product(first, size):
            at = slice(first, first + size)
            return dot(grad_gate[at, :], gate_w[mine, :], LAST) + dot(grad_up[at, :], up_w[mine, :], LAST)

    def joined(first, size):
        return product(first, size) + came[first:first + size, :].astype(F32)

    start = lines * tokens
    for first in range(0, lines, 4):
        count = min(4, lines - first)
        total = joined(start + first * padded, count * padded).astype(BF)
        for k in range(first, first + count):
            messages[k][:padded, :] = total[(k - first) * padded:(k - first + 1) * padded]
            if not forward:
                messages[k][padded:, :] = jnp.zeros((TAIL, width), BF)
                messages[k][padded:, :tokens] = tails[k].astype(BF)
    for first in range(0, lines, 4):
        count = min(4, lines - first)
        total = joined(first * tokens, count * tokens)
        for k in range(first, first + count):
            dense[k] = total[(k - first) * tokens:(k - first + 1) * tokens]


def home_kernel(k, tokens, padded, tailed, info, dense, back, place, *refs):
    message = refs[-1]
    block = dense[k] + dot(place[...], back[:padded, :], FIRST)
    message[:tokens, :] = block.astype(BF)
    if not tailed:
        return
    tails = refs[0]
    message[tokens:, :] = jnp.zeros((TAIL, message.shape[1]), BF)
    theirs = dot(back[padded:, :padded], place[...], ROWS)
    message[tokens:, :tokens] = jnp.concatenate([tails[k][:8], theirs[:8]], axis=0).astype(BF)


def per_device(tokens, expert_ids, router_weights, gate_weight, up_weight, down_weight, grad_out):
    token_count, half_width = tokens.shape
    hidden_half = gate_weight.shape[2]
    top_count = expert_ids.shape[1]
    experts = lax.axis_size("expert")
    capacity = min(token_count, 3 * token_count * top_count // (2 * experts))
    padded = -(-capacity // 16) * 16
    lines = experts // 2
    mine = lax.axis_index("expert")
    core = lax.axis_index("tensor")
    at_line = mine // 2
    peer = mine + 1 - 2 * (mine % 2)
    settle = lax.optimization_barrier

    def over_pair(x):
        return lax.ppermute(x, "expert", [(i, i + 1 - 2 * (i % 2)) for i in range(experts)])

    def over_line(x, k):
        return lax.ppermute(
            x, "expert",
            [(i, ((i // 2 + k) % lines) * 2 + i % 2) for i in range(experts)],
        )

    def over_core(x):
        return lax.ppermute(x, "tensor", [(0, 1), (1, 0)])

    chosen = expert_ids[:, :, None] == jnp.arange(experts, dtype=I32)[None, None, :]
    table = jnp.sum(jnp.where(chosen, router_weights[:, :, None], 0.0), axis=1).T
    part_rows = experts * token_count // half_width
    parts = jnp.concatenate([p.reshape(part_rows, half_width) for p in split_three(table)])
    tail = -(-3 * part_rows // TAIL) * TAIL
    parts = jnp.pad(parts, ((0, tail - 3 * part_rows), (0, 0)))
    first = jnp.concatenate([tokens, parts])

    info = jnp.stack([mine, peer, core]).astype(I32)
    sizes = (lines, token_count, padded)
    row_count = lines * (token_count + padded)
    half_rows = shape_of((row_count, half_width))
    hidden_rows = (row_count, hidden_half)
    gate_local = gate_weight[0]
    up_local = up_weight[0]
    down_local = down_weight[0]
    pieces, chunk = row_chunks(row_count)
    every = range(lines)
    by_reach = sorted(range(1, lines), key=lambda k: min(k, lines - k))

    blocks = {0: first}
    for k in by_reach:
        blocks[k] = over_line(first, k)
    compact, places, own_parts, early = {}, {}, {}, []
    for k in [0] + by_reach:
        packed, places[k], own_parts[k] = local_call(
            functools.partial(token_pack_kernel, token_count, part_rows, capacity, padded),
            (shape_of((padded + TAIL, half_width)), shape_of((padded, token_count)),
             shape_of((TAIL, token_count))),
            (info, blocks[k]),
            (pltpu.VMEM((tail, half_width), F32), pltpu.VMEM((TAIL, token_count), F32)),
        )
        if k != by_reach[-1]:
            early.append(packed)
        compact[k] = over_pair(packed)

    (first_packed,) = local_call(
        grad_pack_kernel, (shape_of((padded, half_width)),), (info, grad_out, places[0]))
    grad_first = over_pair(first_packed)
    soon = {k: compact[k] for k in [0] + by_reach[:-1]}
    held_grad, blocks, early, soon, grad_first = settle((grad_out, blocks, early, soon, grad_first))
    compact.update(soon)
    grad_blocks = {0: held_grad}
    for k in by_reach:
        grad_blocks[k] = over_line(held_grad, k)

    def grad_pack(k):
        return local_call(
            grad_pack_kernel, (shape_of((padded, half_width)),), (info, grad_blocks[k], places[k]))[0]

    near, far = by_reach[:-1], by_reach[-1]
    grad_packed = {k: grad_pack(k) for k in near}
    grad_compact = {k: over_pair(grad_packed[k]) for k in near}
    grad_compact[0] = grad_first
    compact, near_blocks, near_packed = settle(
        (compact, {k: grad_blocks[k] for k in near}, {k: grad_packed[k] for k in near}))
    grad_blocks.update(near_blocks)
    rows, weights = local_call(
        functools.partial(token_rows_kernel, *sizes),
        (half_rows, shape_of((row_count, 1), F32)),
        (info, *[blocks[k] for k in every], *[compact[k] for k in every], *[own_parts[k] for k in every]))
    rows_other = over_core(rows)
    gate, upward, scaled, sent = local_call(
        functools.partial(forward_kernel, pieces, chunk),
        (shape_of(hidden_rows, F32), shape_of(hidden_rows, F32), shape_of(hidden_rows), half_rows),
        (info, rows, rows_other, weights, gate_local, up_local, down_local))
    sent, grad_compact, grad_blocks = settle((sent, grad_compact, grad_blocks))
    grad_compact[far] = over_pair(grad_pack(far))
    out_dense, *out_packed = local_call(
        functools.partial(join_kernel, *sizes, True),
        (shape_of((lines, token_count, half_width), F32),
         *[shape_of((padded, half_width)) for _ in every]),
        (info, over_core(sent), scaled, down_local))

    outward = by_reach[::-1]
    out_back = {k: over_pair(out_packed[k]) for k in near}
    (grad_rows,) = local_call(
        functools.partial(grad_rows_kernel, *sizes), (half_rows,),
        (info, *[grad_blocks[k] for k in every], *[grad_compact[k] for k in every]))
    grad_rows, out_packed = settle((grad_rows, out_packed))
    grad_other = over_core(grad_rows)
    grad_gate, grad_up, sent, dense_tails, compact_tails = local_call(
        functools.partial(backward_kernel, pieces, chunk, *sizes),
        (shape_of(hidden_rows), shape_of(hidden_rows), half_rows,
         shape_of((lines, TAIL, token_count), F32), shape_of((lines, TAIL, token_count), F32)),
        (info, grad_rows, grad_other, weights, gate, upward, gate_local, up_local, down_local),
        (pltpu.VMEM((row_count, 1), F32),))

    def to_home(k, dense, back, *tails):
        extra = TAIL if tails else 0
        return local_call(
            functools.partial(home_kernel, k, token_count, padded, bool(tails)),
            (shape_of((token_count + extra, half_width)),), (info, dense, back[k], places[k], *tails))[0]

    def summed(blocks):
        total = blocks[0][:token_count].astype(F32)
        for k in range(1, lines):
            total = total + blocks[k][:token_count].astype(F32)
        return total.astype(BF)

    sent, out_back = settle((sent, out_back))
    out_home = {k: to_home(k, out_dense, out_back) for k in near}
    last, first_home = settle((out_packed[far], out_home[near[0]]))
    out_back[far] = over_pair(last)
    out_home[near[0]] = first_home
    def whole(own, other):
        return jnp.concatenate(
            [jnp.where(core == 0, own, other), jnp.where(core == 0, other, own)], axis=1)

    came = over_core(sent)
    out_came = {k: over_line(out_home[k], lines - k) for k in near}
    in_dense, *in_packed = local_call(
        functools.partial(join_kernel, *sizes, False),
        (shape_of((lines, token_count, half_width), F32),
         *[shape_of((padded + TAIL, half_width)) for _ in every]),
        (info, came, grad_gate, grad_up, gate_local, up_local, compact_tails))
    in_packed, out_back[far], ahead = settle((in_packed, out_back[far], out_came))
    out_came.update(ahead)
    last, out_back[far] = settle((out_packed[0], out_back[far]))
    out_back[0] = over_pair(last)
    for k in (far, 0):
        out_home[k] = to_home(k, out_dense, out_back)

    out_came[far] = over_line(out_home[far], lines - far)
    out_came[0] = out_home[0]
    in_back, in_home, sequence = {}, {}, outward + [0]
    for i, k in enumerate(sequence):
        packed = in_packed[k]
        if i >= 2:
            packed, _ = settle((packed, in_home[sequence[i - 2]]))
        in_back[k] = over_pair(packed)
        in_home[k] = to_home(k, in_dense, in_back, dense_tails)
    ready, out_came = settle(({k: in_home[k] for k in sequence[:2]}, out_came))
    in_home.update(ready)
    layer_out = summed(out_came)
    rows, rows_other, grad_rows, _ = settle((rows, rows_other, grad_rows, in_packed))
    rows = whole(rows, rows_other)
    gate_grad = dot(rows, grad_gate, FIRST).astype(BF)
    down_grad = dot(scaled, whole(grad_rows, grad_other), FIRST).astype(BF)
    in_home[sequence[0]], gate_grad = settle((in_home[sequence[0]], gate_grad))
    in_home[sequence[1]], down_grad = settle((in_home[sequence[1]], down_grad))
    last_home, rows, grad_up = settle(([in_home[k] for k in outward], rows, grad_up))
    in_home = {k: over_line(in_home[k], lines - k) if k else in_home[0] for k in every}
    input_grad = summed(in_home)

    up_grad = dot(rows, grad_up, FIRST).astype(BF)

    held = []
    for k in every:
        values = in_home[k][token_count:, :token_count].astype(F32)
        held.append(jnp.stack([jnp.sum(values[:8], axis=0), jnp.sum(values[8:], axis=0)]))
    flat = jnp.stack(held).reshape(experts, token_count)
    place = (expert_ids // 2 - at_line) % lines
    slot = place * 2 + ((expert_ids % 2) != (mine % 2)).astype(I32)
    match = slot[:, :, None] == jnp.arange(experts, dtype=I32)[None, None, :]
    half_value = jnp.sum(jnp.where(match, flat.T[:, None, :], 0.0), axis=2)
    weight_grad = half_value + over_core(half_value)
    return (layer_out, input_grad, weight_grad, gate_grad[None], up_grad[None], down_grad[None])


def solution(mesh):
    in_specs = (
        P(("group", "expert"), "tensor"),
        P(("group", "expert"), None),
        P(("group", "expert"), None),
        P("expert", None, "tensor"),
        P("expert", None, "tensor"),
        P("expert", "tensor", None),
        P(("group", "expert"), "tensor"),
    )
    out_specs = (
        P(("group", "expert"), "tensor"),
        P(("group", "expert"), "tensor"),
        P(("group", "expert"), None),
        P(("group", "expert"), None, "tensor"),
        P(("group", "expert"), None, "tensor"),
        P(("group", "expert"), "tensor", None),
    )
    return jax.shard_map(
        per_device, mesh=mesh, in_specs=in_specs, out_specs=out_specs, check_vma=False
    )
```
